256 devices in a mesh: seq: 32 (over y, x, core), tensor: 8 (over z).
Axes of the slice: x: 4, y: 4, z: 8, core: 2. Of those that a mesh axis runs over, the one named last changes fastest.
Arguments:
- tokens: bfloat16 [8192, 4096], P('seq', 'tensor'), may hold values from -6 to 6
- x_gain: bfloat16 [4096], replicated, may hold values from 0.099609375 to 1.8984375
- nbr_gain: bfloat16 [4096], replicated, may hold values from 0.099609375 to 1.8984375
- database: bfloat16 [512, 128, 4096], P('seq', None, 'tensor'), may hold values from -6 to 6
- nbr_shard: int32 [128, 2], P('seq'), may hold values from 0 to 31, all different within a row; in each aligned block of 4 rows (0 to 3, 4 to 7, ...) at most 2 rows name the same one
- nbr_row: int32 [128, 2], P('seq'), may hold values from 0 to 15
- nbr_count: int32 [128], P('seq'), may hold values from 1 to 2
- wq: bfloat16 [4096, 2048], P(None, 'tensor'), may hold values from -8 to 8
- wk: bfloat16 [4096, 2048], P(None, 'tensor'), may hold values from -0.09375 to 0.09375
- wv: bfloat16 [4096, 2048], P(None, 'tensor'), may hold values from -0.09375 to 0.09375
- wo: bfloat16 [2048, 4096], P('tensor'), may hold values from -0.125 to 0.125
Outputs:
- mixed: bfloat16 [8192, 4096], P('seq', 'tensor')
The draws below stay inside these ranges and needn't reach their ends.
Inputs may be any that keep to these rules, and one draw needn't show every extreme that they name: `nbr_shard`: among the spans of one device no shard is named more than 2 times, a bound that some block reaches; the 2 neighbours of a span name different shards.
All inputs are finite; a program needn't handle non-finite values.
Results may differ from the reference program's by a relative error of at most 0.015.
The reference program's roundings to bfloat16 on the way (of `normed`, `queries`, `rows`, `encoded`, `weights`, `attended` and `part`) count: a program that leaves them out, or rounds other values in their place, can miss the bound.
Values may be sent and summed in bfloat16 or wider, within the bound.
No kernel may reach another device: no remote copies, remote signals or barrier semaphores. Data moves between devices by JAX's collectives and lax.ppermute only.
A program may use at most 192 MiB of HBM per device.

```python
import math
import jax
import jax.numpy as jnp
import numpy as np
from jax import lax

D = 4096
HEADS = 16
HS = 128
SPAN = 64
NBR_LEN = 128
NB = 2
CAP = 2
DB_DEV = 16
CH_DEV = 4
TOKENS = 8192
SPANS = 128
DB_ROWS = 512
N_SEQ = 32
N_TENSOR = 8


def draw_wq(key, part):
    key = jax.random.fold_in(key, 5)
    base = jax.random.normal(key, (D, HEADS * HS), jnp.float32) / math.sqrt(D)
    base = jnp.clip(base, -6.0 / math.sqrt(D), 6.0 / math.sqrt(D))
    return base.astype(jnp.bfloat16)


def set_ends(entries, stream_key, least, high):
    shape = entries.shape
    spot = [jax.random.randint(jax.random.fold_in(stream_key, axis), (), 0, shape[axis]) for axis in range(len(shape))]
    entries = entries.at[tuple(spot)].set(least)
    longest = shape.index(max(shape))
    spot[longest] = (spot[longest] + 1) % shape[longest]
    return entries.at[tuple(spot)].set(high)


def level_of(own_key, shape, shards, smallest, top_value):
    def one(axis_at, blocks):
        draws = jax.random.uniform(jax.random.fold_in(jax.random.fold_in(own_key, 6), axis_at), (blocks,), jnp.float32, smallest / len(shards), top_value / len(shards))
        return jnp.repeat(jnp.exp(draws), shape[axis_at] // blocks).reshape((-1,) + (1,) * (len(shape) - axis_at - 1))

    loudness = one(*shards[0])
    for cut in shards[1:]:
        loudness = loudness * one(*cut)
    return loudness


def routed_block(own_key, own, number, rows, count, top, most, skew):
    ranking = jax.random.permutation(own_key, count)
    crowded, ordinary = portions_of(count, rows * top, most, skew, True), portions_of(count, rows * top, most, skew, False)
    places = jnp.arange(count)

    def named(tallies, turn):
        used = int((tallies > 0).sum())
        fixed = max(1, used // 4)
        passed = fixed + (places - fixed + turn * (used - fixed)) % max(1, count - fixed)
        return jnp.zeros((count,), jnp.int32).at[ranking[jnp.where(places < fixed, places, passed)]].set(jnp.asarray(tallies, jnp.int32))

    tallies = jnp.where(number % 4 == 0, named(crowded, number // 4), named(ordinary, number - number // 4 - 1))
    mixed = jax.random.permutation(jax.random.fold_in(own, 3), count)
    giver, sink = mixed[0:count // 2 * 2:2], mixed[1:count // 2 * 2:2]
    margin = jnp.minimum(tallies[giver] - 1, most - tallies[sink]) // 2
    margin = jnp.where((giver == ranking[0]) | (sink == ranking[0]) | (tallies[sink] == 0), 0, jnp.maximum(margin, 0))
    passed = jax.random.randint(jax.random.fold_in(own, 4), (count // 2,), 0, 1 << 20) % (margin + 1)
    tallies = tallies.at[giver].add(-passed).at[sink].add(passed)
    items = jnp.searchsorted(jnp.cumsum(tallies), jnp.arange(rows * top), side="right").astype(jnp.int32)
    grid = items.reshape(top, rows).T
    grid = grid[jax.random.permutation(jax.random.fold_in(own, 1), rows)]
    turn = jax.random.randint(jax.random.fold_in(own, 2), (rows, 1), 0, top)
    return jnp.take_along_axis(grid, (jnp.arange(top)[None, :] + turn) % top, axis=1)


def portions_of(number_of, total, limit, lean, full):
    portions = [(1 << 20) // math.isqrt(standing ** lean) + 1 for standing in range(1, number_of + 1)]
    largest = limit if full else min(limit, max(-(-total // number_of), total * portions[0] // sum(portions)))
    least = 1 if total - largest >= number_of - 1 else 0
    given, surplus = [largest] + [least] * (number_of - 1), total - largest - least * (number_of - 1)
    while surplus > 0:
        free = [i for i in range(1, number_of) if given[i] < largest] or [i for i in range(1, number_of) if given[i] < limit]
        whole, budget = sum([portions[i] for i in free]), surplus
        for i in free:
            more = min(limit - given[i], max(1, budget * portions[i] // whole), surplus)
            given[i] = given[i] + more
            surplus = surplus - more
    return np.array(given)


def scatter_about(key, dims, deviation, limit, pieces=(), kind=jnp.bfloat16):
    entries = jax.random.normal(key, dims, jnp.float32) * deviation
    if len(pieces) > 0:
        entries = level_of(key, dims, pieces, -0.22, 0.18) * entries
    return jnp.clip(entries, min=-limit, max=limit).astype(kind)


def setup_inputs(seed: int = 0) -> dict:
    key_of = jax.random.split(jax.random.key(seed), 12)
    tokens = scatter_about(key_of[0], (TOKENS, D), 1.0, 6.0, ((0, 32), (1, 8)))
    x_gain = jnp.clip(1.0 + 0.18 * jax.random.normal(key_of[1], (D,), jnp.float32), 0.099609375, 1.8984375).astype(jnp.bfloat16)
    nbr_gain = jnp.clip(1.0 + 0.18 * jax.random.normal(key_of[2], (D,), jnp.float32), 0.099609375, 1.8984375).astype(jnp.bfloat16)
    database = scatter_about(key_of[3], (DB_ROWS, NBR_LEN, D), 1.0, 6.0, ((0, 32), (2, 8)))
    nbr_shard_keys = jax.random.split(jax.random.fold_in(key_of[4], 1), SPANS // CH_DEV)
    nbr_shard_turns = jax.random.permutation(jax.random.fold_in(key_of[4], 3), SPANS // CH_DEV)
    nbr_shard = jax.vmap(lambda own, number: routed_block(jax.random.fold_in(key_of[4], 2), own, number, CH_DEV, N_SEQ, NB, CAP, 2))(nbr_shard_keys, nbr_shard_turns).reshape((SPANS, NB))
    nbr_row = set_ends(jax.random.randint(key_of[5], (SPANS, NB), 0, DB_DEV), jax.random.fold_in(key_of[5], 1), 0, DB_DEV - 1).astype(jnp.int32)
    nbr_count = set_ends(jax.random.randint(key_of[6], (SPANS,), 1, NB + 1), jax.random.fold_in(key_of[6], 1), 1, NB).astype(jnp.int32)
    wq = draw_wq(jax.random.fold_in(key_of[11], 71), 0)
    wk = scatter_about(key_of[8], (D, HEADS * HS), D ** -0.5, 0.09375, ((1, 8),))
    wv = scatter_about(key_of[9], (D, HEADS * HS), D ** -0.5, 0.09375, ((1, 8),))
    wo = scatter_about(key_of[10], (HEADS * HS, D), (HEADS * HS) ** -0.5, 0.125, ((0, 8),))
    return {"tokens": tokens, "x_gain": x_gain, "nbr_gain": nbr_gain, "database": database, "nbr_shard": nbr_shard, "nbr_row": nbr_row, "nbr_count": nbr_count, "wq": wq, "wk": wk, "wv": wv, "wo": wo}


def rms_scale(rows, gain):
    values = rows.astype(jnp.float32)
    inverse = lax.rsqrt(lax.optimization_barrier(jnp.mean(values * values, axis=-1, keepdims=True)) + 1e-06)
    return (values * inverse * gain.astype(jnp.float32)).astype(jnp.bfloat16)

def attend(queries, keys, values, count):
    scores = jnp.einsum('bqhe,bkhe->bhqk', queries.astype(jnp.float32), keys.astype(jnp.float32))
    width = keys.shape[1]
    owner = jnp.arange(width, dtype=jnp.int32) // (width // NB)
    valid = (owner[None, :] < count[:, None])[:, None, None, :]
    scores = jnp.where(valid, scores, jnp.float32(-1e+30))
    top = lax.optimization_barrier(jnp.max(scores, axis=-1, keepdims=True))
    expo = jnp.exp(scores - top)
    weights = (expo / lax.optimization_barrier(jnp.sum(expo, axis=-1, keepdims=True))).astype(jnp.bfloat16)
    return jnp.einsum('bhqk,bkhe->bqhe', weights.astype(jnp.float32), values.astype(jnp.float32)).astype(jnp.bfloat16)

def reference(tokens, x_gain, nbr_gain, database, nbr_shard, nbr_row, nbr_count, wq, wk, wv, wo):
    normed = rms_scale(tokens, x_gain)
    queries = (jnp.dot(normed, wq, preferred_element_type=jnp.float32) * HS ** (-0.5)).astype(jnp.bfloat16)
    offset = SPAN - 1
    padded = jnp.concatenate([queries[offset:], jnp.zeros((offset, HEADS * HS), jnp.bfloat16)], axis=0)
    blocks = padded.reshape(SPANS, SPAN, HEADS, HS)

    def one_span(packed):
        block, owners, offsets, count = packed
        index = (owners * DB_DEV + offsets).astype(jnp.int32)
        rows = database[index]
        encoded = rms_scale(rows, nbr_gain).reshape(NB * NBR_LEN, D)
        keys = jnp.dot(encoded, wk, preferred_element_type=jnp.float32).astype(jnp.bfloat16)
        values = jnp.dot(encoded, wv, preferred_element_type=jnp.float32).astype(jnp.bfloat16)
        keys = keys.reshape(NB * NBR_LEN, HEADS, HS)
        values = values.reshape(NB * NBR_LEN, HEADS, HS)
        return attend(block[None], keys[None], values[None], count[None])[0]
    outputs = lax.map(one_span, (blocks, nbr_shard, nbr_row, nbr_count))
    flat = outputs.reshape(TOKENS, HEADS * HS)
    attended = jnp.concatenate([jnp.zeros((offset, HEADS * HS), jnp.bfloat16), flat[:TOKENS - offset]], axis=0)
    total = tokens.astype(jnp.float32)
    group_cols = HEADS * HS // N_TENSOR
    for group in range(N_TENSOR):
        lower = group * group_cols
        part = jnp.dot(attended[:, lower:lower + group_cols], wo[lower:lower + group_cols], preferred_element_type=jnp.float32).astype(jnp.bfloat16)
        part = lax.optimization_barrier(part)
        total = total + part.astype(jnp.float32)
    return total.astype(jnp.bfloat16)
```

```python
import jax
import jax.numpy as jnp
from jax import lax
from jax.sharding import PartitionSpec as P

HS = 128
NB = 2
PIECE_T = 16
PIECE_F = 128


def passed_along(x, axis, by):
    size = lax.axis_size(axis)
    pairs = [(i, i + by) for i in range(size) if 0 <= i + by < size]
    return lax.ppermute(x, axis, pairs)


def rms_scale(rows, gain):
    values = rows.astype(jnp.float32)
    inverse = lax.rsqrt(jnp.mean(values * values, axis=-1, keepdims=True) + 1e-06)
    return (values * inverse * gain.astype(jnp.float32)).astype(jnp.bfloat16)


def attend(queries, keys, values, count):
    scores = jnp.einsum("bqhe,bkhe->bhqk", queries, keys, preferred_element_type=jnp.float32)
    width = keys.shape[1]
    owner = jnp.arange(width, dtype=jnp.int32) // (width // NB)
    valid = (owner[None, :] < count[:, None])[:, None, None, :]
    scores = jnp.where(valid, scores, jnp.float32(-1e30))
    top = jnp.max(scores, axis=-1, keepdims=True)
    expo = jnp.exp(scores - top)
    weights = (expo / jnp.sum(expo, axis=-1, keepdims=True)).astype(jnp.bfloat16)
    return jnp.einsum(
        "bhqk,bkhe->bqhe", weights, values, preferred_element_type=jnp.float32
    ).astype(jnp.bfloat16)


def body(tokens, x_gain, nbr_gain, database, nbr_shard, nbr_row, nbr_count, wq, wk, wv, wo):
    n_seq = lax.axis_size("seq")
    n_ten = lax.axis_size("tensor")
    tok_dev = tokens.shape[0]
    span_dev = nbr_shard.shape[0]
    span_len = tok_dev // span_dev
    nbr_len = database.shape[1]
    d_part = database.shape[2]
    head_cols = wq.shape[1]
    heads_dev = head_cols // HS
    items = span_dev * NB
    pieces_t = nbr_len // PIECE_T
    pieces_f = d_part // PIECE_F
    per_shard = database.shape[0]
    index = (nbr_shard * per_shard + nbr_row).reshape(-1)
    everyone = lax.all_gather(index, "seq", axis=0, tiled=True)
    cut = database.reshape(per_shard, pieces_t, PIECE_T, pieces_f, PIECE_F)
    cut = cut.transpose(1, 3, 0, 2, 4).reshape(n_seq, per_shard, PIECE_T, PIECE_F)
    spread = lax.all_to_all(cut, "seq", split_axis=0, concat_axis=0, tiled=True)
    spread = spread.reshape(n_seq * per_shard, PIECE_T, PIECE_F)
    outgoing = spread[everyone].reshape(n_seq, items, PIECE_T, PIECE_F)
    replies = lax.all_to_all(outgoing, "seq", split_axis=0, concat_axis=0, tiled=True)
    rows = replies.reshape(pieces_t, pieces_f, items, PIECE_T, PIECE_F)
    rows = rows.transpose(2, 0, 3, 1, 4).reshape(items, nbr_len, d_part)
    whole = lax.all_gather(tokens, "tensor", axis=1, tiled=True)
    normed = rms_scale(whole, x_gain)
    queries = (jnp.dot(normed, wq, preferred_element_type=jnp.float32) * HS ** (-0.5)).astype(
        jnp.bfloat16
    )
    n_rows = items * nbr_len
    full_rows = lax.all_gather(rows, "tensor", axis=2, tiled=True)
    encoded = rms_scale(full_rows, nbr_gain).reshape(n_rows, d_part * n_ten)
    keys = jnp.dot(encoded, wk, preferred_element_type=jnp.float32).astype(jnp.bfloat16)
    values = jnp.dot(encoded, wv, preferred_element_type=jnp.float32).astype(jnp.bfloat16)
    key_spans = keys.reshape(span_dev, NB * nbr_len, heads_dev, HS)
    value_spans = values.reshape(span_dev, NB * nbr_len, heads_dev, HS)
    lead = jnp.zeros((1, head_cols), jnp.bfloat16)
    tail = jnp.zeros((span_len - 1, head_cols), jnp.bfloat16)
    query_blocks = jnp.concatenate([lead, queries, tail], axis=0).reshape(
        span_dev + 1, span_len, heads_dev, HS
    )
    prev_keys, prev_values, prev_count = passed_along(
        (key_spans[-1], value_spans[-1], nbr_count[-1:]), "seq", 1
    )
    all_keys = jnp.concatenate([prev_keys[None], key_spans], axis=0)
    all_values = jnp.concatenate([prev_values[None], value_spans], axis=0)
    counts = jnp.concatenate([prev_count, nbr_count], axis=0)
    result = attend(query_blocks, all_keys, all_values, counts)
    attended = result.reshape((span_dev + 1) * span_len, head_cols)[1 : 1 + tok_dev]
    part = jnp.dot(attended, wo, preferred_element_type=jnp.float32).astype(jnp.bfloat16)
    part = lax.optimization_barrier(part)
    summed = lax.psum_scatter(
        part.astype(jnp.float32).astype(jnp.bfloat16), "tensor", scatter_dimension=1, tiled=True
    ).astype(jnp.float32)
    return (tokens.astype(jnp.float32) + summed).astype(jnp.bfloat16)


def solution(mesh):
    placed = (
        P("seq", "tensor"),
        P(),
        P(),
        P("seq", None, "tensor"),
        P("seq", None),
        P("seq", None),
        P("seq"),
        P(None, "tensor"),
        P(None, "tensor"),
        P(None, "tensor"),
        P("tensor", None),
    )
    return jax.shard_map(
        body, mesh=mesh, in_specs=placed, out_specs=P("seq", "tensor"), check_vma=False
    )
```

```python
import functools

import jax
import jax.numpy as jnp
from jax import lax
from jax.experimental import pallas as pl
from jax.experimental.pallas import tpu as pltpu
from jax.sharding import PartitionSpec as P

HS = 128
NB = 2
PIECE_T = 16
PIECE_F = 128
VMEM_LIMIT = 48 * 1024 * 1024


def rms_scale(rows, gain):
    values = rows.astype(jnp.float32)
    inverse = lax.rsqrt(jnp.mean(values * values, axis=-1, keepdims=True) + 1e-06)
    return (values * inverse * gain.astype(jnp.float32)).astype(jnp.bfloat16)


def cut_kernel(db_ref, note_ref, out_ref, sems):
    shard = db_ref.shape[0]
    pieces_t = db_ref.shape[1] // PIECE_T
    pieces_f = db_ref.shape[2] // PIECE_F
    copies = []
    for f in range(pieces_f):
        for i in range(pieces_t):
            piece = f * pieces_t + i
            source = db_ref.at[:, pl.ds(i * PIECE_T, PIECE_T), pl.ds(f * PIECE_F, PIECE_F)]
            copies.append(
                pltpu.make_async_copy(
                    source, out_ref.at[piece, pl.ds(0, shard)], sems.at[0, piece]
                )
            )
            copies.append(
                pltpu.make_async_copy(note_ref, out_ref.at[piece, shard], sems.at[1, piece])
            )
    for copy in copies:
        copy.start()
    for copy in copies:
        copy.wait()


def cut(database, note):
    shard, length, part = database.shape
    pieces = (length // PIECE_T) * (part // PIECE_F)
    return pl.pallas_call(
        cut_kernel,
        in_specs=[pl.BlockSpec(memory_space=pl.ANY)] * 2,
        out_specs=pl.BlockSpec(memory_space=pl.ANY),
        out_shape=jax.ShapeDtypeStruct((pieces, shard + 1, PIECE_T, PIECE_F), database.dtype),
        scratch_shapes=[pltpu.SemaphoreType.DMA((2, pieces))],
        name="cut",
    )(database, note)


def pick_kernel(index_ref, spread_ref, low_ref, high_ref):
    n_seq, half = low_ref.shape[:2]

    def one(dest, carry):
        for j in range(half):
            low_ref[dest, j] = spread_ref[index_ref[dest, j]]
            high_ref[dest, j] = spread_ref[index_ref[dest, half + j]]
        return carry

    lax.fori_loop(0, n_seq, one, 0, unroll=2)


def pick(index, spread):
    n_seq, items = index.shape
    half = jax.ShapeDtypeStruct((n_seq, items // 2, PIECE_T, PIECE_F), spread.dtype)
    return pl.pallas_call(
        pick_kernel,
        in_specs=[
            pl.BlockSpec(memory_space=pltpu.SMEM),
            pl.BlockSpec(memory_space=pltpu.VMEM),
        ],
        out_specs=[pl.BlockSpec(memory_space=pltpu.VMEM)] * 2,
        out_shape=[half, half],
        name="pick",
    )(index, spread)


def add_block(x_ref, w_ref, start, acc, squares):
    features, pieces_t, items = x_ref.shape[:3]
    rows = pieces_t * items * PIECE_T
    pieces = [x_ref[f].reshape(rows, PIECE_F) for f in range(features)]
    for piece in pieces:
        wide = piece.astype(jnp.float32)
        squares = squares + wide * wide
    x = jnp.concatenate(pieces, axis=1)
    w = w_ref[0, start * PIECE_F : (start + features) * PIECE_F, :]
    return acc + jnp.dot(x, w, preferred_element_type=jnp.float32), squares


def gather_kernel(starts, last, where_ref, wr_ref, wl_ref, *rest):
    count = len(starts)
    x_refs = rest[:count]
    rest = rest[count:]
    if last:
        acc_ref, squares_ref, first_ref, second_ref = rest
        acc, squares = acc_ref[...], squares_ref[...]
    elif len(rest) == 4:
        acc_in_ref, squares_in_ref, acc_ref, squares_ref = rest
        acc, squares = acc_in_ref[...], squares_in_ref[...]
    else:
        acc_ref, squares_ref = rest
        acc = jnp.zeros(acc_ref.shape, jnp.float32)
        squares = jnp.zeros(squares_ref.shape, jnp.float32)
    for ref, (side, start) in zip(x_refs, starts):
        acc, squares = add_block(ref, (wr_ref, wl_ref)[side], start, acc, squares)
    if not last:
        acc_ref[...] = acc
        squares_ref[...] = squares
        return
    mean = jnp.sum(squares, axis=1, keepdims=True) * (1.0 / last)
    done = (acc * lax.rsqrt(mean + 1e-06)).astype(jnp.bfloat16)
    pieces_t, half_items = first_ref.shape[:2]
    done = done.reshape(pieces_t, 2 * half_items, PIECE_T, done.shape[-1])
    first_ref[...] = done[:, :half_items]
    second_ref[...] = done[:, half_items:]


def gather_step(blocks, starts, where, weights, state, last):
    n_ten, part, cols = weights.shape
    _, pieces_t, items = blocks[0].shape[:3]
    rows = pieces_t * items * PIECE_T
    vmem = pl.BlockSpec(memory_space=pltpu.VMEM)
    state = list(state)
    if last:
        span = jax.ShapeDtypeStruct((pieces_t, items // 2, PIECE_T, cols), jnp.bfloat16)
        out_shape = [span, span]
    else:
        out_shape = [
            jax.ShapeDtypeStruct((rows, cols), jnp.float32),
            jax.ShapeDtypeStruct((rows, PIECE_F), jnp.float32),
        ]
    return pl.pallas_call(
        functools.partial(gather_kernel, tuple(starts), n_ten * part if last else 0),
        grid_spec=pltpu.PrefetchScalarGridSpec(
            num_scalar_prefetch=1,
            grid=(1,),
            in_specs=[
                pl.BlockSpec((1, part, cols), lambda g, at: (at[0], 0, 0)),
                pl.BlockSpec((1, part, cols), lambda g, at: (at[1], 0, 0)),
            ]
            + [vmem] * (len(blocks) + len(state)),
            out_specs=[vmem] * 2,
        ),
        out_shape=out_shape,
        compiler_params=pltpu.CompilerParams(vmem_limit_bytes=VMEM_LIMIT),
        cost_estimate=pl.CostEstimate(
            flops=2 * rows * cols * PIECE_F * sum(b.shape[0] for b in blocks),
            bytes_accessed=2 * sum(b.size for b in blocks) + 4 * part * cols + 8 * rows * cols,
            transcendentals=0,
        ),
        name="gather_last" if last else "gather_step",
    )(where, weights, weights, *blocks, *state)


def ring_project(pair, weights, me, n_ten, between=None):
    right = [(i, (i + 1) % n_ten) for i in range(n_ten)]
    left = [(i, (i - 1) % n_ten) for i in range(n_ten)]
    width = pair[0].shape[0]
    go_right, go_left = list(pair), list(pair)
    here = jnp.stack([me, me]).astype(jnp.int32)
    state = gather_step(pair, [(0, 0), (0, width)], here, weights, (), False)
    last_step = n_ten // 2
    marks = None
    for step in range(1, last_step + 1):
        where = jnp.stack([(me + n_ten - step) % n_ten, (me + step) % n_ten]).astype(jnp.int32)
        last = step == last_step
        if last:
            half = width // 2
            go_right = [x[:half] for x in go_right]
            go_left = [x[half:] for x in go_left]
        if step == last_step - 1 and between is not None:
            *held, between = lax.optimization_barrier((*go_right, *go_left, between))
            go_right, go_left = held[:2], held[2:]
        for s in range(2):
            go_right[s] = lax.ppermute(go_right[s], "tensor", right)
            go_left[s] = lax.ppermute(go_left[s], "tensor", left)
        blocks, starts = [], []
        for s in range(2):
            blocks += [go_right[s], go_left[s]]
            starts += [(0, s * width), (1, s * width + (width // 2 if last else 0))]
        state = gather_step(blocks, starts, where, weights, state, last)
        if step == last_step - 1:
            marks = state
    return state, marks, between


def finish_kernel(shift, low_ref, high_ref, tokens_ref, out_ref):
    groups = low_ref.shape[0]
    sums = []
    for ref in (low_ref, high_ref):
        total = ref[0].astype(jnp.float32)
        for g in range(1, groups):
            total = total + ref[g].astype(jnp.float32)
        sums.append(total)
    total = pltpu.roll(jnp.concatenate(sums, axis=0), shift, 0)
    out_ref[...] = (tokens_ref[...].astype(jnp.float32) + total).astype(jnp.bfloat16)


def finish(low, high, tokens, shift):
    return pl.pallas_call(
        functools.partial(finish_kernel, shift),
        in_specs=[pl.BlockSpec(memory_space=pltpu.VMEM)] * 3,
        out_specs=pl.BlockSpec(memory_space=pltpu.VMEM),
        out_shape=jax.ShapeDtypeStruct(tokens.shape, jnp.bfloat16),
        compiler_params=pltpu.CompilerParams(vmem_limit_bytes=VMEM_LIMIT),
        name="finish",
    )(low, high, tokens)


def weigh(scores, count, keys_axis_owner):
    scores = jnp.where(keys_axis_owner < count, scores, jnp.float32(-1e30))
    top = jnp.max(scores, axis=-1, keepdims=True)
    expo = jnp.exp(scores - top)
    return expo / jnp.sum(expo, axis=-1, keepdims=True)


def scores_of(queries, keys):
    return lax.dot_general(
        queries, keys, (((1,), (1,)), ((), ())), preferred_element_type=jnp.float32
    )


def attend_kernel(with_prev, span_len, count_ref, q_ref, first_ref, second_ref, *rest):
    if with_prev:
        prev_ref, wo_ref, out_ref = rest
    else:
        wo_ref, out_ref = rest
    cols = q_ref.shape[1]
    heads = cols // HS
    keys = first_ref.shape[0] * first_ref.shape[1] * first_ref.shape[2]
    owner = (lax.broadcasted_iota(jnp.int32, (span_len, keys), 1) // PIECE_T) % NB
    row = lax.broadcasted_iota(jnp.int32, (span_len, keys), 0)
    blocks = []
    for span in range(2):
        pair_ref = (first_ref, second_ref)[span]
        pair = pair_ref[...].reshape(keys, 2 * cols)
        queries = q_ref[span * span_len : (span + 1) * span_len, :]
        mixed_heads = []
        for head in range(heads):
            at = slice(head * HS, (head + 1) * HS)
            value_at = slice(cols + head * HS, cols + (head + 1) * HS)
            query = queries[:, at]
            scores = scores_of(query, pair[:, at])
            if with_prev and span == 1:
                prev = prev_ref[...].reshape(keys, 2 * cols)
                own = row == 0
                scores = jnp.where(own, scores, scores_of(query, prev[:, at]))
                count = jnp.where(own, count_ref[1], count_ref[2])
                weights = weigh(scores, count, owner)
                ours = jnp.where(own, weights, 0.0).astype(jnp.bfloat16)
                theirs = jnp.where(own, 0.0, weights).astype(jnp.bfloat16)
                result = jnp.dot(
                    ours, pair[:, value_at], preferred_element_type=jnp.float32
                ) + jnp.dot(theirs, prev[:, value_at], preferred_element_type=jnp.float32)
            else:
                weights = weigh(scores, count_ref[span], owner).astype(jnp.bfloat16)
                result = jnp.dot(
                    weights, pair[:, value_at], preferred_element_type=jnp.float32
                )
            mixed_heads.append(result.astype(jnp.bfloat16))
        blocks.append(jnp.concatenate(mixed_heads, axis=1))
    attended = jnp.concatenate(blocks, axis=0)
    groups, _, width = out_ref.shape
    for g in range(groups):
        out_ref[g] = jnp.dot(
            attended, wo_ref[:, g * width : (g + 1) * width], preferred_element_type=jnp.float32
        ).astype(jnp.bfloat16)


def attend(counts, queries, first, second, prev, wo, groups):
    rows = queries.shape[0]
    span_len = rows // 2
    width = wo.shape[1] // groups
    with_prev = prev is not None
    operands = [counts, queries, first, second] + ([prev] if with_prev else []) + [wo]
    vmem = pl.BlockSpec(memory_space=pltpu.VMEM)
    return pl.pallas_call(
        functools.partial(attend_kernel, with_prev, span_len),
        in_specs=[pl.BlockSpec(memory_space=pltpu.SMEM)] + [vmem] * (len(operands) - 1),
        out_specs=vmem,
        out_shape=jax.ShapeDtypeStruct((groups, rows, width), jnp.bfloat16),
        compiler_params=pltpu.CompilerParams(vmem_limit_bytes=VMEM_LIMIT),
        cost_estimate=pl.CostEstimate(
            flops=2 * rows * wo.shape[0] * wo.shape[1] + 8 * rows * 256 * wo.shape[0],
            bytes_accessed=2 * (wo.size + rows * wo.shape[1] + 2 * first.size),
            transcendentals=0,
        ),
        name="attend_prev" if with_prev else "attend",
    )(*operands)


def body(tokens, x_gain, nbr_gain, database, nbr_shard, nbr_row, nbr_count, wq, wk, wv, wo):
    n_seq = lax.axis_size("seq")
    n_ten = lax.axis_size("tensor")
    tok_dev = tokens.shape[0]
    span_dev = nbr_shard.shape[0]
    span_len = tok_dev // span_dev
    shift = span_len - 1
    per_shard, nbr_len, d_part = database.shape
    items = span_dev * NB
    half = items // 2
    pieces_t = nbr_len // PIECE_T
    pieces_f = d_part // PIECE_F
    seq_at = lax.axis_index("seq")
    me = lax.axis_index("tensor")

    note = jnp.concatenate([nbr_shard.reshape(-1), nbr_row.reshape(-1), nbr_count])
    n_notes = note.shape[0]
    note = jnp.pad(note.astype(jnp.bfloat16)[None], ((0, PIECE_T - 1), (0, PIECE_F - n_notes)))
    spread = lax.all_to_all(cut(database, note), "seq", split_axis=0, concat_axis=0, tiled=True)
    notes = spread[:, per_shard, 0, :n_notes].astype(jnp.int32)
    index = notes[:, :items] * (per_shard + 1) + notes[:, items : 2 * items]
    prev_count = jnp.where(seq_at > 0, notes[jnp.maximum(seq_at - 1, 0), n_notes - 1], 0)
    low, high = pick(index, spread.reshape(n_seq * (per_shard + 1), PIECE_T, PIECE_F))
    whole = lax.all_gather(tokens, "tensor", axis=1, tiled=True)
    low, high, whole = lax.optimization_barrier((low, high, whole))
    high = lax.all_to_all(high, "seq", split_axis=0, concat_axis=0, tiled=True)
    low = lax.all_to_all(low, "seq", split_axis=0, concat_axis=0, tiled=True)

    both = jnp.concatenate([wk, wv], axis=1).astype(jnp.float32)
    both = (both * nbr_gain.astype(jnp.float32)[:, None]).astype(jnp.bfloat16)
    both = both.reshape(n_ten, d_part, both.shape[1])
    normed = rms_scale(whole, x_gain)
    queries = (jnp.dot(normed, wq, preferred_element_type=jnp.float32) * HS ** (-0.5)).astype(
        jnp.bfloat16
    )
    queries = jnp.concatenate([queries[shift:], queries[:shift]], axis=0)
    split = tok_dev // 2
    spans = span_dev // 2

    def streams(part):
        part = part.reshape(pieces_f, pieces_t, half, PIECE_T, PIECE_F)
        return [part[: pieces_f // 2], part[pieces_f // 2 :]]

    (third, fourth), marks, _ = ring_project(streams(high), both, me, n_ten)
    low_streams, _ = lax.optimization_barrier((streams(low), marks))
    prev = lax.ppermute(fourth, "seq", [(i, i + 1) for i in range(n_seq - 1)])
    high_counts = jnp.concatenate([nbr_count[spans:], prev_count[None]])
    high_part = attend(high_counts, queries[split:], third, fourth, prev, wo, n_ten)

    (first, second), _, high_part = ring_project(low_streams, both, me, n_ten, high_part)
    high_got = lax.all_to_all(high_part, "tensor", split_axis=0, concat_axis=0, tiled=True)
    low_part = attend(nbr_count[:spans], queries[:split], first, second, None, wo, n_ten)
    low_got = lax.all_to_all(low_part, "tensor", split_axis=0, concat_axis=0, tiled=True)
    return finish(low_got, high_got, tokens, shift)


def solution(mesh):
    placed = (
        P("seq", "tensor"),
        P(),
        P(),
        P("seq", None, "tensor"),
        P("seq", None),
        P("seq", None),
        P("seq"),
        P(None, "tensor"),
        P(None, "tensor"),
        P(None, "tensor"),
        P("tensor", None),
    )
    return jax.shard_map(
        body, mesh=mesh, in_specs=placed, out_specs=P("seq", "tensor"), check_vma=False
    )
```

```python
import functools

import jax
import jax.numpy as jnp
from jax import lax
from jax.experimental import pallas as pl
from jax.experimental.pallas import tpu as pltpu
from jax.sharding import PartitionSpec as P

HS = 128
NB = 2
PIECE_T = 16
PIECE_F = 128
FEW = 1
VMEM_LIMIT = 48 * 1024 * 1024


def rms_scale(rows, gain):
    values = rows.astype(jnp.float32)
    inverse = lax.rsqrt(jnp.mean(values * values, axis=-1, keepdims=True) + 1e-06)
    return (values * inverse * gain.astype(jnp.float32)).astype(jnp.bfloat16)


def cut_kernel(db_ref, note_ref, out_ref):
    shard = db_ref.shape[0]
    pieces_t = db_ref.shape[1] // PIECE_T
    pieces_f = db_ref.shape[2] // PIECE_F
    for f in range(pieces_f):
        for i in range(pieces_t):
            piece = f * pieces_t + i
            out_ref[piece, :shard] = db_ref[
                :, i * PIECE_T : (i + 1) * PIECE_T, f * PIECE_F : (f + 1) * PIECE_F
            ]
            out_ref[piece, shard] = note_ref[...]


def cut(database, note):
    shard, length, part = database.shape
    pieces = (length // PIECE_T) * (part // PIECE_F)
    vmem = pl.BlockSpec(memory_space=pltpu.VMEM)
    return pl.pallas_call(
        cut_kernel,
        in_specs=[vmem] * 2,
        out_specs=vmem,
        out_shape=jax.ShapeDtypeStruct((pieces, shard + 1, PIECE_T, PIECE_F), database.dtype),
        compiler_params=pltpu.CompilerParams(vmem_limit_bytes=VMEM_LIMIT),
        name="cut",
    )(database, note)


def pick_kernel(index_ref, spread_ref, low_ref, high_ref):
    n_seq, few = low_ref.shape[:2]

    def one(dest, carry):
        for j in range(few):
            low_ref[dest, j] = spread_ref[index_ref[dest, j]]
        for j in range(high_ref.shape[1]):
            high_ref[dest, j] = spread_ref[index_ref[dest, few + j]]
        return carry

    lax.fori_loop(0, n_seq, one, 0, unroll=2)


def pick(index, spread, few):
    n_seq, items = index.shape
    vmem = pl.BlockSpec(memory_space=pltpu.VMEM)
    return pl.pallas_call(
        pick_kernel,
        in_specs=[pl.BlockSpec(memory_space=pltpu.SMEM), vmem],
        out_specs=[vmem] * 2,
        out_shape=[
            jax.ShapeDtypeStruct((n_seq, count, PIECE_T, PIECE_F), spread.dtype)
            for count in (few, items - few)
        ],
        compiler_params=pltpu.CompilerParams(vmem_limit_bytes=VMEM_LIMIT),
        name="pick",
    )(index, spread)


def unpack(x_ref):
    features, pieces_t, items = x_ref.shape[:3]
    rows = pieces_t * items * PIECE_T
    pieces = [x_ref[f].reshape(rows, PIECE_F) for f in range(features)]
    squares = jnp.zeros((rows, PIECE_F), jnp.float32)
    for piece in pieces:
        wide = piece.astype(jnp.float32)
        squares = squares + wide * wide
    return jnp.concatenate(pieces, axis=1), squares


def store_spans(acc, squares, features, out_refs):
    mean = jnp.sum(squares, axis=1, keepdims=True) * (1.0 / features)
    done = (acc * lax.rsqrt(mean + 1e-06)).astype(jnp.bfloat16)
    pieces_t = out_refs[0].shape[0]
    done = done.reshape(pieces_t, NB * len(out_refs), PIECE_T, done.shape[-1])
    for span, ref in enumerate(out_refs):
        ref[...] = done[:, span * NB : (span + 1) * NB]


def project_kernel(x_ref, w_ref, *rest):
    spans = len(rest) - 2
    out_refs, (acc_ref, squares_ref) = rest[:spans], rest[spans:]
    step = pl.program_id(0)
    steps = pl.num_programs(0)
    x, squares = unpack(x_ref.at[0])
    term = jnp.dot(x, w_ref[0], preferred_element_type=jnp.float32)

    @pl.when(step == 0)
    def _():
        acc_ref[...] = term
        squares_ref[...] = squares

    @pl.when(step > 0)
    def _():
        acc_ref[...] += term
        squares_ref[...] += squares

    @pl.when(step == steps - 1)
    def _():
        store_spans(acc_ref[...], squares_ref[...], steps * x.shape[1], out_refs)


def project(x, weights):
    steps, pieces_f, pieces_t, items, _, _ = x.shape
    rows = pieces_t * items * PIECE_T
    _, part, cols = weights.shape
    span = jax.ShapeDtypeStruct((pieces_t, NB, PIECE_T, cols), jnp.bfloat16)
    return pl.pallas_call(
        project_kernel,
        grid=(steps,),
        in_specs=[
            pl.BlockSpec((1,) + x.shape[1:], lambda t: (t, 0, 0, 0, 0, 0)),
            pl.BlockSpec((1, part, cols), lambda t: (t, 0, 0)),
        ],
        out_specs=[pl.BlockSpec(span.shape, lambda t: (0, 0, 0, 0))] * (items // NB),
        out_shape=[span] * (items // NB),
        scratch_shapes=[
            pltpu.VMEM((rows, cols), jnp.float32),
            pltpu.VMEM((rows, PIECE_F), jnp.float32),
        ],
        compiler_params=pltpu.CompilerParams(vmem_limit_bytes=VMEM_LIMIT),
        cost_estimate=pl.CostEstimate(
            flops=8 * steps * rows * part * cols,
            bytes_accessed=2 * steps * part * (rows + cols),
            transcendentals=0,
        ),
        name="project",
    )(x, weights)


def project_blocks_kernel(places, where_ref, w_ref, *rest):
    count = len(places)
    x_refs, rest = rest[:count], rest[count:]
    spans = len(rest) - 2
    out_refs, (acc_ref, squares_ref) = rest[:spans], rest[spans:]
    for at, (x_ref, (place, start)) in enumerate(zip(x_refs, places)):
        x, squares = unpack(x_ref)
        first = start * PIECE_F
        w = w_ref[where_ref[place], first : first + x.shape[1], :]
        term = jnp.dot(x, w, preferred_element_type=jnp.float32)
        if at == 0:
            acc_ref[...] = term
            squares_ref[...] = squares
        else:
            acc_ref[...] += term
            squares_ref[...] += squares
    features = w_ref.shape[0] * w_ref.shape[1]
    store_spans(acc_ref[...], squares_ref[...], features, out_refs)


def project_blocks(blocks, places, where, weights):
    n_ten, part, cols = weights.shape
    _, pieces_t, items = blocks[0].shape[:3]
    rows = pieces_t * items * PIECE_T
    span = jax.ShapeDtypeStruct((pieces_t, NB, PIECE_T, cols), jnp.bfloat16)
    vmem = pl.BlockSpec(memory_space=pltpu.VMEM)
    return pl.pallas_call(
        functools.partial(project_blocks_kernel, tuple(places)),
        in_specs=[pl.BlockSpec(memory_space=pltpu.SMEM)] + [vmem] * (1 + len(blocks)),
        out_specs=[vmem] * (items // NB),
        out_shape=[span] * (items // NB),
        scratch_shapes=[
            pltpu.VMEM((rows, cols), jnp.float32),
            pltpu.VMEM((rows, PIECE_F), jnp.float32),
        ],
        compiler_params=pltpu.CompilerParams(vmem_limit_bytes=VMEM_LIMIT),
        cost_estimate=pl.CostEstimate(
            flops=8 * n_ten * rows * part * cols,
            bytes_accessed=2 * n_ten * part * (rows + cols),
            transcendentals=0,
        ),
        name="project_blocks",
    )(where, weights, *blocks)


def ring_gather(pair, me, n_ten):
    right = [(i, (i + 1) % n_ten) for i in range(n_ten)]
    left = [(i, (i - 1) % n_ten) for i in range(n_ten)]
    width = pair[0].shape[0]
    last = n_ten // 2
    go_right, go_left = list(pair), list(pair)
    blocks, places = list(pair), [(0, 0), (0, width)]
    marks = None
    for step in range(1, last + 1):
        half = width // 2 if step == last else 0
        if half:
            marks = go_right + go_left
            go_right = [x[:half] for x in go_right]
            go_left = [x[half:] for x in go_left]
        for s in range(2):
            go_right[s] = lax.ppermute(go_right[s], "tensor", right)
            go_left[s] = lax.ppermute(go_left[s], "tensor", left)
            blocks += [go_right[s], go_left[s]]
            places += [(n_ten - step, s * width), (step, s * width + half)]
    where = (me + jnp.arange(n_ten, dtype=jnp.int32)) % n_ten
    return blocks, places, where, marks


def weigh(scores, count, keys_axis_owner):
    scores = jnp.where(keys_axis_owner < count, scores, jnp.float32(-1e30))
    top = jnp.max(scores, axis=-1, keepdims=True)
    expo = jnp.exp(scores - top)
    return expo / jnp.sum(expo, axis=-1, keepdims=True)


def scores_of(queries, keys):
    return lax.dot_general(
        queries, keys, (((1,), (1,)), ((), ())), preferred_element_type=jnp.float32
    )


def attend_kernel(with_prev, span_len, count_ref, q_ref, *rest):
    pair_refs, prev_ref, out_ref = rest[: -2 if with_prev else -1], rest[-2], rest[-1]
    cols = q_ref.shape[1]
    heads = cols // HS
    spans = len(pair_refs)
    keys = pair_refs[0].shape[0] * pair_refs[0].shape[1] * pair_refs[0].shape[2]
    owner = (lax.broadcasted_iota(jnp.int32, (span_len, keys), 1) // PIECE_T) % NB
    row = lax.broadcasted_iota(jnp.int32, (span_len, keys), 0)
    for span in range(spans):
        pair = pair_refs[span][...].reshape(keys, 2 * cols)
        queries = q_ref[span * span_len : (span + 1) * span_len, :]
        mixed_heads = []
        for head in range(heads):
            at = slice(head * HS, (head + 1) * HS)
            value_at = slice(cols + head * HS, cols + (head + 1) * HS)
            query = queries[:, at]
            scores = scores_of(query, pair[:, at])
            if with_prev and span == spans - 1:
                prev = prev_ref[...].reshape(keys, 2 * cols)
                own = row == 0
                scores = jnp.where(own, scores, scores_of(query, prev[:, at]))
                count = jnp.where(own, count_ref[span], count_ref[span + 1])
                weights = weigh(scores, count, owner)
                ours = jnp.where(own, weights, 0.0).astype(jnp.bfloat16)
                theirs = jnp.where(own, 0.0, weights).astype(jnp.bfloat16)
                result = jnp.dot(
                    ours, pair[:, value_at], preferred_element_type=jnp.float32
                ) + jnp.dot(theirs, prev[:, value_at], preferred_element_type=jnp.float32)
            else:
                weights = weigh(scores, count_ref[span], owner).astype(jnp.bfloat16)
                result = jnp.dot(
                    weights, pair[:, value_at], preferred_element_type=jnp.float32
                )
            mixed_heads.append(result.astype(jnp.bfloat16))
        attended = jnp.concatenate(mixed_heads, axis=1)
        for g in range(out_ref.shape[0]):
            out_ref[g, span * span_len : (span + 1) * span_len, :] = attended


def attend(counts, queries, pairs, prev, groups):
    rows, cols = queries.shape
    with_prev = prev is not None
    operands = [counts, queries, *pairs] + ([prev] if with_prev else [])
    vmem = pl.BlockSpec(memory_space=pltpu.VMEM)
    return pl.pallas_call(
        functools.partial(attend_kernel, with_prev, rows // len(pairs)),
        in_specs=[pl.BlockSpec(memory_space=pltpu.SMEM)] + [vmem] * (len(operands) - 1),
        out_specs=vmem,
        out_shape=jax.ShapeDtypeStruct((groups, rows, cols), jnp.bfloat16),
        compiler_params=pltpu.CompilerParams(vmem_limit_bytes=VMEM_LIMIT),
        cost_estimate=pl.CostEstimate(
            flops=32 * rows * 256 * cols,
            bytes_accessed=2 * groups * rows * cols,
            transcendentals=0,
        ),
        name="attend_prev" if with_prev else "attend",
    )(*operands)


def sum_groups(attended_ref, wo_ref):
    total = None
    for g in range(wo_ref.shape[0]):
        part = jnp.dot(attended_ref[g], wo_ref[g], preferred_element_type=jnp.float32)
        part = part.astype(jnp.bfloat16).astype(jnp.float32)
        total = part if total is None else total + part
    return total


def output_kernel(attended_ref, wo_ref, out_ref):
    out_ref[...] = sum_groups(attended_ref, wo_ref)


def output(attended, wo):
    vmem = pl.BlockSpec(memory_space=pltpu.VMEM)
    return pl.pallas_call(
        output_kernel,
        in_specs=[vmem] * 2,
        out_specs=vmem,
        out_shape=jax.ShapeDtypeStruct((attended.shape[1], wo.shape[2]), jnp.float32),
        compiler_params=pltpu.CompilerParams(vmem_limit_bytes=VMEM_LIMIT),
        name="output",
    )(attended, wo)


def finish_kernel(shift, low_ref, high_ref, wo_ref, tokens_ref, out_ref):
    low = sum_groups(low_ref, wo_ref)
    total = pltpu.roll(jnp.concatenate([low, high_ref[...]], axis=0), shift, 0)
    out_ref[...] = (tokens_ref[...].astype(jnp.float32) + total).astype(jnp.bfloat16)


def finish(low, high, wo, tokens, shift):
    return pl.pallas_call(
        functools.partial(finish_kernel, shift),
        in_specs=[pl.BlockSpec(memory_space=pltpu.VMEM)] * 4,
        out_specs=pl.BlockSpec(memory_space=pltpu.VMEM),
        out_shape=jax.ShapeDtypeStruct(tokens.shape, jnp.bfloat16),
        compiler_params=pltpu.CompilerParams(vmem_limit_bytes=VMEM_LIMIT),
        name="finish",
    )(low, high, wo, tokens)


def body(tokens, x_gain, nbr_gain, database, nbr_shard, nbr_row, nbr_count, wq, wk, wv, wo):
    n_seq = lax.axis_size("seq")
    n_ten = lax.axis_size("tensor")
    tok_dev = tokens.shape[0]
    span_dev = nbr_shard.shape[0]
    span_len = tok_dev // span_dev
    shift = span_len - 1
    per_shard, nbr_len, d_part = database.shape
    items = span_dev * NB
    few = NB * FEW
    pieces_t = nbr_len // PIECE_T
    pieces_f = d_part // PIECE_F
    seq_at = lax.axis_index("seq")
    me = lax.axis_index("tensor")

    note = jnp.concatenate([nbr_shard.reshape(-1), nbr_row.reshape(-1), nbr_count])
    n_notes = note.shape[0]
    note = jnp.pad(note.astype(jnp.bfloat16)[None], ((0, PIECE_T - 1), (0, PIECE_F - n_notes)))
    pieces = cut(database, note)
    spread = lax.all_to_all(pieces, "seq", split_axis=0, concat_axis=0, tiled=True)
    notes = spread[:, per_shard, 0, :n_notes].astype(jnp.int32)
    index = notes[:, :items] * (per_shard + 1) + notes[:, items : 2 * items]
    prev_count = jnp.where(seq_at > 0, notes[jnp.maximum(seq_at - 1, 0), n_notes - 1], 0)
    low, high = pick(index, spread.reshape(n_seq * (per_shard + 1), PIECE_T, PIECE_F), few)

    own_rows = wo.shape[0] // n_seq
    wo_rows = lax.dynamic_slice_in_dim(wo, seq_at * own_rows, own_rows, axis=0)
    wo_rows, _ = lax.optimization_barrier((wo_rows, pieces))
    wo_rows = wo_rows.reshape(own_rows, n_ten, d_part).transpose(1, 0, 2)
    wo_rows = lax.all_to_all(wo_rows, "tensor", split_axis=0, concat_axis=0, tiled=True)

    whole = lax.all_gather(tokens, "tensor", axis=1, tiled=True)
    low, high, whole = lax.optimization_barrier((low, high, whole))
    high = lax.all_to_all(high, "seq", split_axis=0, concat_axis=0, tiled=True)
    low = lax.all_to_all(low, "seq", split_axis=0, concat_axis=0, tiled=True)
    wo_cols = lax.all_gather(wo_rows, "seq", axis=1, tiled=True)

    both = jnp.concatenate([wk, wv], axis=1).astype(jnp.float32)
    both = (both * nbr_gain.astype(jnp.float32)[:, None]).astype(jnp.bfloat16)
    both = both.reshape(n_ten, d_part, both.shape[1])

    high = high.reshape(pieces_f, pieces_t, items - few, PIECE_T, PIECE_F)
    streams = [high[: pieces_f // 2], high[pieces_f // 2 :]]
    blocks, places, where, marks = ring_gather(streams, me, n_ten)
    low, wo_cols, marks = lax.optimization_barrier((low, wo_cols, marks))
    low_x = lax.all_gather(low, "tensor", axis=0, tiled=True)
    low_x = low_x.reshape(n_ten, pieces_f, pieces_t, few, PIECE_T, PIECE_F)
    whole, blocks = lax.optimization_barrier((whole, blocks))

    *middle, final = project_blocks(blocks, places, where, both)
    prev = lax.ppermute(final, "seq", [(i, i + 1) for i in range(n_seq - 1)])
    normed = rms_scale(whole, x_gain)
    queries = (jnp.dot(normed, wq, preferred_element_type=jnp.float32) * HS ** (-0.5)).astype(
        jnp.bfloat16
    )
    queries = jnp.concatenate([queries[shift:], queries[:shift]], axis=0)
    split = FEW * span_len

    high_counts = jnp.concatenate([nbr_count[FEW:], prev_count[None]])
    high_rows = attend(high_counts, queries[split:], [*middle, final], prev, n_ten)
    high_rows = lax.all_to_all(high_rows, "tensor", split_axis=0, concat_axis=0, tiled=True)
    high_sum = output(high_rows, wo_cols)

    low_x, high_sum = lax.optimization_barrier((low_x, high_sum))
    low_rows = attend(nbr_count[:FEW], queries[:split], project(low_x, both), None, n_ten)
    low_rows = lax.all_to_all(low_rows, "tensor", split_axis=0, concat_axis=0, tiled=True)
    return finish(low_rows, high_sum, wo_cols, tokens, shift)


def solution(mesh):
    placed = (
        P("seq", "tensor"),
        P(),
        P(),
        P("seq", None, "tensor"),
        P("seq", None),
        P("seq", None),
        P("seq"),
        P(None, "tensor"),
        P(None, "tensor"),
        P(None, "tensor"),
        P("tensor", None),
    )
    return jax.shard_map(
        body, mesh=mesh, in_specs=placed, out_specs=P("seq", "tensor"), check_vma=False
    )
```

```python
import functools

import jax
import jax.numpy as jnp
from jax import lax
from jax.experimental import pallas as pl
from jax.experimental.pallas import tpu as pltpu
from jax.sharding import PartitionSpec as P

HS = 128
NB = 2
PIECE_T = 16
PIECE_F = 128
FEW = 1
PIECES_WO = 2
VMEM_LIMIT = 48 * 1024 * 1024


def cut_kernel(shard_ref, row_ref, count_ref, db_ref, out_ref):
    shard = db_ref.shape[0]
    pieces_t = db_ref.shape[1] // PIECE_T
    pieces_f = db_ref.shape[2] // PIECE_F
    spans, each = shard_ref.shape
    lane = lax.broadcasted_iota(jnp.int32, (PIECE_T, PIECE_F), 1)
    note = jnp.zeros((PIECE_T, PIECE_F), jnp.int32)
    for span in range(spans):
        for j in range(each):
            at = span * each + j
            note = jnp.where(lane == at, shard_ref[span, j], note)
            note = jnp.where(lane == spans * each + at, row_ref[span, j], note)
        note = jnp.where(lane == 2 * spans * each + span, count_ref[span], note)
    note = note.astype(jnp.float32).astype(jnp.bfloat16)
    for f in range(pieces_f):
        for i in range(pieces_t):
            piece = f * pieces_t + i
            out_ref[piece, :shard] = db_ref[
                :, i * PIECE_T : (i + 1) * PIECE_T, f * PIECE_F : (f + 1) * PIECE_F
            ]
            out_ref[piece, shard] = note


def cut(nbr_shard, nbr_row, nbr_count, database):
    shard, length, part = database.shape
    pieces = (length // PIECE_T) * (part // PIECE_F)
    vmem = pl.BlockSpec(memory_space=pltpu.VMEM)
    return pl.pallas_call(
        cut_kernel,
        in_specs=[pl.BlockSpec(memory_space=pltpu.SMEM)] * 3 + [vmem],
        out_specs=vmem,
        out_shape=jax.ShapeDtypeStruct((pieces, shard + 1, PIECE_T, PIECE_F), database.dtype),
        compiler_params=pltpu.CompilerParams(vmem_limit_bytes=VMEM_LIMIT),
        name="cut",
    )(nbr_shard, nbr_row, nbr_count, database)


def query_kernel(shift, x_ref, gain_ref, wq_ref, out_ref):
    groups, _, part = x_ref.shape
    rows = out_ref.shape[0]
    squares = jnp.zeros((rows, PIECE_F), jnp.float32)
    for g in range(groups):
        for f in range(0, part, PIECE_F):
            wide = x_ref[g, :rows, f : f + PIECE_F].astype(jnp.float32)
            squares = squares + wide * wide
    mean = jnp.sum(squares, axis=1, keepdims=True) * (1.0 / (groups * part))
    inverse = lax.rsqrt(mean + 1e-06)
    total = jnp.zeros(out_ref.shape, jnp.float32)
    for g in range(groups):
        wide = x_ref[g, :rows, :].astype(jnp.float32)
        normed = (wide * inverse * gain_ref[g].astype(jnp.float32)).astype(jnp.bfloat16)
        total = total + jnp.dot(normed, wq_ref[g], preferred_element_type=jnp.float32)
    total = pltpu.roll(total * HS ** (-0.5), rows - shift, 0)
    out_ref[...] = total.astype(jnp.bfloat16)


def query(x, gain, wq, rows, shift):
    groups, _, part = x.shape
    vmem = pl.BlockSpec(memory_space=pltpu.VMEM)
    cols = wq.shape[1]
    return pl.pallas_call(
        functools.partial(query_kernel, shift),
        in_specs=[vmem] * 3,
        out_specs=vmem,
        out_shape=jax.ShapeDtypeStruct((rows, cols), jnp.bfloat16),
        compiler_params=pltpu.CompilerParams(vmem_limit_bytes=VMEM_LIMIT),
        cost_estimate=pl.CostEstimate(
            flops=8 * rows * groups * part * cols,
            bytes_accessed=4 * groups * part * (rows + cols),
            transcendentals=0,
        ),
        name="query",
    )(x, gain.reshape(groups, 1, part), wq.reshape(groups, part, cols))


def pick_kernel(index_ref, spread_ref, low_ref, high_ref):
    n_seq, few = low_ref.shape[:2]

    def one(dest, carry):
        for j in range(few):
            low_ref[dest, j] = spread_ref[index_ref[dest, j]]
        for j in range(high_ref.shape[1]):
            high_ref[dest, j] = spread_ref[index_ref[dest, few + j]]
        return carry

    lax.fori_loop(0, n_seq, one, 0, unroll=2)


def pick(index, spread, few):
    n_seq, items = index.shape
    vmem = pl.BlockSpec(memory_space=pltpu.VMEM)
    return pl.pallas_call(
        pick_kernel,
        in_specs=[pl.BlockSpec(memory_space=pltpu.SMEM), vmem],
        out_specs=[vmem] * 2,
        out_shape=[
            jax.ShapeDtypeStruct((n_seq, count, PIECE_T, PIECE_F), spread.dtype)
            for count in (few, items - few)
        ],
        compiler_params=pltpu.CompilerParams(vmem_limit_bytes=VMEM_LIMIT),
        name="pick",
    )(index, spread)


def unpack(x_ref):
    features, pieces_t, items = x_ref.shape[:3]
    rows = pieces_t * items * PIECE_T
    pieces = [x_ref[f].reshape(rows, PIECE_F) for f in range(features)]
    squares = jnp.zeros((rows, PIECE_F), jnp.float32)
    for piece in pieces:
        wide = piece.astype(jnp.float32)
        squares = squares + wide * wide
    return jnp.concatenate(pieces, axis=1), squares


def store_spans(acc, squares, features, out_refs):
    mean = jnp.sum(squares, axis=1, keepdims=True) * (1.0 / features)
    done = (acc * lax.rsqrt(mean + 1e-06)).astype(jnp.bfloat16)
    pieces_t = out_refs[0].shape[0]
    done = done.reshape(pieces_t, NB * len(out_refs), PIECE_T, done.shape[-1])
    for span, ref in enumerate(out_refs):
        ref[...] = done[:, span * NB : (span + 1) * NB]


def project_blocks_kernel(places, where_ref, w_ref, *rest):
    count = len(places)
    x_refs, rest = rest[:count], rest[count:]
    spans = len(rest) - 2
    out_refs, (acc_ref, squares_ref) = rest[:spans], rest[spans:]
    for at, (x_ref, (place, start)) in enumerate(zip(x_refs, places)):
        x, squares = unpack(x_ref)
        first = start * PIECE_F
        w = w_ref[where_ref[place], first : first + x.shape[1], :]
        term = jnp.dot(x, w, preferred_element_type=jnp.float32)
        if at == 0:
            acc_ref[...] = term
            squares_ref[...] = squares
        else:
            acc_ref[...] += term
            squares_ref[...] += squares
    features = w_ref.shape[0] * w_ref.shape[1]
    store_spans(acc_ref[...], squares_ref[...], features, out_refs)


def project_blocks(blocks, places, where, weights):
    n_ten, part, cols = weights.shape
    _, pieces_t, items = blocks[0].shape[:3]
    rows = pieces_t * items * PIECE_T
    span = jax.ShapeDtypeStruct((pieces_t, NB, PIECE_T, cols), jnp.bfloat16)
    vmem = pl.BlockSpec(memory_space=pltpu.VMEM)
    return pl.pallas_call(
        functools.partial(project_blocks_kernel, tuple(places)),
        in_specs=[pl.BlockSpec(memory_space=pltpu.SMEM)] + [vmem] * (1 + len(blocks)),
        out_specs=[vmem] * (items // NB),
        out_shape=[span] * (items // NB),
        scratch_shapes=[
            pltpu.VMEM((rows, cols), jnp.float32),
            pltpu.VMEM((rows, PIECE_F), jnp.float32),
        ],
        compiler_params=pltpu.CompilerParams(vmem_limit_bytes=VMEM_LIMIT),
        cost_estimate=pl.CostEstimate(
            flops=8 * n_ten * rows * part * cols,
            bytes_accessed=2 * n_ten * part * (rows + cols),
            transcendentals=0,
        ),
        name="project_blocks",
    )(where, weights, *blocks)


def ring_gather(streams, me, n_ten):
    right = [(i, (i + 1) % n_ten) for i in range(n_ten)]
    left = [(i, (i - 1) % n_ten) for i in range(n_ten)]
    width = streams[0].shape[0]
    last = n_ten // 2
    go_right, go_left = list(streams), list(streams)
    blocks = list(streams)
    places = [(0, s * width) for s in range(len(streams))]
    arrivals = []
    for step in range(1, last):
        for s in range(len(streams)):
            go_right[s] = lax.ppermute(go_right[s], "tensor", right)
            go_left[s] = lax.ppermute(go_left[s], "tensor", left)
            blocks += [go_right[s], go_left[s]]
            places += [(n_ten - step, s * width), (step, s * width)]
        arrivals.append(go_right + go_left)
    if len(streams) == 2:
        from_left, from_right, start = go_right[0], go_left[1], width
    else:
        start = width // 2
        from_left, from_right = go_right[0][:start], go_left[0][start:]
    blocks += [
        lax.ppermute(from_left, "tensor", right),
        lax.ppermute(from_right, "tensor", left),
    ]
    places += [(last, 0), (last, start)]
    where = (me + jnp.arange(n_ten, dtype=jnp.int32)) % n_ten
    return blocks, places, where, arrivals


def weigh(scores, count, keys_axis_owner):
    scores = jnp.where(keys_axis_owner < count, scores, jnp.float32(-1e30))
    top = jnp.max(scores, axis=-1, keepdims=True)
    expo = jnp.exp(scores - top)
    return expo / jnp.sum(expo, axis=-1, keepdims=True)


def scores_of(queries, keys):
    return lax.dot_general(
        queries, keys, (((1,), (1,)), ((), ())), preferred_element_type=jnp.float32
    )


def attend_kernel(with_prev, span_len, count_ref, q_ref, *rest):
    pair_refs, prev_ref, out_ref = rest[: -2 if with_prev else -1], rest[-2], rest[-1]
    cols = q_ref.shape[1]
    heads = cols // HS
    spans = len(pair_refs)
    keys = pair_refs[0].shape[0] * pair_refs[0].shape[1] * pair_refs[0].shape[2]
    owner = (lax.broadcasted_iota(jnp.int32, (span_len, keys), 1) // PIECE_T) % NB
    row = lax.broadcasted_iota(jnp.int32, (span_len, keys), 0)
    for span in range(spans):
        pair = pair_refs[span][...].reshape(keys, 2 * cols)
        queries = q_ref[span * span_len : (span + 1) * span_len, :]
        mixed_heads = []
        for head in range(heads):
            at = slice(head * HS, (head + 1) * HS)
            value_at = slice(cols + head * HS, cols + (head + 1) * HS)
            query = queries[:, at]
            scores = scores_of(query, pair[:, at])
            if with_prev and span == spans - 1:
                prev = prev_ref[...].reshape(keys, 2 * cols)
                own = row == 0
                scores = jnp.where(own, scores, scores_of(query, prev[:, at]))
                count = jnp.where(own, count_ref[span], count_ref[span + 1])
                weights = weigh(scores, count, owner)
                ours = jnp.where(own, weights, 0.0).astype(jnp.bfloat16)
                theirs = jnp.where(own, 0.0, weights).astype(jnp.bfloat16)
                result = jnp.dot(
                    ours, pair[:, value_at], preferred_element_type=jnp.float32
                ) + jnp.dot(theirs, prev[:, value_at], preferred_element_type=jnp.float32)
            else:
                weights = weigh(scores, count_ref[span], owner).astype(jnp.bfloat16)
                result = jnp.dot(
                    weights, pair[:, value_at], preferred_element_type=jnp.float32
                )
            mixed_heads.append(result.astype(jnp.bfloat16))
        attended = jnp.concatenate(mixed_heads, axis=1)
        for g in range(out_ref.shape[0]):
            out_ref[g, span * span_len : (span + 1) * span_len, :] = attended


def attend(counts, queries, pairs, prev, groups):
    rows, cols = queries.shape
    with_prev = prev is not None
    operands = [counts, queries, *pairs] + ([prev] if with_prev else [])
    vmem = pl.BlockSpec(memory_space=pltpu.VMEM)
    return pl.pallas_call(
        functools.partial(attend_kernel, with_prev, rows // len(pairs)),
        in_specs=[pl.BlockSpec(memory_space=pltpu.SMEM)] + [vmem] * (len(operands) - 1),
        out_specs=vmem,
        out_shape=jax.ShapeDtypeStruct((groups, rows, cols), jnp.bfloat16),
        compiler_params=pltpu.CompilerParams(vmem_limit_bytes=VMEM_LIMIT),
        cost_estimate=pl.CostEstimate(
            flops=32 * rows * 256 * cols,
            bytes_accessed=2 * groups * rows * cols,
            transcendentals=0,
        ),
        name="attend_prev" if with_prev else "attend",
    )(*operands)


def sum_groups(attended_ref, mail_ref):
    total = None
    per_group = PIECES_WO
    first = mail_ref.shape[2] - per_group * attended_ref.shape[0]
    depth = attended_ref.shape[2]
    for g in range(attended_ref.shape[0]):
        tiles = [
            mail_ref[:, h, first + g * per_group + f].reshape(depth, PIECE_F)
            for h in range(mail_ref.shape[1])
            for f in range(per_group)
        ]
        wo = jnp.concatenate(tiles, axis=1)
        part = jnp.dot(attended_ref[g], wo, preferred_element_type=jnp.float32)
        part = part.astype(jnp.bfloat16).astype(jnp.float32)
        total = part if total is None else total + part
    return total


def output_kernel(attended_ref, wo_ref, out_ref):
    out_ref[...] = sum_groups(attended_ref, wo_ref)


def output(attended, wo, width):
    vmem = pl.BlockSpec(memory_space=pltpu.VMEM)
    return pl.pallas_call(
        output_kernel,
        in_specs=[vmem] * 2,
        out_specs=vmem,
        out_shape=jax.ShapeDtypeStruct((attended.shape[1], width), jnp.float32),
        compiler_params=pltpu.CompilerParams(vmem_limit_bytes=VMEM_LIMIT),
        name="output",
    )(attended, wo)


def finish_kernel(shift, low_ref, high_ref, wo_ref, tokens_ref, out_ref):
    low = sum_groups(low_ref, wo_ref)
    total = pltpu.roll(jnp.concatenate([low, high_ref[...]], axis=0), shift, 0)
    out_ref[...] = (tokens_ref[...].astype(jnp.float32) + total).astype(jnp.bfloat16)


def finish(low, high, wo, tokens, shift):
    return pl.pallas_call(
        functools.partial(finish_kernel, shift),
        in_specs=[pl.BlockSpec(memory_space=pltpu.VMEM)] * 4,
        out_specs=pl.BlockSpec(memory_space=pltpu.VMEM),
        out_shape=jax.ShapeDtypeStruct(tokens.shape, jnp.bfloat16),
        compiler_params=pltpu.CompilerParams(vmem_limit_bytes=VMEM_LIMIT),
        name="finish",
    )(low, high, wo, tokens)


def body(tokens, x_gain, nbr_gain, database, nbr_shard, nbr_row, nbr_count, wq, wk, wv, wo):
    n_seq = lax.axis_size("seq")
    n_ten = lax.axis_size("tensor")
    tok_dev = tokens.shape[0]
    span_dev = nbr_shard.shape[0]
    span_len = tok_dev // span_dev
    shift = span_len - 1
    per_shard, nbr_len, d_part = database.shape
    items = span_dev * NB
    few = NB * FEW
    pieces_t = nbr_len // PIECE_T
    pieces_f = d_part // PIECE_F
    seq_at = lax.axis_index("seq")
    me = lax.axis_index("tensor")

    pieces = cut(nbr_shard, nbr_row, nbr_count, database)
    spread = lax.all_to_all(pieces, "seq", split_axis=0, concat_axis=0, tiled=True)
    n_notes = 2 * items + span_dev
    notes = spread[:, per_shard, 0, :n_notes].astype(jnp.int32)
    index = notes[:, :items] * (per_shard + 1) + notes[:, items : 2 * items]
    prev_count = jnp.where(seq_at > 0, notes[jnp.maximum(seq_at - 1, 0), n_notes - 1], 0)
    low, high = pick(index, spread.reshape(n_seq * (per_shard + 1), PIECE_T, PIECE_F), few)

    halves = d_part // (PIECES_WO * PIECE_F)
    strips = n_seq // halves
    depth = wo.shape[0] // strips
    own = wo.reshape(strips, depth, n_ten, halves, PIECES_WO * PIECE_F)
    own = lax.dynamic_slice(
        own,
        (seq_at // halves, 0, 0, seq_at % halves, 0),
        (1, depth, n_ten, 1, PIECES_WO * PIECE_F),
    )
    own = own.reshape(depth, n_ten, PIECES_WO * PIECE_F).transpose(1, 0, 2)
    own = own.reshape(n_ten, depth // halves, d_part)
    letters = jnp.broadcast_to(tokens[None], (n_ten,) + tokens.shape)
    letters = jnp.concatenate([letters, own], axis=1)
    letters, _ = lax.optimization_barrier((letters, pieces))
    letters = lax.all_to_all(letters, "tensor", split_axis=0, concat_axis=0, tiled=True)

    both = jnp.concatenate([wk, wv], axis=1).astype(jnp.float32)
    both = (both * nbr_gain.astype(jnp.float32)[:, None]).astype(jnp.bfloat16)
    both = both.reshape(n_ten, d_part, both.shape[1])
    high, both = lax.optimization_barrier((high, both))
    high = lax.all_to_all(high, "seq", split_axis=0, concat_axis=0, tiled=True)
    high = high.reshape(pieces_f, pieces_t, items - few, PIECE_T, PIECE_F)
    streams = [high[: pieces_f // 2], high[pieces_f // 2 :]]
    streams, letters = lax.optimization_barrier((streams, letters))
    blocks, places, where, arrivals = ring_gather(streams, me, n_ten)

    letters, low, _ = lax.optimization_barrier((letters, low, arrivals[0]))
    strip = letters[:, tok_dev:].reshape(n_ten, depth, PIECES_WO, PIECE_F)
    strip = strip.transpose(0, 2, 1, 3).reshape(1, n_ten * PIECES_WO, depth, PIECE_F)
    mail = jnp.concatenate([low, jnp.broadcast_to(strip, (n_seq,) + strip.shape[1:])], axis=1)
    mail = lax.all_to_all(mail, "seq", split_axis=0, concat_axis=0, tiled=True)
    low = mail[:, :few].reshape(pieces_f, pieces_t, few, PIECE_T, PIECE_F)
    mail = mail.reshape(strips, halves, *mail.shape[1:])
    queries = query(letters, x_gain, wq, tok_dev, shift)
    split = FEW * span_len

    low, queries, _ = lax.optimization_barrier((low, queries, arrivals[-1]))
    low_blocks, low_places, _, low_arrivals = ring_gather([low], me, n_ten)

    blocks, _ = lax.optimization_barrier((blocks, low_arrivals[0]))
    *middle, final = project_blocks(blocks, places, where, both)
    prev = lax.ppermute(final, "seq", [(i, i + 1) for i in range(n_seq - 1)])
    prev, _ = lax.optimization_barrier((prev, low_arrivals[1]))
    high_counts = jnp.concatenate([nbr_count[FEW:], prev_count[None]])
    high_rows = attend(high_counts, queries[split:], [*middle, final], prev, n_ten)
    low_blocks, _ = lax.optimization_barrier((low_blocks, high_rows))
    high_rows = lax.all_to_all(high_rows, "tensor", split_axis=0, concat_axis=0, tiled=True)
    high_sum = output(high_rows, mail, d_part)

    low_spans = project_blocks(low_blocks, low_places, where, both)
    low_rows = attend(nbr_count[:FEW], queries[:split], low_spans, None, n_ten)
    low_rows = lax.all_to_all(low_rows, "tensor", split_axis=0, concat_axis=0, tiled=True)
    return finish(low_rows, high_sum, mail, tokens, shift)


def solution(mesh):
    placed = (
        P("seq", "tensor"),
        P(),
        P(),
        P("seq", None, "tensor"),
        P("seq", None),
        P("seq", None),
        P("seq"),
        P(None, "tensor"),
        P(None, "tensor"),
        P(None, "tensor"),
        P("tensor", None),
    )
    return jax.shard_map(
        body, mesh=mesh, in_specs=placed, out_specs=P("seq", "tensor"), check_vma=False
    )
```

```python
import functools

import jax
import jax.numpy as jnp
from jax import lax
from jax.experimental import pallas as pl
from jax.experimental.pallas import tpu as pltpu
from jax.sharding import PartitionSpec as P

HS = 128
NB = 2
PIECE_T = 16
PIECE_F = 128
PIECES_WO = 2
RING_ORDER = (0, 7, 1, 6, 2, 5, 3, 4)
VMEM_LIMIT = 48 * 1024 * 1024


def cut_kernel(shard_ref, row_ref, count_ref, db_ref, out_ref):
    shard = db_ref.shape[0]
    pieces_t = db_ref.shape[1] // PIECE_T
    pieces_f = db_ref.shape[2] // PIECE_F
    spans, each = shard_ref.shape
    lane = lax.broadcasted_iota(jnp.int32, (PIECE_T, PIECE_F), 1)
    note = jnp.zeros((PIECE_T, PIECE_F), jnp.int32)
    for span in range(spans):
        for j in range(each):
            at = span * each + j
            note = jnp.where(lane == at, shard_ref[span, j], note)
            note = jnp.where(lane == spans * each + at, row_ref[span, j], note)
        note = jnp.where(lane == 2 * spans * each + span, count_ref[span], note)
    note = note.astype(jnp.float32).astype(jnp.bfloat16)
    for f in range(pieces_f):
        for i in range(pieces_t):
            piece = f * pieces_t + i
            out_ref[piece, :shard] = db_ref[
                :, i * PIECE_T : (i + 1) * PIECE_T, f * PIECE_F : (f + 1) * PIECE_F
            ]
            out_ref[piece, shard] = note


def cut(nbr_shard, nbr_row, nbr_count, database):
    shard, length, part = database.shape
    pieces = (length // PIECE_T) * (part // PIECE_F)
    vmem = pl.BlockSpec(memory_space=pltpu.VMEM)
    return pl.pallas_call(
        cut_kernel,
        in_specs=[pl.BlockSpec(memory_space=pltpu.SMEM)] * 3 + [vmem],
        out_specs=vmem,
        out_shape=jax.ShapeDtypeStruct((pieces, shard + 1, PIECE_T, PIECE_F), database.dtype),
        compiler_params=pltpu.CompilerParams(vmem_limit_bytes=VMEM_LIMIT),
        name="cut",
    )(nbr_shard, nbr_row, nbr_count, database)


def pick_kernel(index_ref, spread_ref, out_ref):
    n_seq, items = out_ref.shape[:2]

    def one(dest, carry):
        for j in range(items):
            out_ref[dest, j] = spread_ref[index_ref[dest, j]]
        return carry

    lax.fori_loop(0, n_seq, one, 0, unroll=2)


def pick(index, spread):
    vmem = pl.BlockSpec(memory_space=pltpu.VMEM)
    return pl.pallas_call(
        pick_kernel,
        in_specs=[pl.BlockSpec(memory_space=pltpu.SMEM), vmem],
        out_specs=vmem,
        out_shape=jax.ShapeDtypeStruct(index.shape + (PIECE_T, PIECE_F), spread.dtype),
        compiler_params=pltpu.CompilerParams(vmem_limit_bytes=VMEM_LIMIT),
        name="pick",
    )(index, spread)


def letter_kernel(at_ref, tokens_ref, wo_ref, out_ref):
    rows, part = tokens_ref.shape
    pieces_t = rows // PIECE_T
    pieces_f = part // PIECE_F
    for f in range(pieces_f):
        for i in range(pieces_t):
            out_ref[f * pieces_t + i] = tokens_ref[
                i * PIECE_T : (i + 1) * PIECE_T, f * PIECE_F : (f + 1) * PIECE_F
            ]
    strip = PIECES_WO * PIECE_F
    for group in range(wo_ref.shape[1] // part):
        for f in range(PIECES_WO):
            start = pl.multiple_of(group * part + at_ref[1] * strip + f * PIECE_F, PIECE_F)
            out_ref[pieces_f * pieces_t + group * PIECES_WO + f] = wo_ref[:, pl.ds(start, PIECE_F)]


def letter(at, tokens, wo, depth):
    rows, part = tokens.shape
    tiles = rows * part // (PIECE_T * PIECE_F) + wo.shape[1] // part * PIECES_WO
    return pl.pallas_call(
        letter_kernel,
        grid_spec=pltpu.PrefetchScalarGridSpec(
            num_scalar_prefetch=1,
            grid=(1,),
            in_specs=[
                pl.BlockSpec((rows, part), lambda g, at: (0, 0)),
                pl.BlockSpec((depth, wo.shape[1]), lambda g, at: (at[0], 0)),
            ],
            out_specs=pl.BlockSpec((tiles, PIECE_T, PIECE_F), lambda g, at: (0, 0, 0)),
        ),
        out_shape=jax.ShapeDtypeStruct((tiles, PIECE_T, PIECE_F), tokens.dtype),
        name="letter",
    )(at, tokens, wo)


def unpack(x_ref):
    features, pieces_t, items = x_ref.shape[:3]
    rows = pieces_t * items * PIECE_T
    pieces = [x_ref[f].reshape(rows, PIECE_F) for f in range(features)]
    squares = jnp.zeros((rows, PIECE_F), jnp.float32)
    for piece in pieces:
        wide = piece.astype(jnp.float32)
        squares = squares + wide * wide
    return jnp.concatenate(pieces, axis=1), squares


def store_spans(acc, squares, features, out_refs):
    mean = jnp.sum(squares, axis=1, keepdims=True) * (1.0 / features)
    done = (acc * lax.rsqrt(mean + 1e-06)).astype(jnp.bfloat16)
    pieces_t = out_refs[0].shape[0]
    done = done.reshape(pieces_t, NB * len(out_refs), PIECE_T, done.shape[-1])
    for span, ref in enumerate(out_refs):
        ref[...] = done[:, span * NB : (span + 1) * NB]


def query_kernel(shift, halved, where_ref, gain_ref, wq_ref, *rest):
    x_refs, (out_ref, strip_ref) = rest[:-2], rest[-2:]
    rows = out_ref.shape[0]
    groups, _, part = gain_ref.shape
    pieces_t = rows // PIECE_T
    tiles = pieces_t * (part // PIECE_F)
    whole = list(x_refs[:-2])

    def tile_rows(k, f):
        first = f * pieces_t
        if k < groups - 1:
            return x_refs[k][first : first + pieces_t].reshape(rows, PIECE_F)
        ref, start = (x_refs[-2], 0) if first < halved else (x_refs[-1], halved)
        return ref[first - start : first - start + pieces_t].reshape(rows, PIECE_F)

    squares = jnp.zeros((rows, PIECE_F), jnp.float32)
    for k in range(groups):
        for f in range(part // PIECE_F):
            wide = tile_rows(k, f).astype(jnp.float32)
            squares = squares + wide * wide
    mean = jnp.sum(squares, axis=1, keepdims=True) * (1.0 / (groups * part))
    inverse = lax.rsqrt(mean + 1e-06)
    total = jnp.zeros(out_ref.shape, jnp.float32)
    me = where_ref[0]
    for k in range(groups):
        group = where_ref[RING_ORDER[k]]
        x = jnp.concatenate([tile_rows(k, f) for f in range(part // PIECE_F)], axis=1)
        gain = gain_ref[group].astype(jnp.float32)
        normed = (x.astype(jnp.float32) * inverse * gain).astype(jnp.bfloat16)
        total = total + jnp.dot(normed, wq_ref[group], preferred_element_type=jnp.float32)
        for f in range(PIECES_WO):
            at = tiles + me * PIECES_WO + f
            ref = whole[k] if k < groups - 1 else x_refs[-1]
            at = at if k < groups - 1 else at - halved
            strip_ref[group * PIECES_WO + f] = ref[at]
    total = pltpu.roll(total * HS ** (-0.5), rows - shift, 0)
    out_ref[...] = total.astype(jnp.bfloat16)


def query(where, letters, gain, wq, rows, shift):
    groups = where.shape[0]
    part = wq.shape[0] // groups
    cols = wq.shape[1]
    vmem = pl.BlockSpec(memory_space=pltpu.VMEM)
    return pl.pallas_call(
        functools.partial(query_kernel, shift, letters[-2].shape[0]),
        in_specs=[pl.BlockSpec(memory_space=pltpu.SMEM)] + [vmem] * (2 + len(letters)),
        out_specs=[vmem] * 2,
        out_shape=[
            jax.ShapeDtypeStruct((rows, cols), jnp.bfloat16),
            jax.ShapeDtypeStruct((groups * PIECES_WO, PIECE_T, PIECE_F), jnp.bfloat16),
        ],
        compiler_params=pltpu.CompilerParams(vmem_limit_bytes=VMEM_LIMIT),
        cost_estimate=pl.CostEstimate(
            flops=8 * rows * groups * part * cols,
            bytes_accessed=4 * groups * part * (rows + cols),
            transcendentals=0,
        ),
        name="query",
    )(where, gain.reshape(groups, 1, part), wq.reshape(groups, part, cols), *letters)


def gather_kernel(places, first, last, where_ref, w_ref, *rest):
    count = len(places)
    x_refs, rest = rest[:count], rest[count:]
    if not first:
        acc, squares = rest[0][...], rest[1][...]
        rest = rest[2:]
    for at, (x_ref, (place, start)) in enumerate(zip(x_refs, places)):
        x, more = unpack(x_ref)
        lane = start * PIECE_F
        w = w_ref[where_ref[place], lane : lane + x.shape[1], :]
        term = jnp.dot(x, w, preferred_element_type=jnp.float32)
        if first and at == 0:
            acc, squares = term, more
        else:
            acc, squares = acc + term, squares + more
    if last:
        store_spans(acc, squares, w_ref.shape[0] * w_ref.shape[1], rest)
    else:
        rest[0][...] = acc
        rest[1][...] = squares


def gather_step(blocks, places, where, weights, state, last):
    _, part, cols = weights.shape
    _, pieces_t, items = blocks[0].shape[:3]
    rows = pieces_t * items * PIECE_T
    vmem = pl.BlockSpec(memory_space=pltpu.VMEM)
    if last:
        span = jax.ShapeDtypeStruct((pieces_t, NB, PIECE_T, cols), jnp.bfloat16)
        out_shape = [span] * (items // NB)
    else:
        out_shape = [
            jax.ShapeDtypeStruct((rows, cols), jnp.float32),
            jax.ShapeDtypeStruct((rows, PIECE_F), jnp.float32),
        ]
    return pl.pallas_call(
        functools.partial(gather_kernel, tuple(places), not state, last),
        in_specs=[pl.BlockSpec(memory_space=pltpu.SMEM)]
        + [vmem] * (1 + len(blocks) + len(state)),
        out_specs=[vmem] * len(out_shape),
        out_shape=out_shape,
        compiler_params=pltpu.CompilerParams(vmem_limit_bytes=VMEM_LIMIT),
        cost_estimate=pl.CostEstimate(
            flops=8 * rows * cols * sum(block.shape[0] for block in blocks) * PIECE_F,
            bytes_accessed=2 * sum(block.size for block in blocks) + 8 * rows * cols,
            transcendentals=0,
        ),
        name="gather_last" if last else "gather_step",
    )(where, weights, *blocks, *state)


def ring_ways(n_ten):
    right = [(i, (i + 1) % n_ten) for i in range(n_ten)]
    left = [(i, (i - 1) % n_ten) for i in range(n_ten)]
    return right, left


def ring_gather(block, n_ten, cut_at):
    right, left = ring_ways(n_ten)
    go_right = go_left = block
    blocks = [block]
    for _ in range(1, n_ten // 2):
        go_right = lax.ppermute(go_right, "tensor", right)
        go_left = lax.ppermute(go_left, "tensor", left)
        blocks += [go_right, go_left]
    return blocks + [
        lax.ppermute(go_right[:cut_at], "tensor", right),
        lax.ppermute(go_left[cut_at:], "tensor", left),
    ]


def ring_project(streams, where, weights, n_ten, beside):
    right, left = ring_ways(n_ten)
    width = streams[0].shape[0]
    go_right, go_left = list(streams), list(streams)
    state = gather_step(streams, [(0, 0), (0, width)], where, weights, (), False)
    for step in range(1, n_ten // 2):
        blocks, places = [], []
        for s in range(2):
            go_right[s] = lax.ppermute(go_right[s], "tensor", right)
            go_left[s] = lax.ppermute(go_left[s], "tensor", left)
            blocks += [go_right[s], go_left[s]]
            places += [(n_ten - step, s * width), (step, s * width)]
        state = gather_step(blocks, places, where, weights, state, False)
    from_left, from_right, beside = lax.optimization_barrier((go_right[0], go_left[1], beside))
    blocks = [
        lax.ppermute(from_left, "tensor", right),
        lax.ppermute(from_right, "tensor", left),
    ]
    places = [(n_ten // 2, 0), (n_ten // 2, width)]
    return gather_step(blocks, places, where, weights, state, True), beside


def weigh(scores, count, keys_axis_owner):
    scores = jnp.where(keys_axis_owner < count, scores, jnp.float32(-1e30))
    top = jnp.max(scores, axis=-1, keepdims=True)
    expo = jnp.exp(scores - top)
    return expo / jnp.sum(expo, axis=-1, keepdims=True)


def scores_of(queries, keys):
    return lax.dot_general(
        queries, keys, (((1,), (1,)), ((), ())), preferred_element_type=jnp.float32
    )


def attend_kernel(with_prev, span_len, count_ref, q_ref, *rest):
    out_ref = rest[-1]
    if with_prev:
        prev_ref, before_ref = rest[-3:-1]
        pair_refs = rest[:-3]
        done = before_ref.shape[0]
        out_ref[:done, :] = before_ref[...]
    else:
        pair_refs = rest[:-1]
        done = 0
    cols = out_ref.shape[1]
    heads = cols // HS
    spans = len(pair_refs)
    keys = pair_refs[0].shape[0] * pair_refs[0].shape[1] * pair_refs[0].shape[2]
    owner = (lax.broadcasted_iota(jnp.int32, (span_len, keys), 1) // PIECE_T) % NB
    row = lax.broadcasted_iota(jnp.int32, (span_len, keys), 0)
    for span in range(spans):
        pair = pair_refs[span][...].reshape(keys, 2 * cols)
        rows = slice(done + span * span_len, done + (span + 1) * span_len)
        queries = q_ref[rows, :]
        mixed_heads = []
        for head in range(heads):
            at = slice(head * HS, (head + 1) * HS)
            value_at = slice(cols + head * HS, cols + (head + 1) * HS)
            query = queries[:, at]
            scores = scores_of(query, pair[:, at])
            if with_prev:
                prev = prev_ref[...].reshape(keys, 2 * cols)
                own = row == 0
                scores = jnp.where(own, scores, scores_of(query, prev[:, at]))
                count = jnp.where(own, count_ref[span], count_ref[span + 1])
                weights = weigh(scores, count, owner)
                ours = jnp.where(own, weights, 0.0).astype(jnp.bfloat16)
                theirs = jnp.where(own, 0.0, weights).astype(jnp.bfloat16)
                result = jnp.dot(
                    ours, pair[:, value_at], preferred_element_type=jnp.float32
                ) + jnp.dot(theirs, prev[:, value_at], preferred_element_type=jnp.float32)
            else:
                weights = weigh(scores, count_ref[span], owner).astype(jnp.bfloat16)
                result = jnp.dot(
                    weights, pair[:, value_at], preferred_element_type=jnp.float32
                )
            mixed_heads.append(result.astype(jnp.bfloat16))
        out_ref[rows, :] = jnp.concatenate(mixed_heads, axis=1)


def attend(counts, queries, pairs, span_len, prev=None, before=None):
    cols = queries.shape[1]
    with_prev = prev is not None
    rows = len(pairs) * span_len + (before.shape[0] if with_prev else 0)
    operands = [counts, queries, *pairs] + ([prev, before] if with_prev else [])
    vmem = pl.BlockSpec(memory_space=pltpu.VMEM)
    return pl.pallas_call(
        functools.partial(attend_kernel, with_prev, span_len),
        in_specs=[pl.BlockSpec(memory_space=pltpu.SMEM)] + [vmem] * (len(operands) - 1),
        out_specs=vmem,
        out_shape=jax.ShapeDtypeStruct((rows, cols), jnp.bfloat16),
        compiler_params=pltpu.CompilerParams(vmem_limit_bytes=VMEM_LIMIT),
        cost_estimate=pl.CostEstimate(
            flops=32 * len(pairs) * span_len * 256 * cols,
            bytes_accessed=4 * rows * cols,
            transcendentals=0,
        ),
        name="attend_prev" if with_prev else "attend",
    )(*operands)


def finish_kernel(shift, where_ref, mail_ref, tokens_ref, *rest):
    attended_refs, out_ref = rest[:-1], rest[-1]
    groups = where_ref.shape[0]
    depth = attended_refs[0].shape[1]
    total = None
    for k in range(groups):
        group = where_ref[RING_ORDER[k]]
        if k < groups - 1:
            attended = attended_refs[k][...]
        else:
            attended = jnp.concatenate([ref[...] for ref in attended_refs[k:]], axis=0)
        tiles = [
            mail_ref[:, h, group * PIECES_WO + f].reshape(depth, PIECE_F)
            for h in range(mail_ref.shape[1])
            for f in range(PIECES_WO)
        ]
        wo = jnp.concatenate(tiles, axis=1)
        part = jnp.dot(attended, wo, preferred_element_type=jnp.float32)
        part = part.astype(jnp.bfloat16).astype(jnp.float32)
        total = part if total is None else total + part
    total = pltpu.roll(total, shift, 0)
    out_ref[...] = (tokens_ref[...].astype(jnp.float32) + total).astype(jnp.bfloat16)


def finish(where, mail, tokens, attended, shift):
    vmem = pl.BlockSpec(memory_space=pltpu.VMEM)
    return pl.pallas_call(
        functools.partial(finish_kernel, shift),
        in_specs=[pl.BlockSpec(memory_space=pltpu.SMEM)] + [vmem] * (2 + len(attended)),
        out_specs=vmem,
        out_shape=jax.ShapeDtypeStruct(tokens.shape, jnp.bfloat16),
        compiler_params=pltpu.CompilerParams(vmem_limit_bytes=VMEM_LIMIT),
        name="finish",
    )(where, mail, tokens, *attended)


def body(tokens, x_gain, nbr_gain, database, nbr_shard, nbr_row, nbr_count, wq, wk, wv, wo):
    n_seq = lax.axis_size("seq")
    n_ten = lax.axis_size("tensor")
    tok_dev = tokens.shape[0]
    span_dev = nbr_shard.shape[0]
    span_len = tok_dev // span_dev
    shift = span_len - 1
    per_shard, nbr_len, d_part = database.shape
    items = span_dev * NB
    pieces_t = nbr_len // PIECE_T
    pieces_f = d_part // PIECE_F
    seq_at = lax.axis_index("seq")
    me = lax.axis_index("tensor")
    where = ((me + jnp.arange(n_ten, dtype=jnp.int32)) % n_ten).astype(jnp.int32)

    pieces = cut(nbr_shard, nbr_row, nbr_count, database)
    spread = lax.all_to_all(pieces, "seq", split_axis=0, concat_axis=0, tiled=True)
    n_notes = 2 * items + span_dev
    notes = spread[:, per_shard, 0, :n_notes].astype(jnp.int32)
    index = notes[:, :items] * (per_shard + 1) + notes[:, items : 2 * items]
    prev_count = jnp.where(seq_at > 0, notes[jnp.maximum(seq_at - 1, 0), n_notes - 1], 0)
    picked = pick(index, spread.reshape(n_seq * (per_shard + 1), PIECE_T, PIECE_F))

    halves = d_part // (PIECES_WO * PIECE_F)
    strips = n_seq // halves
    own = jnp.stack([seq_at // halves, seq_at % halves]).astype(jnp.int32)
    own, _ = lax.optimization_barrier((own, pieces))
    mine = letter(own, tokens, wo, wo.shape[0] // strips)
    letters = ring_gather(mine, n_ten, tok_dev // PIECE_T * (pieces_f // 2))

    both = jnp.concatenate([wk, wv], axis=1).astype(jnp.float32)
    both = (both * nbr_gain.astype(jnp.float32)[:, None]).astype(jnp.bfloat16)
    both = both.reshape(n_ten, d_part, both.shape[1])
    picked, both = lax.optimization_barrier((picked, both))
    rows = lax.all_to_all(picked, "seq", split_axis=0, concat_axis=0, tiled=True)
    rows = rows.reshape(pieces_f, pieces_t, items, PIECE_T, PIECE_F)
    streams = [rows[: pieces_f // 2], rows[pieces_f // 2 :]]
    queries, strip = query(where, letters, x_gain, wq, tok_dev, shift)
    streams, queries, strip = lax.optimization_barrier((streams, queries, strip))
    mail = jnp.broadcast_to(strip[None], (n_seq,) + strip.shape)
    mail = lax.all_to_all(mail, "seq", split_axis=0, concat_axis=0, tiled=True)
    mail = mail.reshape(strips, halves, *strip.shape)

    pairs, mail = ring_project(streams, where, both, n_ten, mail)
    prev = lax.ppermute(pairs[-1], "seq", [(i, i + 1) for i in range(n_seq - 1)])
    attended = attend(nbr_count[:-1], queries, pairs[:-1], span_len)
    last_counts = jnp.stack([nbr_count[-1], prev_count])
    attended = attend(last_counts, queries, pairs[-1:], span_len, prev, attended)
    gathered = ring_gather(attended, n_ten, tok_dev // 2)
    return finish(where, mail, tokens, gathered, shift)


def solution(mesh):
    placed = (
        P("seq", "tensor"),
        P(),
        P(),
        P("seq", None, "tensor"),
        P("seq", None),
        P("seq", None),
        P("seq"),
        P(None, "tensor"),
        P(None, "tensor"),
        P(None, "tensor"),
        P("tensor", None),
    )
    return jax.shard_map(
        body, mesh=mesh, in_specs=placed, out_specs=P("seq", "tensor"), check_vma=False
    )
```

```python
import functools

import jax
import jax.numpy as jnp
from jax import lax
from jax.experimental import pallas as pl
from jax.experimental.pallas import tpu as pltpu
from jax.sharding import PartitionSpec as P

HS = 128
NB = 2
PIECE_T = 16
PIECE_F = 128
PIECES_WO = 2
RING_ORDER = (0, 7, 1, 6, 2, 5, 3, 4)
VMEM_LIMIT = 48 * 1024 * 1024


def cut_kernel(shard_ref, row_ref, count_ref, db_ref, out_ref):
    shard = db_ref.shape[0]
    pieces_t = db_ref.shape[1] // PIECE_T
    pieces_f = db_ref.shape[2] // PIECE_F
    each, spans = shard_ref.shape
    lane = lax.broadcasted_iota(jnp.int32, (PIECE_T, PIECE_F), 1)
    note = jnp.zeros((PIECE_T, PIECE_F), jnp.int32)
    for span in range(spans):
        for j in range(each):
            at = span * each + j
            note = jnp.where(lane == at, shard_ref[j, span], note)
            note = jnp.where(lane == spans * each + at, row_ref[j, span], note)
        note = jnp.where(lane == 2 * spans * each + span, count_ref[span], note)
    note = note.astype(jnp.float32).astype(jnp.bfloat16)
    for f in range(pieces_f):
        for i in range(pieces_t):
            piece = f * pieces_t + i
            out_ref[piece, :shard] = db_ref[
                :, i * PIECE_T : (i + 1) * PIECE_T, f * PIECE_F : (f + 1) * PIECE_F
            ]
            out_ref[piece, shard] = note


def cut(nbr_shard, nbr_row, nbr_count, database):
    shard, length, part = database.shape
    pieces = (length // PIECE_T) * (part // PIECE_F)
    vmem = pl.BlockSpec(memory_space=pltpu.VMEM)
    return pl.pallas_call(
        cut_kernel,
        in_specs=[pl.BlockSpec(memory_space=pltpu.SMEM)] * 3 + [vmem],
        out_specs=vmem,
        out_shape=jax.ShapeDtypeStruct((pieces, shard + 1, PIECE_T, PIECE_F), database.dtype),
        compiler_params=pltpu.CompilerParams(vmem_limit_bytes=VMEM_LIMIT),
        name="cut",
    )(nbr_shard.T, nbr_row.T, nbr_count, database)


def pick_kernel(index_ref, spread_ref, *out_refs):
    n_seq, items = out_refs[0].shape[:2]

    def one(dest, carry):
        for at, out_ref in enumerate(out_refs):
            for j in range(items):
                out_ref[dest, j] = spread_ref[index_ref[dest, at * items + j]]
        return carry

    lax.fori_loop(0, n_seq, one, 0, unroll=2)


def pick(index, spread, parts):
    vmem = pl.BlockSpec(memory_space=pltpu.VMEM)
    shape = (index.shape[0], index.shape[1] // parts, PIECE_T, PIECE_F)
    return pl.pallas_call(
        pick_kernel,
        in_specs=[pl.BlockSpec(memory_space=pltpu.SMEM), vmem],
        out_specs=[vmem] * parts,
        out_shape=[jax.ShapeDtypeStruct(shape, spread.dtype)] * parts,
        compiler_params=pltpu.CompilerParams(vmem_limit_bytes=VMEM_LIMIT),
        name="pick",
    )(index, spread)


def letter_kernel(at_ref, tokens_ref, wo_ref, out_ref):
    rows, part = tokens_ref.shape
    pieces_t = rows // PIECE_T
    pieces_f = part // PIECE_F
    for f in range(pieces_f):
        for i in range(pieces_t):
            out_ref[f * pieces_t + i] = tokens_ref[
                i * PIECE_T : (i + 1) * PIECE_T, f * PIECE_F : (f + 1) * PIECE_F
            ]
    strip = PIECES_WO * PIECE_F
    for group in range(wo_ref.shape[1] // part):
        for f in range(PIECES_WO):
            start = pl.multiple_of(group * part + at_ref[1] * strip + f * PIECE_F, PIECE_F)
            out_ref[pieces_f * pieces_t + group * PIECES_WO + f] = wo_ref[:, pl.ds(start, PIECE_F)]


def letter(at, tokens, wo, depth):
    rows, part = tokens.shape
    tiles = rows * part // (PIECE_T * PIECE_F) + wo.shape[1] // part * PIECES_WO
    return pl.pallas_call(
        letter_kernel,
        grid_spec=pltpu.PrefetchScalarGridSpec(
            num_scalar_prefetch=1,
            grid=(1,),
            in_specs=[
                pl.BlockSpec((rows, part), lambda g, at: (0, 0)),
                pl.BlockSpec((depth, wo.shape[1]), lambda g, at: (at[0], 0)),
            ],
            out_specs=pl.BlockSpec((tiles, PIECE_T, PIECE_F), lambda g, at: (0, 0, 0)),
        ),
        out_shape=jax.ShapeDtypeStruct((tiles, PIECE_T, PIECE_F), tokens.dtype),
        name="letter",
    )(at, tokens, wo)


def unpack(x_ref):
    features, pieces_t, items = x_ref.shape[:3]
    rows = pieces_t * items * PIECE_T
    pieces = [x_ref[f].reshape(rows, PIECE_F) for f in range(features)]
    squares = jnp.zeros((rows, PIECE_F), jnp.float32)
    for piece in pieces:
        wide = piece.astype(jnp.float32)
        squares = squares + wide * wide
    return jnp.concatenate(pieces, axis=1), squares


def store_spans(acc, squares, features, out_refs):
    mean = jnp.sum(squares, axis=1, keepdims=True) * (1.0 / features)
    done = (acc * lax.rsqrt(mean + 1e-06)).astype(jnp.bfloat16)
    pieces_t = out_refs[0].shape[0]
    done = done.reshape(pieces_t, NB * len(out_refs), PIECE_T, done.shape[-1])
    for span, ref in enumerate(out_refs):
        ref[...] = done[:, span * NB : (span + 1) * NB]


def query_kernel(shift, halved, where_ref, gain_ref, wq_ref, *rest):
    x_refs, (out_ref, strip_ref) = rest[:-2], rest[-2:]
    rows = out_ref.shape[0]
    groups, _, part = gain_ref.shape
    pieces_t = rows // PIECE_T
    tiles = pieces_t * (part // PIECE_F)
    whole = list(x_refs[:-2])

    def tile_rows(k, f):
        first = f * pieces_t
        if k < groups - 1:
            return x_refs[k][first : first + pieces_t].reshape(rows, PIECE_F)
        ref, start = (x_refs[-2], 0) if first < halved else (x_refs[-1], halved)
        return ref[first - start : first - start + pieces_t].reshape(rows, PIECE_F)

    squares = jnp.zeros((rows, PIECE_F), jnp.float32)
    for k in range(groups):
        for f in range(part // PIECE_F):
            wide = tile_rows(k, f).astype(jnp.float32)
            squares = squares + wide * wide
    mean = jnp.sum(squares, axis=1, keepdims=True) * (1.0 / (groups * part))
    inverse = lax.rsqrt(mean + 1e-06)
    total = jnp.zeros(out_ref.shape, jnp.float32)
    me = where_ref[0]
    for k in range(groups):
        group = where_ref[RING_ORDER[k]]
        x = jnp.concatenate([tile_rows(k, f) for f in range(part // PIECE_F)], axis=1)
        gain = gain_ref[group].astype(jnp.float32)
        normed = (x.astype(jnp.float32) * inverse * gain).astype(jnp.bfloat16)
        total = total + jnp.dot(normed, wq_ref[group], preferred_element_type=jnp.float32)
        for f in range(PIECES_WO):
            at = tiles + me * PIECES_WO + f
            ref = whole[k] if k < groups - 1 else x_refs[-1]
            at = at if k < groups - 1 else at - halved
            tile = ref[at]
            for dest in range(strip_ref.shape[0]):
                strip_ref[dest, group * PIECES_WO + f] = tile
    total = pltpu.roll(total * HS ** (-0.5), rows - shift, 0)
    out_ref[...] = total.astype(jnp.bfloat16)


def query(where, letters, gain, wq, rows, shift, copies):
    groups = where.shape[0]
    part = wq.shape[0] // groups
    cols = wq.shape[1]
    vmem = pl.BlockSpec(memory_space=pltpu.VMEM)
    return pl.pallas_call(
        functools.partial(query_kernel, shift, letters[-2].shape[0]),
        in_specs=[pl.BlockSpec(memory_space=pltpu.SMEM)] + [vmem] * (2 + len(letters)),
        out_specs=[vmem] * 2,
        out_shape=[
            jax.ShapeDtypeStruct((rows, cols), jnp.bfloat16),
            jax.ShapeDtypeStruct((copies, groups * PIECES_WO, PIECE_T, PIECE_F), jnp.bfloat16),
        ],
        compiler_params=pltpu.CompilerParams(vmem_limit_bytes=VMEM_LIMIT),
        cost_estimate=pl.CostEstimate(
            flops=8 * rows * groups * part * cols,
            bytes_accessed=4 * groups * part * (rows + cols),
            transcendentals=0,
        ),
        name="query",
    )(where, gain.reshape(groups, 1, part), wq.reshape(groups, part, cols), *letters)


def gather_kernel(places, first, last, where_ref, w_ref, *rest):
    count = len(places)
    x_refs, rest = rest[:count], rest[count:]
    if not first:
        acc, squares = rest[0][...], rest[1][...]
        rest = rest[2:]
    for at, (x_ref, (place, start)) in enumerate(zip(x_refs, places)):
        x, more = unpack(x_ref)
        lane = start * PIECE_F
        w = w_ref[where_ref[place], lane : lane + x.shape[1], :]
        term = jnp.dot(x, w, preferred_element_type=jnp.float32)
        if first and at == 0:
            acc, squares = term, more
        else:
            acc, squares = acc + term, squares + more
    if last:
        store_spans(acc, squares, w_ref.shape[0] * w_ref.shape[1], rest)
    else:
        rest[0][...] = acc
        rest[1][...] = squares


def gather_step(blocks, places, where, weights, state, last):
    _, part, cols = weights.shape
    _, pieces_t, items = blocks[0].shape[:3]
    rows = pieces_t * items * PIECE_T
    vmem = pl.BlockSpec(memory_space=pltpu.VMEM)
    if last:
        span = jax.ShapeDtypeStruct((pieces_t, NB, PIECE_T, cols), jnp.bfloat16)
        out_shape = [span] * (items // NB)
    else:
        out_shape = [
            jax.ShapeDtypeStruct((rows, cols), jnp.float32),
            jax.ShapeDtypeStruct((rows, PIECE_F), jnp.float32),
        ]
    return pl.pallas_call(
        functools.partial(gather_kernel, tuple(places), not state, last),
        in_specs=[pl.BlockSpec(memory_space=pltpu.SMEM)]
        + [vmem] * (1 + len(blocks) + len(state)),
        out_specs=[vmem] * len(out_shape),
        out_shape=out_shape,
        compiler_params=pltpu.CompilerParams(vmem_limit_bytes=VMEM_LIMIT),
        cost_estimate=pl.CostEstimate(
            flops=8 * rows * cols * sum(block.shape[0] for block in blocks) * PIECE_F,
            bytes_accessed=2 * sum(block.size for block in blocks) + 8 * rows * cols,
            transcendentals=0,
        ),
        name="gather_last" if last else "gather_step",
    )(where, weights, *blocks, *state)


def ring_ways(n_ten):
    right = [(i, (i + 1) % n_ten) for i in range(n_ten)]
    left = [(i, (i - 1) % n_ten) for i in range(n_ten)]
    return right, left


def ring_gather(block, n_ten, cut_at):
    right, left = ring_ways(n_ten)
    go_right = go_left = block
    blocks = [block]
    for _ in range(1, n_ten // 2):
        go_right = lax.ppermute(go_right, "tensor", right)
        go_left = lax.ppermute(go_left, "tensor", left)
        blocks += [go_right, go_left]
    return blocks + [
        lax.ppermute(go_right[:cut_at], "tensor", right),
        lax.ppermute(go_left[cut_at:], "tensor", left),
    ]


def ring_project(streams, where, weights, n_ten, send_beside):
    right, left = ring_ways(n_ten)
    half = streams[0].shape[0] // 2
    go_right, go_left = list(streams), list(streams)
    states = [gather_step([x], [(0, 0)], where, weights, (), False) for x in streams]
    for step in range(1, n_ten // 2):
        for s in range(len(streams)):
            go_right[s] = lax.ppermute(go_right[s], "tensor", right)
            go_left[s] = lax.ppermute(go_left[s], "tensor", left)
            states[s] = gather_step(
                [go_right[s], go_left[s]],
                [(n_ten - step, 0), (step, 0)],
                where,
                weights,
                states[s],
                False,
            )
        if step == 1:
            beside = send_beside(go_right[0])
    places = [(n_ten // 2, 0), (n_ten // 2, half)]
    for s in range(len(streams)):
        from_left, from_right, beside = lax.optimization_barrier((go_right[s], go_left[s], beside))
        blocks = [
            lax.ppermute(from_left[:half], "tensor", right),
            lax.ppermute(from_right[half:], "tensor", left),
        ]
        states[s] = gather_step(blocks, places, where, weights, states[s], True)
    return states, beside


def weigh(scores, count, keys_axis_owner):
    scores = jnp.where(keys_axis_owner < count, scores, jnp.float32(-1e30))
    top = jnp.max(scores, axis=-1, keepdims=True)
    expo = jnp.exp(scores - top)
    return expo / jnp.sum(expo, axis=-1, keepdims=True)


def scores_of(queries, keys):
    return lax.dot_general(
        queries, keys, (((1,), (1,)), ((), ())), preferred_element_type=jnp.float32
    )


def attend_kernel(first, with_prev, span_len, count_ref, q_ref, *rest):
    out_ref = rest[-1]
    pair_refs, other_ref = rest[:-2], rest[-2]
    if not with_prev:
        done = other_ref.shape[0]
        out_ref[out_ref.shape[0] - done :, :] = other_ref[...]
    cols = out_ref.shape[1]
    heads = cols // HS
    spans = len(pair_refs)
    keys = pair_refs[0].shape[0] * pair_refs[0].shape[1] * pair_refs[0].shape[2]
    owner = (lax.broadcasted_iota(jnp.int32, (span_len, keys), 1) // PIECE_T) % NB
    row = lax.broadcasted_iota(jnp.int32, (span_len, keys), 0)
    for span in range(spans):
        pair = pair_refs[span][...].reshape(keys, 2 * cols)
        queries = q_ref[(first + span) * span_len : (first + span + 1) * span_len, :]
        mixed_heads = []
        for head in range(heads):
            at = slice(head * HS, (head + 1) * HS)
            value_at = slice(cols + head * HS, cols + (head + 1) * HS)
            query = queries[:, at]
            scores = scores_of(query, pair[:, at])
            if with_prev and span == spans - 1:
                prev = other_ref[...].reshape(keys, 2 * cols)
                own = row == 0
                scores = jnp.where(own, scores, scores_of(query, prev[:, at]))
                count = jnp.where(own, count_ref[first + span], count_ref[first + span + 1])
                weights = weigh(scores, count, owner)
                ours = jnp.where(own, weights, 0.0).astype(jnp.bfloat16)
                theirs = jnp.where(own, 0.0, weights).astype(jnp.bfloat16)
                result = jnp.dot(
                    ours, pair[:, value_at], preferred_element_type=jnp.float32
                ) + jnp.dot(theirs, prev[:, value_at], preferred_element_type=jnp.float32)
            else:
                weights = weigh(scores, count_ref[first + span], owner).astype(jnp.bfloat16)
                result = jnp.dot(
                    weights, pair[:, value_at], preferred_element_type=jnp.float32
                )
            mixed_heads.append(result.astype(jnp.bfloat16))
        out_ref[span * span_len : (span + 1) * span_len, :] = jnp.concatenate(mixed_heads, axis=1)


def attend(counts, queries, pairs, first, span_len, prev=None, after=None):
    cols = queries.shape[1]
    with_prev = prev is not None
    rows = len(pairs) * span_len + (0 if with_prev else after.shape[0])
    operands = [counts, queries, *pairs, prev if with_prev else after]
    vmem = pl.BlockSpec(memory_space=pltpu.VMEM)
    return pl.pallas_call(
        functools.partial(attend_kernel, first, with_prev, span_len),
        in_specs=[pl.BlockSpec(memory_space=pltpu.SMEM)] + [vmem] * (len(operands) - 1),
        out_specs=vmem,
        out_shape=jax.ShapeDtypeStruct((rows, cols), jnp.bfloat16),
        compiler_params=pltpu.CompilerParams(vmem_limit_bytes=VMEM_LIMIT),
        cost_estimate=pl.CostEstimate(
            flops=32 * len(pairs) * span_len * 256 * cols,
            bytes_accessed=4 * rows * cols,
            transcendentals=0,
        ),
        name="attend_prev" if with_prev else "attend",
    )(*operands)


def finish_kernel(shift, where_ref, mail_ref, tokens_ref, *rest):
    attended_refs, out_ref = rest[:-1], rest[-1]
    groups = where_ref.shape[0]
    depth = attended_refs[0].shape[1]
    total = None
    for k in range(groups):
        group = where_ref[RING_ORDER[k]]
        if k < groups - 1:
            attended = attended_refs[k][...]
        else:
            attended = jnp.concatenate([ref[...] for ref in attended_refs[k:]], axis=0)
        tiles = [
            mail_ref[:, h, group * PIECES_WO + f].reshape(depth, PIECE_F)
            for h in range(mail_ref.shape[1])
            for f in range(PIECES_WO)
        ]
        wo = jnp.concatenate(tiles, axis=1)
        part = jnp.dot(attended, wo, preferred_element_type=jnp.float32)
        part = part.astype(jnp.bfloat16).astype(jnp.float32)
        total = part if total is None else total + part
    total = pltpu.roll(total, shift, 0)
    out_ref[...] = (tokens_ref[...].astype(jnp.float32) + total).astype(jnp.bfloat16)


def finish(where, mail, tokens, attended, shift):
    vmem = pl.BlockSpec(memory_space=pltpu.VMEM)
    return pl.pallas_call(
        functools.partial(finish_kernel, shift),
        in_specs=[pl.BlockSpec(memory_space=pltpu.SMEM)] + [vmem] * (2 + len(attended)),
        out_specs=vmem,
        out_shape=jax.ShapeDtypeStruct(tokens.shape, jnp.bfloat16),
        compiler_params=pltpu.CompilerParams(vmem_limit_bytes=VMEM_LIMIT),
        name="finish",
    )(where, mail, tokens, *attended)


def body(tokens, x_gain, nbr_gain, database, nbr_shard, nbr_row, nbr_count, wq, wk, wv, wo):
    n_seq = lax.axis_size("seq")
    n_ten = lax.axis_size("tensor")
    tok_dev = tokens.shape[0]
    span_dev = nbr_shard.shape[0]
    span_len = tok_dev // span_dev
    shift = span_len - 1
    per_shard, nbr_len, d_part = database.shape
    items = span_dev * NB
    pieces_t = nbr_len // PIECE_T
    pieces_f = d_part // PIECE_F
    seq_at = lax.axis_index("seq")
    me = lax.axis_index("tensor")
    where = ((me + jnp.arange(n_ten, dtype=jnp.int32)) % n_ten).astype(jnp.int32)

    pieces = cut(nbr_shard, nbr_row, nbr_count, database)
    spread = lax.all_to_all(pieces, "seq", split_axis=0, concat_axis=0, tiled=True)
    n_notes = 2 * items + span_dev
    notes = spread[:, per_shard, 0, :n_notes].astype(jnp.int32)
    index = notes[:, :items] * (per_shard + 1) + notes[:, items : 2 * items]
    prev_count = jnp.where(seq_at > 0, notes[jnp.maximum(seq_at - 1, 0), n_notes - 1], 0)
    counts = jnp.concatenate([nbr_count, prev_count[None]])

    halves = d_part // (PIECES_WO * PIECE_F)
    strips = n_seq // halves
    own = jnp.stack([seq_at // halves, seq_at % halves]).astype(jnp.int32)
    own, _ = lax.optimization_barrier((own, pieces))
    mine = letter(own, tokens, wo, wo.shape[0] // strips)
    letters = ring_gather(mine, n_ten, tok_dev // PIECE_T * (pieces_f // 2))

    spread, index, _ = lax.optimization_barrier((spread, index, letters[3:5]))
    spread = spread.reshape(n_seq * (per_shard + 1), PIECE_T, PIECE_F)
    low, high = pick(index, spread, 2)
    nbr_gain, _ = lax.optimization_barrier((nbr_gain, high))
    both = jnp.concatenate([wk, wv], axis=1).astype(jnp.float32)
    both = (both * nbr_gain.astype(jnp.float32)[:, None]).astype(jnp.bfloat16)
    both = both.reshape(n_ten, d_part, both.shape[1])
    high = lax.all_to_all(high, "seq", split_axis=0, concat_axis=0, tiled=True)
    high, low, letters, both, counts = lax.optimization_barrier(
        (high, low, letters, both, counts)
    )
    low = lax.all_to_all(low, "seq", split_axis=0, concat_axis=0, tiled=True)
    queries, strip = query(where, letters, x_gain, wq, tok_dev, shift, n_seq)

    def send_mail(arrived):
        mail, _ = lax.optimization_barrier((strip, arrived))
        mail = lax.all_to_all(mail, "seq", split_axis=0, concat_axis=0, tiled=True)
        return mail.reshape(strips, halves, *strip.shape[1:])

    shape = (pieces_f, pieces_t, items // 2, PIECE_T, PIECE_F)
    streams = [high.reshape(shape), low.reshape(shape)]
    (late, early), mail = ring_project(streams, where, both, n_ten, send_mail)
    prev = lax.ppermute(late[-1], "seq", [(i, i + 1) for i in range(n_seq - 1)])
    attended = attend(counts, queries, late, span_dev // 2, span_len, prev=prev)
    attended = attend(counts, queries, early, 0, span_len, after=attended)
    gathered = ring_gather(attended, n_ten, tok_dev // 2)
    return finish(where, mail, tokens, gathered, shift)


def solution(mesh):
    placed = (
        P("seq", "tensor"),
        P(),
        P(),
        P("seq", None, "tensor"),
        P("seq", None),
        P("seq", None),
        P("seq"),
        P(None, "tensor"),
        P(None, "tensor"),
        P(None, "tensor"),
        P("tensor", None),
    )
    return jax.shard_map(
        body, mesh=mesh, in_specs=placed, out_specs=P("seq", "tensor"), check_vma=False
    )
```

```python
import functools

import jax
import jax.numpy as jnp
from jax import lax
from jax.experimental import pallas as pl
from jax.experimental.pallas import tpu as pltpu
from jax.sharding import PartitionSpec as P

HS = 128
NB = 2
PIECE_T = 16
PIECE_F = 128
PIECES_WO = 2
RING_ORDER = (0, 7, 1, 6, 2, 5, 3, 4)
VMEM_LIMIT = 48 * 1024 * 1024


def cut_kernel(shard_ref, row_ref, count_ref, db_ref, out_ref):
    shard = db_ref.shape[0]
    pieces_t = db_ref.shape[1] // PIECE_T
    pieces_f = db_ref.shape[2] // PIECE_F
    each, spans = shard_ref.shape
    lane = lax.broadcasted_iota(jnp.int32, (PIECE_T, PIECE_F), 1)
    note = jnp.zeros((PIECE_T, PIECE_F), jnp.int32)
    for span in range(spans):
        for j in range(each):
            at = span * each + j
            note = jnp.where(lane == at, shard_ref[j, span], note)
            note = jnp.where(lane == spans * each + at, row_ref[j, span], note)
        note = jnp.where(lane == 2 * spans * each + span, count_ref[span], note)
    note = note.astype(jnp.float32).astype(jnp.bfloat16)
    for f in range(pieces_f):
        for i in range(pieces_t):
            piece = f * pieces_t + i
            out_ref[piece, :shard] = db_ref[
                :, i * PIECE_T : (i + 1) * PIECE_T, f * PIECE_F : (f + 1) * PIECE_F
            ]
            out_ref[piece, shard] = note


def cut(nbr_shard, nbr_row, nbr_count, database):
    shard, length, part = database.shape
    pieces = (length // PIECE_T) * (part // PIECE_F)
    vmem = pl.BlockSpec(memory_space=pltpu.VMEM)
    return pl.pallas_call(
        cut_kernel,
        in_specs=[pl.BlockSpec(memory_space=pltpu.SMEM)] * 3 + [vmem],
        out_specs=vmem,
        out_shape=jax.ShapeDtypeStruct((pieces, shard + 1, PIECE_T, PIECE_F), database.dtype),
        compiler_params=pltpu.CompilerParams(vmem_limit_bytes=VMEM_LIMIT),
        name="cut",
    )(nbr_shard.T, nbr_row.T, nbr_count, database)


def pick_kernel(index_ref, spread_ref, *out_refs):
    n_seq, items = out_refs[0].shape[:2]

    def one(dest, carry):
        for at, out_ref in enumerate(out_refs):
            for j in range(items):
                out_ref[dest, j] = spread_ref[index_ref[dest, at * items + j]]
        return carry

    lax.fori_loop(0, n_seq, one, 0, unroll=2)


def pick(index, spread, parts):
    vmem = pl.BlockSpec(memory_space=pltpu.VMEM)
    shape = (index.shape[0], index.shape[1] // parts, PIECE_T, PIECE_F)
    return pl.pallas_call(
        pick_kernel,
        in_specs=[pl.BlockSpec(memory_space=pltpu.SMEM), vmem],
        out_specs=[vmem] * parts,
        out_shape=[jax.ShapeDtypeStruct(shape, spread.dtype)] * parts,
        compiler_params=pltpu.CompilerParams(vmem_limit_bytes=VMEM_LIMIT),
        name="pick",
    )(index, spread)


def letter_kernel(at_ref, tokens_ref, wo_ref, out_ref):
    rows, part = tokens_ref.shape
    pieces_t = rows // PIECE_T
    pieces_f = part // PIECE_F
    for f in range(pieces_f):
        for i in range(pieces_t):
            out_ref[f * pieces_t + i] = tokens_ref[
                i * PIECE_T : (i + 1) * PIECE_T, f * PIECE_F : (f + 1) * PIECE_F
            ]
    strip = PIECES_WO * PIECE_F
    for group in range(wo_ref.shape[1] // part):
        for f in range(PIECES_WO):
            start = pl.multiple_of(group * part + at_ref[1] * strip + f * PIECE_F, PIECE_F)
            out_ref[pieces_f * pieces_t + group * PIECES_WO + f] = wo_ref[:, pl.ds(start, PIECE_F)]


def letter(at, tokens, wo, depth):
    rows, part = tokens.shape
    tiles = rows * part // (PIECE_T * PIECE_F) + wo.shape[1] // part * PIECES_WO
    return pl.pallas_call(
        letter_kernel,
        grid_spec=pltpu.PrefetchScalarGridSpec(
            num_scalar_prefetch=1,
            grid=(1,),
            in_specs=[
                pl.BlockSpec((rows, part), lambda g, at: (0, 0)),
                pl.BlockSpec((depth, wo.shape[1]), lambda g, at: (at[0], 0)),
            ],
            out_specs=pl.BlockSpec((tiles, PIECE_T, PIECE_F), lambda g, at: (0, 0, 0)),
        ),
        out_shape=jax.ShapeDtypeStruct((tiles, PIECE_T, PIECE_F), tokens.dtype),
        name="letter",
    )(at, tokens, wo)


def unpack(x_ref):
    features, pieces_t, items = x_ref.shape[:3]
    rows = pieces_t * items * PIECE_T
    pieces = [x_ref[f].reshape(rows, PIECE_F) for f in range(features)]
    squares = jnp.zeros((rows, PIECE_F), jnp.float32)
    for piece in pieces:
        wide = piece.astype(jnp.float32)
        squares = squares + wide * wide
    return jnp.concatenate(pieces, axis=1), squares


def store_spans(acc, squares, features, out_refs):
    mean = jnp.sum(squares, axis=1, keepdims=True) * (1.0 / features)
    done = (acc * lax.rsqrt(mean + 1e-06)).astype(jnp.bfloat16)
    pieces_t = out_refs[0].shape[0]
    done = done.reshape(pieces_t, NB * len(out_refs), PIECE_T, done.shape[-1])
    for span, ref in enumerate(out_refs):
        ref[...] = done[:, span * NB : (span + 1) * NB]


def query_kernel(shift, halved, where_ref, gain_ref, wq_ref, *rest):
    x_refs, (out_ref, strip_ref) = rest[:-2], rest[-2:]
    rows = out_ref.shape[0]
    groups, _, part = gain_ref.shape
    pieces_t = rows // PIECE_T
    tiles = pieces_t * (part // PIECE_F)
    whole = list(x_refs[:-2])

    def tile_rows(k, f):
        first = f * pieces_t
        if k < groups - 1:
            return x_refs[k][first : first + pieces_t].reshape(rows, PIECE_F)
        ref, start = (x_refs[-2], 0) if first < halved else (x_refs[-1], halved)
        return ref[first - start : first - start + pieces_t].reshape(rows, PIECE_F)

    squares = jnp.zeros((rows, PIECE_F), jnp.float32)
    for k in range(groups):
        for f in range(part // PIECE_F):
            wide = tile_rows(k, f).astype(jnp.float32)
            squares = squares + wide * wide
    mean = jnp.sum(squares, axis=1, keepdims=True) * (1.0 / (groups * part))
    inverse = lax.rsqrt(mean + 1e-06)
    total = jnp.zeros(out_ref.shape, jnp.float32)
    me = where_ref[0]
    for k in range(groups):
        group = where_ref[RING_ORDER[k]]
        x = jnp.concatenate([tile_rows(k, f) for f in range(part // PIECE_F)], axis=1)
        gain = gain_ref[group].astype(jnp.float32)
        normed = (x.astype(jnp.float32) * inverse * gain).astype(jnp.bfloat16)
        total = total + jnp.dot(normed, wq_ref[group], preferred_element_type=jnp.float32)
        for f in range(PIECES_WO):
            at = tiles + me * PIECES_WO + f
            ref = whole[k] if k < groups - 1 else x_refs[-1]
            at = at if k < groups - 1 else at - halved
            tile = ref[at]
            for dest in range(strip_ref.shape[0]):
                strip_ref[dest, group * PIECES_WO + f] = tile
    total = pltpu.roll(total * HS ** (-0.5), rows - shift, 0)
    out_ref[...] = total.astype(jnp.bfloat16)


def query(where, letters, gain, wq, rows, shift, copies):
    groups = where.shape[0]
    part = wq.shape[0] // groups
    cols = wq.shape[1]
    vmem = pl.BlockSpec(memory_space=pltpu.VMEM)
    return pl.pallas_call(
        functools.partial(query_kernel, shift, letters[-2].shape[0]),
        in_specs=[pl.BlockSpec(memory_space=pltpu.SMEM)] + [vmem] * (2 + len(letters)),
        out_specs=[vmem] * 2,
        out_shape=[
            jax.ShapeDtypeStruct((rows, cols), jnp.bfloat16),
            jax.ShapeDtypeStruct((copies, groups * PIECES_WO, PIECE_T, PIECE_F), jnp.bfloat16),
        ],
        compiler_params=pltpu.CompilerParams(vmem_limit_bytes=VMEM_LIMIT),
        cost_estimate=pl.CostEstimate(
            flops=8 * rows * groups * part * cols,
            bytes_accessed=4 * groups * part * (rows + cols),
            transcendentals=0,
        ),
        name="query",
    )(where, gain.reshape(groups, 1, part), wq.reshape(groups, part, cols), *letters)


def gather_kernel(places, first, last, where_ref, w_ref, *rest):
    count = len(places)
    x_refs, rest = rest[:count], rest[count:]
    if not first:
        acc, squares = rest[0][...], rest[1][...]
        rest = rest[2:]
    for at, (x_ref, (place, start)) in enumerate(zip(x_refs, places)):
        x, more = unpack(x_ref)
        lane = start * PIECE_F
        w = w_ref[where_ref[place], lane : lane + x.shape[1], :]
        term = jnp.dot(x, w, preferred_element_type=jnp.float32)
        if first and at == 0:
            acc, squares = term, more
        else:
            acc, squares = acc + term, squares + more
    if last:
        store_spans(acc, squares, w_ref.shape[0] * w_ref.shape[1], rest)
    else:
        rest[0][...] = acc
        rest[1][...] = squares


def gather_step(blocks, places, where, weights, state, last):
    _, part, cols = weights.shape
    _, pieces_t, items = blocks[0].shape[:3]
    rows = pieces_t * items * PIECE_T
    vmem = pl.BlockSpec(memory_space=pltpu.VMEM)
    if last:
        span = jax.ShapeDtypeStruct((pieces_t, NB, PIECE_T, cols), jnp.bfloat16)
        out_shape = [span] * (items // NB)
    else:
        out_shape = [
            jax.ShapeDtypeStruct((rows, cols), jnp.float32),
            jax.ShapeDtypeStruct((rows, PIECE_F), jnp.float32),
        ]
    return pl.pallas_call(
        functools.partial(gather_kernel, tuple(places), not state, last),
        in_specs=[pl.BlockSpec(memory_space=pltpu.SMEM)]
        + [vmem] * (1 + len(blocks) + len(state)),
        out_specs=[vmem] * len(out_shape),
        out_shape=out_shape,
        compiler_params=pltpu.CompilerParams(vmem_limit_bytes=VMEM_LIMIT),
        cost_estimate=pl.CostEstimate(
            flops=8 * rows * cols * sum(block.shape[0] for block in blocks) * PIECE_F,
            bytes_accessed=2 * sum(block.size for block in blocks) + 8 * rows * cols,
            transcendentals=0,
        ),
        name="gather_last" if last else "gather_step",
    )(where, weights, *blocks, *state)


def ring_ways(n_ten):
    right = [(i, (i + 1) % n_ten) for i in range(n_ten)]
    left = [(i, (i - 1) % n_ten) for i in range(n_ten)]
    return right, left


def ring_gather(block, n_ten, cut_at):
    right, left = ring_ways(n_ten)
    go_right = go_left = block
    blocks = [block]
    for _ in range(1, n_ten // 2):
        go_right = lax.ppermute(go_right, "tensor", right)
        go_left = lax.ppermute(go_left, "tensor", left)
        blocks += [go_right, go_left]
    return blocks + [
        lax.ppermute(go_right[:cut_at], "tensor", right),
        lax.ppermute(go_left[cut_at:], "tensor", left),
    ]


def ring_project(stream, where, weights, n_ten, hold=None):
    right, left = ring_ways(n_ten)
    half = stream.shape[0] // 2
    go_right = go_left = stream
    arrivals = []
    state = gather_step([stream], [(0, 0)], where, weights, (), False)
    for step in range(1, n_ten // 2):
        go_right = lax.ppermute(go_right, "tensor", right)
        go_left = lax.ppermute(go_left, "tensor", left)
        arrivals.append((go_right, go_left))
        places = [(n_ten - step, 0), (step, 0)]
        state = gather_step([go_right, go_left], places, where, weights, state, False)
    go_right, go_left, hold = lax.optimization_barrier((go_right, go_left, hold))
    blocks = [
        lax.ppermute(go_right[:half], "tensor", right),
        lax.ppermute(go_left[half:], "tensor", left),
    ]
    places = [(n_ten // 2, 0), (n_ten // 2, half)]
    return gather_step(blocks, places, where, weights, state, True), arrivals, hold


def weigh(scores, count, keys_axis_owner):
    scores = jnp.where(keys_axis_owner < count, scores, jnp.float32(-1e30))
    top = jnp.max(scores, axis=-1, keepdims=True)
    expo = jnp.exp(scores - top)
    return expo / jnp.sum(expo, axis=-1, keepdims=True)


def scores_of(queries, keys):
    return lax.dot_general(
        queries, keys, (((1,), (1,)), ((), ())), preferred_element_type=jnp.float32
    )


def attend_kernel(first, with_prev, span_len, count_ref, q_ref, *rest):
    out_ref = rest[-1]
    pair_refs, other_ref = (rest[:-2], rest[-2]) if with_prev else (rest[:-1], None)
    cols = out_ref.shape[1]
    heads = cols // HS
    spans = len(pair_refs)
    keys = pair_refs[0].shape[0] * pair_refs[0].shape[1] * pair_refs[0].shape[2]
    owner = (lax.broadcasted_iota(jnp.int32, (span_len, keys), 1) // PIECE_T) % NB
    row = lax.broadcasted_iota(jnp.int32, (span_len, keys), 0)
    for span in range(spans):
        pair = pair_refs[span][...].reshape(keys, 2 * cols)
        queries = q_ref[(first + span) * span_len : (first + span + 1) * span_len, :]
        mixed_heads = []
        for head in range(heads):
            at = slice(head * HS, (head + 1) * HS)
            value_at = slice(cols + head * HS, cols + (head + 1) * HS)
            query = queries[:, at]
            scores = scores_of(query, pair[:, at])
            if with_prev and span == spans - 1:
                prev = other_ref[...].reshape(keys, 2 * cols)
                own = row == 0
                scores = jnp.where(own, scores, scores_of(query, prev[:, at]))
                count = jnp.where(own, count_ref[first + span], count_ref[first + span + 1])
                weights = weigh(scores, count, owner)
                ours = jnp.where(own, weights, 0.0).astype(jnp.bfloat16)
                theirs = jnp.where(own, 0.0, weights).astype(jnp.bfloat16)
                result = jnp.dot(
                    ours, pair[:, value_at], preferred_element_type=jnp.float32
                ) + jnp.dot(theirs, prev[:, value_at], preferred_element_type=jnp.float32)
            else:
                weights = weigh(scores, count_ref[first + span], owner).astype(jnp.bfloat16)
                result = jnp.dot(
                    weights, pair[:, value_at], preferred_element_type=jnp.float32
                )
            mixed_heads.append(result.astype(jnp.bfloat16))
        out_ref[span * span_len : (span + 1) * span_len, :] = jnp.concatenate(mixed_heads, axis=1)


def attend(counts, queries, pairs, first, span_len, prev=None):
    cols = queries.shape[1]
    with_prev = prev is not None
    rows = len(pairs) * span_len
    operands = [counts, queries, *pairs] + ([prev] if with_prev else [])
    vmem = pl.BlockSpec(memory_space=pltpu.VMEM)
    return pl.pallas_call(
        functools.partial(attend_kernel, first, with_prev, span_len),
        in_specs=[pl.BlockSpec(memory_space=pltpu.SMEM)] + [vmem] * (len(operands) - 1),
        out_specs=vmem,
        out_shape=jax.ShapeDtypeStruct((rows, cols), jnp.bfloat16),
        compiler_params=pltpu.CompilerParams(vmem_limit_bytes=VMEM_LIMIT),
        cost_estimate=pl.CostEstimate(
            flops=32 * len(pairs) * span_len * 256 * cols,
            bytes_accessed=4 * rows * cols,
            transcendentals=0,
        ),
        name="attend_prev" if with_prev else "attend",
    )(*operands)


def finish_kernel(shift, parts, where_ref, mail_ref, tokens_ref, *rest):
    attended_refs, out_ref = rest[:-1], rest[-1]
    groups = where_ref.shape[0]
    depth = attended_refs[0].shape[1]
    each = len(attended_refs) // parts
    total = None
    for k in range(groups):
        group = where_ref[RING_ORDER[k]]
        refs = []
        for p in range(parts):
            own = attended_refs[p * each : (p + 1) * each]
            refs += own[k : k + 1] if k < groups - 1 else own[k:]
        attended = jnp.concatenate([ref[...] for ref in refs], axis=0)
        tiles = [
            mail_ref[:, h, group * PIECES_WO + f].reshape(depth, PIECE_F)
            for h in range(mail_ref.shape[1])
            for f in range(PIECES_WO)
        ]
        wo = jnp.concatenate(tiles, axis=1)
        part = jnp.dot(attended, wo, preferred_element_type=jnp.float32)
        part = part.astype(jnp.bfloat16).astype(jnp.float32)
        total = part if total is None else total + part
    total = pltpu.roll(total, shift, 0)
    out_ref[...] = (tokens_ref[...].astype(jnp.float32) + total).astype(jnp.bfloat16)


def finish(where, mail, tokens, attended, shift):
    blocks = [block for part in attended for block in part]
    vmem = pl.BlockSpec(memory_space=pltpu.VMEM)
    return pl.pallas_call(
        functools.partial(finish_kernel, shift, len(attended)),
        in_specs=[pl.BlockSpec(memory_space=pltpu.SMEM)] + [vmem] * (2 + len(blocks)),
        out_specs=vmem,
        out_shape=jax.ShapeDtypeStruct(tokens.shape, jnp.bfloat16),
        compiler_params=pltpu.CompilerParams(vmem_limit_bytes=VMEM_LIMIT),
        name="finish",
    )(where, mail, tokens, *blocks)


def body(tokens, x_gain, nbr_gain, database, nbr_shard, nbr_row, nbr_count, wq, wk, wv, wo):
    n_seq = lax.axis_size("seq")
    n_ten = lax.axis_size("tensor")
    tok_dev = tokens.shape[0]
    span_dev = nbr_shard.shape[0]
    span_len = tok_dev // span_dev
    shift = span_len - 1
    per_shard, nbr_len, d_part = database.shape
    items = span_dev * NB
    pieces_t = nbr_len // PIECE_T
    pieces_f = d_part // PIECE_F
    seq_at = lax.axis_index("seq")
    me = lax.axis_index("tensor")
    where = ((me + jnp.arange(n_ten, dtype=jnp.int32)) % n_ten).astype(jnp.int32)

    pieces = cut(nbr_shard, nbr_row, nbr_count, database)
    spread = lax.all_to_all(pieces, "seq", split_axis=0, concat_axis=0, tiled=True)
    n_notes = 2 * items + span_dev
    notes = spread[:, per_shard, 0, :n_notes].astype(jnp.int32)
    index = notes[:, :items] * (per_shard + 1) + notes[:, items : 2 * items]
    prev_count = jnp.where(seq_at > 0, notes[jnp.maximum(seq_at - 1, 0), n_notes - 1], 0)
    counts = jnp.concatenate([nbr_count, prev_count[None]])

    halves = d_part // (PIECES_WO * PIECE_F)
    strips = n_seq // halves
    own = jnp.stack([seq_at // halves, seq_at % halves]).astype(jnp.int32)
    own, _ = lax.optimization_barrier((own, pieces))
    mine = letter(own, tokens, wo, wo.shape[0] // strips)
    letters = ring_gather(mine, n_ten, tok_dev // PIECE_T * (pieces_f // 2))

    spread, index, _ = lax.optimization_barrier((spread, index, letters[3:5]))
    spread = spread.reshape(n_seq * (per_shard + 1), PIECE_T, PIECE_F)
    low, high = pick(index, spread, 2)
    nbr_gain, _ = lax.optimization_barrier((nbr_gain, high))
    both = jnp.concatenate([wk, wv], axis=1).astype(jnp.float32)
    both = (both * nbr_gain.astype(jnp.float32)[:, None]).astype(jnp.bfloat16)
    both = both.reshape(n_ten, d_part, both.shape[1])
    high = lax.all_to_all(high, "seq", split_axis=0, concat_axis=0, tiled=True)
    high, letters, both, counts = lax.optimization_barrier((high, letters, both, counts))
    shape = (pieces_f, pieces_t, items // 2, PIECE_T, PIECE_F)
    late, arrivals, _ = ring_project(high.reshape(shape), where, both, n_ten)

    low, letters, _ = lax.optimization_barrier((low, letters, arrivals[0]))
    low = lax.all_to_all(low, "seq", split_axis=0, concat_axis=0, tiled=True)
    queries, strip = query(where, letters, x_gain, wq, tok_dev, shift, n_seq)
    strip, _ = lax.optimization_barrier((strip, arrivals[1]))
    mail = lax.all_to_all(strip, "seq", split_axis=0, concat_axis=0, tiled=True)
    mail = mail.reshape(strips, halves, *strip.shape[1:])

    prev = lax.ppermute(late[-1], "seq", [(i, i + 1) for i in range(n_seq - 1)])
    attended = attend(counts, queries, late, span_dev // 2, span_len, prev)
    gathered = [ring_gather(attended, n_ten, attended.shape[0] // 2)]
    hold = (mail, gathered[0][3:5])
    early, _, (mail, _) = ring_project(low.reshape(shape), where, both, n_ten, hold)
    queries, _ = lax.optimization_barrier((queries, gathered[0][7:9]))
    attended = attend(counts, queries, early, 0, span_len)
    gathered = [ring_gather(attended, n_ten, attended.shape[0] // 2)] + gathered
    return finish(where, mail, tokens, gathered, shift)


def solution(mesh):
    placed = (
        P("seq", "tensor"),
        P(),
        P(),
        P("seq", None, "tensor"),
        P("seq", None),
        P("seq", None),
        P("seq"),
        P(None, "tensor"),
        P(None, "tensor"),
        P(None, "tensor"),
        P("tensor", None),
    )
    return jax.shard_map(
        body, mesh=mesh, in_specs=placed, out_specs=P("seq", "tensor"), check_vma=False
    )
```

```python
import functools

import jax
import jax.numpy as jnp
from jax import lax
from jax.experimental import pallas as pl
from jax.experimental.pallas import tpu as pltpu
from jax.sharding import PartitionSpec as P

HS = 128
NB = 2
PIECE_T = 16
PIECE_F = 128
PIECES_WO = 2
RING_ORDER = (0, 7, 1, 6, 2, 5, 3, 4)
VMEM_LIMIT = 48 * 1024 * 1024


def cut_kernel(shard_ref, row_ref, count_ref, db_ref, out_ref):
    shard = db_ref.shape[0]
    pieces_t = db_ref.shape[1] // PIECE_T
    pieces_f = db_ref.shape[2] // PIECE_F
    each, spans = shard_ref.shape
    lane = lax.broadcasted_iota(jnp.int32, (PIECE_T, PIECE_F), 1)
    note = jnp.zeros((PIECE_T, PIECE_F), jnp.int32)
    for span in range(spans):
        for j in range(each):
            at = span * each + j
            note = jnp.where(lane == at, shard_ref[j : j + 1, span : span + 1], note)
            row = row_ref[j : j + 1, span : span + 1]
            note = jnp.where(lane == spans * each + at, row, note)
        count = count_ref[:, span : span + 1]
        note = jnp.where(lane == 2 * spans * each + span, count, note)
    note = note.astype(jnp.float32).astype(jnp.bfloat16)
    for f in range(pieces_f):
        for i in range(pieces_t):
            piece = f * pieces_t + i
            out_ref[piece, :shard] = db_ref[
                :, i * PIECE_T : (i + 1) * PIECE_T, f * PIECE_F : (f + 1) * PIECE_F
            ]
            out_ref[piece, shard] = note


def cut(nbr_shard, nbr_row, nbr_count, database):
    shard, length, part = database.shape
    pieces = (length // PIECE_T) * (part // PIECE_F)
    vmem = pl.BlockSpec(memory_space=pltpu.VMEM)
    return pl.pallas_call(
        cut_kernel,
        in_specs=[vmem] * 4,
        out_specs=vmem,
        out_shape=jax.ShapeDtypeStruct((pieces, shard + 1, PIECE_T, PIECE_F), database.dtype),
        compiler_params=pltpu.CompilerParams(vmem_limit_bytes=VMEM_LIMIT),
        name="cut",
    )(nbr_shard.T, nbr_row.T, nbr_count.reshape(1, -1), database)


def pick_kernel(index_ref, spread_ref, *out_refs):
    n_seq, items = out_refs[0].shape[:2]

    def one(dest, carry):
        for at, out_ref in enumerate(out_refs):
            for j in range(items):
                out_ref[dest, j] = spread_ref[index_ref[dest, at * items + j]]
        return carry

    lax.fori_loop(0, n_seq, one, 0, unroll=2)


def pick(index, spread, parts):
    vmem = pl.BlockSpec(memory_space=pltpu.VMEM)
    shape = (index.shape[0], index.shape[1] // parts, PIECE_T, PIECE_F)
    return pl.pallas_call(
        pick_kernel,
        in_specs=[pl.BlockSpec(memory_space=pltpu.SMEM), vmem],
        out_specs=[vmem] * parts,
        out_shape=[jax.ShapeDtypeStruct(shape, spread.dtype)] * parts,
        compiler_params=pltpu.CompilerParams(vmem_limit_bytes=VMEM_LIMIT),
        name="pick",
    )(index, spread)


def letter_kernel(at_ref, tokens_ref, wo_ref, out_ref):
    rows, part = tokens_ref.shape
    pieces_t = rows // PIECE_T
    pieces_f = part // PIECE_F
    for f in range(pieces_f):
        for i in range(pieces_t):
            out_ref[f * pieces_t + i] = tokens_ref[
                i * PIECE_T : (i + 1) * PIECE_T, f * PIECE_F : (f + 1) * PIECE_F
            ]
    strip = PIECES_WO * PIECE_F
    for group in range(wo_ref.shape[1] // part):
        for f in range(PIECES_WO):
            start = pl.multiple_of(group * part + at_ref[1] * strip + f * PIECE_F, PIECE_F)
            out_ref[pieces_f * pieces_t + group * PIECES_WO + f] = wo_ref[:, pl.ds(start, PIECE_F)]


def letter(at, tokens, wo, depth):
    rows, part = tokens.shape
    tiles = rows * part // (PIECE_T * PIECE_F) + wo.shape[1] // part * PIECES_WO
    return pl.pallas_call(
        letter_kernel,
        grid_spec=pltpu.PrefetchScalarGridSpec(
            num_scalar_prefetch=1,
            grid=(1,),
            in_specs=[
                pl.BlockSpec((rows, part), lambda g, at: (0, 0)),
                pl.BlockSpec((depth, wo.shape[1]), lambda g, at: (at[0], 0)),
            ],
            out_specs=pl.BlockSpec((tiles, PIECE_T, PIECE_F), lambda g, at: (0, 0, 0)),
        ),
        out_shape=jax.ShapeDtypeStruct((tiles, PIECE_T, PIECE_F), tokens.dtype),
        name="letter",
    )(at, tokens, wo)


def unpack(x_ref):
    features, pieces_t, items = x_ref.shape[:3]
    rows = pieces_t * items * PIECE_T
    pieces = [x_ref[f].reshape(rows, PIECE_F) for f in range(features)]
    squares = jnp.zeros((rows, PIECE_F), jnp.float32)
    for piece in pieces:
        wide = piece.astype(jnp.float32)
        squares = squares + wide * wide
    return jnp.concatenate(pieces, axis=1), squares


def store_spans(acc, squares, features, out_refs):
    mean = jnp.sum(squares, axis=1, keepdims=True) * (1.0 / features)
    done = (acc * lax.rsqrt(mean + 1e-06)).astype(jnp.bfloat16)
    pieces_t = out_refs[0].shape[0]
    done = done.reshape(pieces_t, NB * len(out_refs), PIECE_T, done.shape[-1])
    for span, ref in enumerate(out_refs):
        ref[...] = done[:, span * NB : (span + 1) * NB]


def query_kernel(shift, halved, where_ref, gain_ref, wq_ref, *rest):
    x_refs, (out_ref, strip_ref) = rest[:-2], rest[-2:]
    rows = out_ref.shape[0]
    groups, _, part = gain_ref.shape
    pieces_t = rows // PIECE_T
    tiles = pieces_t * (part // PIECE_F)
    whole = list(x_refs[:-2])

    def tile_rows(k, f):
        first = f * pieces_t
        if k < groups - 1:
            return x_refs[k][first : first + pieces_t].reshape(rows, PIECE_F)
        ref, start = (x_refs[-2], 0) if first < halved else (x_refs[-1], halved)
        return ref[first - start : first - start + pieces_t].reshape(rows, PIECE_F)

    squares = jnp.zeros((rows, PIECE_F), jnp.float32)
    for k in range(groups):
        for f in range(part // PIECE_F):
            wide = tile_rows(k, f).astype(jnp.float32)
            squares = squares + wide * wide
    mean = jnp.sum(squares, axis=1, keepdims=True) * (1.0 / (groups * part))
    inverse = lax.rsqrt(mean + 1e-06)
    total = jnp.zeros(out_ref.shape, jnp.float32)
    me = where_ref[0]
    for k in range(groups):
        group = where_ref[RING_ORDER[k]]
        x = jnp.concatenate([tile_rows(k, f) for f in range(part // PIECE_F)], axis=1)
        gain = gain_ref[group].astype(jnp.float32)
        normed = (x.astype(jnp.float32) * inverse * gain).astype(jnp.bfloat16)
        total = total + jnp.dot(normed, wq_ref[group], preferred_element_type=jnp.float32)
        for f in range(PIECES_WO):
            at = tiles + me * PIECES_WO + f
            ref = whole[k] if k < groups - 1 else x_refs[-1]
            at = at if k < groups - 1 else at - halved
            tile = ref[at]
            for dest in range(strip_ref.shape[0]):
                strip_ref[dest, group * PIECES_WO + f] = tile
    total = pltpu.roll(total * HS ** (-0.5), rows - shift, 0)
    out_ref[...] = total.astype(jnp.bfloat16)


def query(where, letters, gain, wq, rows, shift, copies):
    groups = where.shape[0]
    part = wq.shape[0] // groups
    cols = wq.shape[1]
    vmem = pl.BlockSpec(memory_space=pltpu.VMEM)
    return pl.pallas_call(
        functools.partial(query_kernel, shift, letters[-2].shape[0]),
        in_specs=[pl.BlockSpec(memory_space=pltpu.SMEM)] + [vmem] * (2 + len(letters)),
        out_specs=[vmem] * 2,
        out_shape=[
            jax.ShapeDtypeStruct((rows, cols), jnp.bfloat16),
            jax.ShapeDtypeStruct((copies, groups * PIECES_WO, PIECE_T, PIECE_F), jnp.bfloat16),
        ],
        compiler_params=pltpu.CompilerParams(vmem_limit_bytes=VMEM_LIMIT),
        cost_estimate=pl.CostEstimate(
            flops=8 * rows * groups * part * cols,
            bytes_accessed=4 * groups * part * (rows + cols),
            transcendentals=0,
        ),
        name="query",
    )(where, gain.reshape(groups, 1, part), wq.reshape(groups, part, cols), *letters)


def gather_kernel(places, first, last, where_ref, w_ref, *rest):
    count = len(places)
    x_refs, rest = rest[:count], rest[count:]
    if not first:
        acc, squares = rest[0][...], rest[1][...]
        rest = rest[2:]
    for at, (x_ref, (place, start)) in enumerate(zip(x_refs, places)):
        x, more = unpack(x_ref)
        lane = start * PIECE_F
        w = w_ref[where_ref[place], lane : lane + x.shape[1], :]
        term = jnp.dot(x, w, preferred_element_type=jnp.float32)
        if first and at == 0:
            acc, squares = term, more
        else:
            acc, squares = acc + term, squares + more
    if last:
        store_spans(acc, squares, w_ref.shape[0] * w_ref.shape[1], rest)
    else:
        rest[0][...] = acc
        rest[1][...] = squares


def gather_step(blocks, places, where, weights, state, last):
    _, part, cols = weights.shape
    _, pieces_t, items = blocks[0].shape[:3]
    rows = pieces_t * items * PIECE_T
    vmem = pl.BlockSpec(memory_space=pltpu.VMEM)
    if last:
        span = jax.ShapeDtypeStruct((pieces_t, NB, PIECE_T, cols), jnp.bfloat16)
        out_shape = [span] * (items // NB)
    else:
        out_shape = [
            jax.ShapeDtypeStruct((rows, cols), jnp.float32),
            jax.ShapeDtypeStruct((rows, PIECE_F), jnp.float32),
        ]
    return pl.pallas_call(
        functools.partial(gather_kernel, tuple(places), not state, last),
        in_specs=[pl.BlockSpec(memory_space=pltpu.SMEM)]
        + [vmem] * (1 + len(blocks) + len(state)),
        out_specs=[vmem] * len(out_shape),
        out_shape=out_shape,
        compiler_params=pltpu.CompilerParams(vmem_limit_bytes=VMEM_LIMIT),
        cost_estimate=pl.CostEstimate(
            flops=8 * rows * cols * sum(block.shape[0] for block in blocks) * PIECE_F,
            bytes_accessed=2 * sum(block.size for block in blocks) + 8 * rows * cols,
            transcendentals=0,
        ),
        name="gather_last" if last else "gather_step",
    )(where, weights, *blocks, *state)


def ring_ways(n_ten):
    right = [(i, (i + 1) % n_ten) for i in range(n_ten)]
    left = [(i, (i - 1) % n_ten) for i in range(n_ten)]
    return right, left


def ring_gather(block, n_ten, cut_at):
    right, left = ring_ways(n_ten)
    go_right = go_left = block
    blocks = [block]
    for _ in range(1, n_ten // 2):
        go_right = lax.ppermute(go_right, "tensor", right)
        go_left = lax.ppermute(go_left, "tensor", left)
        blocks += [go_right, go_left]
    return blocks + [
        lax.ppermute(go_right[:cut_at], "tensor", right),
        lax.ppermute(go_left[cut_at:], "tensor", left),
    ]


def ring_project(streams, where, weights, n_ten, send_beside):
    right, left = ring_ways(n_ten)
    half = streams[0].shape[0] // 2
    go_right, go_left = list(streams), list(streams)
    states = [gather_step([x], [(0, 0)], where, weights, (), False) for x in streams]
    for step in range(1, n_ten // 2):
        for s in range(len(streams)):
            go_right[s] = lax.ppermute(go_right[s], "tensor", right)
            go_left[s] = lax.ppermute(go_left[s], "tensor", left)
            states[s] = gather_step(
                [go_right[s], go_left[s]],
                [(n_ten - step, 0), (step, 0)],
                where,
                weights,
                states[s],
                False,
            )
        if step == 1:
            beside = send_beside(*zip(go_right, go_left))
    places = [(n_ten // 2, 0), (n_ten // 2, half)]
    for s in range(len(streams)):
        from_left, from_right = go_right[s], go_left[s]
        if s == len(streams) - 1:
            held = lax.optimization_barrier((from_left, from_right, beside))
            from_left, from_right, beside = held
        blocks = [
            lax.ppermute(from_left[:half], "tensor", right),
            lax.ppermute(from_right[half:], "tensor", left),
        ]
        states[s] = gather_step(blocks, places, where, weights, states[s], True)
    return states, beside


def weigh(scores, count, keys_axis_owner):
    scores = jnp.where(keys_axis_owner < count, scores, jnp.float32(-1e30))
    top = jnp.max(scores, axis=-1, keepdims=True)
    expo = jnp.exp(scores - top)
    return expo / jnp.sum(expo, axis=-1, keepdims=True)


def scores_of(queries, keys):
    return lax.dot_general(
        queries, keys, (((1,), (1,)), ((), ())), preferred_element_type=jnp.float32
    )


def attend_kernel(first, with_prev, span_len, count_ref, q_ref, *rest):
    out_ref = rest[-1]
    pair_refs, other_ref = rest[:-2], rest[-2]
    if not with_prev:
        done = other_ref.shape[0]
        out_ref[out_ref.shape[0] - done :, :] = other_ref[...]
    cols = out_ref.shape[1]
    heads = cols // HS
    spans = len(pair_refs)
    keys = pair_refs[0].shape[0] * pair_refs[0].shape[1] * pair_refs[0].shape[2]
    owner = (lax.broadcasted_iota(jnp.int32, (span_len, keys), 1) // PIECE_T) % NB
    row = lax.broadcasted_iota(jnp.int32, (span_len, keys), 0)
    for span in range(spans):
        pair = pair_refs[span][...].reshape(keys, 2 * cols)
        queries = q_ref[(first + span) * span_len : (first + span + 1) * span_len, :]
        mixed_heads = []
        for head in range(heads):
            at = slice(head * HS, (head + 1) * HS)
            value_at = slice(cols + head * HS, cols + (head + 1) * HS)
            query = queries[:, at]
            scores = scores_of(query, pair[:, at])
            if with_prev and span == spans - 1:
                prev = other_ref[...].reshape(keys, 2 * cols)
                own = row == 0
                scores = jnp.where(own, scores, scores_of(query, prev[:, at]))
                count = jnp.where(own, count_ref[first + span], count_ref[first + span + 1])
                weights = weigh(scores, count, owner)
                ours = jnp.where(own, weights, 0.0).astype(jnp.bfloat16)
                theirs = jnp.where(own, 0.0, weights).astype(jnp.bfloat16)
                result = jnp.dot(
                    ours, pair[:, value_at], preferred_element_type=jnp.float32
                ) + jnp.dot(theirs, prev[:, value_at], preferred_element_type=jnp.float32)
            else:
                weights = weigh(scores, count_ref[first + span], owner).astype(jnp.bfloat16)
                result = jnp.dot(
                    weights, pair[:, value_at], preferred_element_type=jnp.float32
                )
            mixed_heads.append(result.astype(jnp.bfloat16))
        out_ref[span * span_len : (span + 1) * span_len, :] = jnp.concatenate(mixed_heads, axis=1)


def attend(counts, queries, pairs, first, span_len, prev=None, after=None):
    cols = queries.shape[1]
    with_prev = prev is not None
    rows = len(pairs) * span_len + (0 if with_prev else after.shape[0])
    operands = [counts, queries, *pairs, prev if with_prev else after]
    vmem = pl.BlockSpec(memory_space=pltpu.VMEM)
    return pl.pallas_call(
        functools.partial(attend_kernel, first, with_prev, span_len),
        in_specs=[pl.BlockSpec(memory_space=pltpu.SMEM)] + [vmem] * (len(operands) - 1),
        out_specs=vmem,
        out_shape=jax.ShapeDtypeStruct((rows, cols), jnp.bfloat16),
        compiler_params=pltpu.CompilerParams(vmem_limit_bytes=VMEM_LIMIT),
        cost_estimate=pl.CostEstimate(
            flops=32 * len(pairs) * span_len * 256 * cols,
            bytes_accessed=4 * rows * cols,
            transcendentals=0,
        ),
        name="attend_prev" if with_prev else "attend",
    )(*operands)


def finish_kernel(shift, where_ref, mail_ref, tokens_ref, *rest):
    attended_refs, out_ref = rest[:-1], rest[-1]
    groups = where_ref.shape[0]
    depth = attended_refs[0].shape[1]
    total = None
    for k in range(groups):
        group = where_ref[RING_ORDER[k]]
        if k < groups - 1:
            attended = attended_refs[k][...]
        else:
            attended = jnp.concatenate([ref[...] for ref in attended_refs[k:]], axis=0)
        tiles = [
            mail_ref[:, h, group * PIECES_WO + f].reshape(depth, PIECE_F)
            for h in range(mail_ref.shape[1])
            for f in range(PIECES_WO)
        ]
        wo = jnp.concatenate(tiles, axis=1)
        part = jnp.dot(attended, wo, preferred_element_type=jnp.float32)
        part = part.astype(jnp.bfloat16).astype(jnp.float32)
        total = part if total is None else total + part
    total = pltpu.roll(total, shift, 0)
    out_ref[...] = (tokens_ref[...].astype(jnp.float32) + total).astype(jnp.bfloat16)


def finish(where, mail, tokens, attended, shift):
    vmem = pl.BlockSpec(memory_space=pltpu.VMEM)
    return pl.pallas_call(
        functools.partial(finish_kernel, shift),
        in_specs=[pl.BlockSpec(memory_space=pltpu.SMEM)] + [vmem] * (2 + len(attended)),
        out_specs=vmem,
        out_shape=jax.ShapeDtypeStruct(tokens.shape, jnp.bfloat16),
        compiler_params=pltpu.CompilerParams(vmem_limit_bytes=VMEM_LIMIT),
        name="finish",
    )(where, mail, tokens, *attended)


def body(tokens, x_gain, nbr_gain, database, nbr_shard, nbr_row, nbr_count, wq, wk, wv, wo):
    n_seq = lax.axis_size("seq")
    n_ten = lax.axis_size("tensor")
    tok_dev = tokens.shape[0]
    span_dev = nbr_shard.shape[0]
    span_len = tok_dev // span_dev
    shift = span_len - 1
    per_shard, nbr_len, d_part = database.shape
    items = span_dev * NB
    pieces_t = nbr_len // PIECE_T
    pieces_f = d_part // PIECE_F
    seq_at = lax.axis_index("seq")
    me = lax.axis_index("tensor")
    where = ((me + jnp.arange(n_ten, dtype=jnp.int32)) % n_ten).astype(jnp.int32)

    pieces = cut(nbr_shard, nbr_row, nbr_count, database)
    spread = lax.all_to_all(pieces, "seq", split_axis=0, concat_axis=0, tiled=True)
    n_notes = 2 * items + span_dev
    notes = spread[:, per_shard, 0, :n_notes].astype(jnp.int32)
    index = notes[:, :items] * (per_shard + 1) + notes[:, items : 2 * items]
    prev_count = jnp.where(seq_at > 0, notes[jnp.maximum(seq_at - 1, 0), n_notes - 1], 0)
    counts = jnp.concatenate([nbr_count, prev_count[None]])

    halves = d_part // (PIECES_WO * PIECE_F)
    strips = n_seq // halves
    own = jnp.stack([seq_at // halves, seq_at % halves]).astype(jnp.int32)
    own, _ = lax.optimization_barrier((own, pieces))
    mine = letter(own, tokens, wo, wo.shape[0] // strips)
    letters = ring_gather(mine, n_ten, tok_dev // PIECE_T * (pieces_f // 2))

    spread, index, _ = lax.optimization_barrier((spread, index, letters[3:5]))
    spread = spread.reshape(n_seq * (per_shard + 1), PIECE_T, PIECE_F)
    (picked,) = pick(index, spread, 1)
    nbr_gain, _ = lax.optimization_barrier((nbr_gain, picked))
    both = jnp.concatenate([wk, wv], axis=1).astype(jnp.float32)
    both = (both * nbr_gain.astype(jnp.float32)[:, None]).astype(jnp.bfloat16)
    both = both.reshape(n_ten, d_part, both.shape[1])
    rows = lax.all_to_all(picked, "seq", split_axis=0, concat_axis=0, tiled=True)
    queries, strip = query(where, letters, x_gain, wq, tok_dev, shift, n_seq)
    rows, queries, strip, both, counts = lax.optimization_barrier(
        (rows, queries, strip, both, counts)
    )

    def send_mail(first, second):
        mail, _ = lax.optimization_barrier((strip, second))
        mail = lax.all_to_all(mail, "seq", split_axis=0, concat_axis=0, tiled=True)
        return mail.reshape(strips, halves, *strip.shape[1:])

    rows = rows.reshape(pieces_f, pieces_t, items, PIECE_T, PIECE_F)
    streams = [rows[:, :, items // 2 :], rows[:, :, : items // 2]]
    (late, early), mail = ring_project(streams, where, both, n_ten, send_mail)
    prev = lax.ppermute(late[-1], "seq", [(i, i + 1) for i in range(n_seq - 1)])
    attended = attend(counts, queries, late, span_dev // 2, span_len, prev=prev)
    attended = attend(counts, queries, early, 0, span_len, after=attended)
    gathered = ring_gather(attended, n_ten, tok_dev // 2)
    return finish(where, mail, tokens, gathered, shift)


def solution(mesh):
    placed = (
        P("seq", "tensor"),
        P(),
        P(),
        P("seq", None, "tensor"),
        P("seq", None),
        P("seq", None),
        P("seq"),
        P(None, "tensor"),
        P(None, "tensor"),
        P(None, "tensor"),
        P("tensor", None),
    )
    return jax.shard_map(
        body, mesh=mesh, in_specs=placed, out_specs=P("seq", "tensor"), check_vma=False
    )
```

```python
import functools

import jax
import jax.numpy as jnp
from jax import lax
from jax.experimental import pallas as pl
from jax.experimental.pallas import tpu as pltpu
from jax.sharding import PartitionSpec as P

HS = 128
NB = 2
PIECE_T = 16
PIECE_F = 128
PIECES_WO = 2
RING_ORDER = (0, 7, 1, 6, 2, 5, 3, 4)
VMEM_LIMIT = 48 * 1024 * 1024


def cut_kernel(shard_ref, row_ref, count_ref, db_ref, out_ref):
    shard = db_ref.shape[0]
    pieces_t = db_ref.shape[1] // PIECE_T
    pieces_f = db_ref.shape[2] // PIECE_F
    each, spans = shard_ref.shape
    lane = lax.broadcasted_iota(jnp.int32, (PIECE_T, PIECE_F), 1)
    note = jnp.zeros((PIECE_T, PIECE_F), jnp.int32)
    for span in range(spans):
        for j in range(each):
            at = span * each + j
            note = jnp.where(lane == at, shard_ref[j : j + 1, span : span + 1], note)
            row = row_ref[j : j + 1, span : span + 1]
            note = jnp.where(lane == spans * each + at, row, note)
        count = count_ref[:, span : span + 1]
        note = jnp.where(lane == 2 * spans * each + span, count, note)
    note = note.astype(jnp.float32).astype(jnp.bfloat16)
    for f in range(pieces_f):
        for i in range(pieces_t):
            piece = f * pieces_t + i
            out_ref[piece, :shard] = db_ref[
                :, i * PIECE_T : (i + 1) * PIECE_T, f * PIECE_F : (f + 1) * PIECE_F
            ]
            out_ref[piece, shard] = note


def cut(nbr_shard, nbr_row, nbr_count, database):
    shard, length, part = database.shape
    pieces = (length // PIECE_T) * (part // PIECE_F)
    vmem = pl.BlockSpec(memory_space=pltpu.VMEM)
    return pl.pallas_call(
        cut_kernel,
        in_specs=[vmem] * 4,
        out_specs=vmem,
        out_shape=jax.ShapeDtypeStruct((pieces, shard + 1, PIECE_T, PIECE_F), database.dtype),
        compiler_params=pltpu.CompilerParams(vmem_limit_bytes=VMEM_LIMIT),
        name="cut",
    )(nbr_shard.T, nbr_row.T, nbr_count.reshape(1, -1), database)


def pick_kernel(index_ref, spread_ref, *out_refs):
    n_seq, items = out_refs[0].shape[:2]

    def one(dest, carry):
        for at, out_ref in enumerate(out_refs):
            for j in range(items):
                out_ref[dest, j] = spread_ref[index_ref[dest, at * items + j]]
        return carry

    lax.fori_loop(0, n_seq, one, 0, unroll=2)


def pick(index, spread, parts):
    vmem = pl.BlockSpec(memory_space=pltpu.VMEM)
    shape = (index.shape[0], index.shape[1] // parts, PIECE_T, PIECE_F)
    return pl.pallas_call(
        pick_kernel,
        in_specs=[pl.BlockSpec(memory_space=pltpu.SMEM), vmem],
        out_specs=[vmem] * parts,
        out_shape=[jax.ShapeDtypeStruct(shape, spread.dtype)] * parts,
        compiler_params=pltpu.CompilerParams(vmem_limit_bytes=VMEM_LIMIT),
        name="pick",
    )(index, spread)


def letter_kernel(at_ref, tokens_ref, wo_ref, out_ref):
    rows, part = tokens_ref.shape
    pieces_t = rows // PIECE_T
    pieces_f = part // PIECE_F
    for f in range(pieces_f):
        for i in range(pieces_t):
            out_ref[f * pieces_t + i] = tokens_ref[
                i * PIECE_T : (i + 1) * PIECE_T, f * PIECE_F : (f + 1) * PIECE_F
            ]
    strip = PIECES_WO * PIECE_F
    for group in range(wo_ref.shape[1] // part):
        for f in range(PIECES_WO):
            start = pl.multiple_of(group * part + at_ref[1] * strip + f * PIECE_F, PIECE_F)
            out_ref[pieces_f * pieces_t + group * PIECES_WO + f] = wo_ref[:, pl.ds(start, PIECE_F)]


def letter(at, tokens, wo, depth):
    rows, part = tokens.shape
    tiles = rows * part // (PIECE_T * PIECE_F) + wo.shape[1] // part * PIECES_WO
    return pl.pallas_call(
        letter_kernel,
        grid_spec=pltpu.PrefetchScalarGridSpec(
            num_scalar_prefetch=1,
            grid=(1,),
            in_specs=[
                pl.BlockSpec((rows, part), lambda g, at: (0, 0)),
                pl.BlockSpec((depth, wo.shape[1]), lambda g, at: (at[0], 0)),
            ],
            out_specs=pl.BlockSpec((tiles, PIECE_T, PIECE_F), lambda g, at: (0, 0, 0)),
        ),
        out_shape=jax.ShapeDtypeStruct((tiles, PIECE_T, PIECE_F), tokens.dtype),
        name="letter",
    )(at, tokens, wo)


def unpack(x_ref):
    features, pieces_t, items = x_ref.shape[:3]
    rows = pieces_t * items * PIECE_T
    pieces = [x_ref[f].reshape(rows, PIECE_F) for f in range(features)]
    squares = jnp.zeros((rows, PIECE_F), jnp.float32)
    for piece in pieces:
        wide = piece.astype(jnp.float32)
        squares = squares + wide * wide
    return jnp.concatenate(pieces, axis=1), squares


def store_spans(acc, squares, features, out_refs):
    mean = jnp.sum(squares, axis=1, keepdims=True) * (1.0 / features)
    done = (acc * lax.rsqrt(mean + 1e-06)).astype(jnp.bfloat16)
    pieces_t = out_refs[0].shape[0]
    done = done.reshape(pieces_t, NB * len(out_refs), PIECE_T, done.shape[-1])
    for span, ref in enumerate(out_refs):
        ref[...] = done[:, span * NB : (span + 1) * NB]


def query_kernel(shift, halved, where_ref, gain_ref, wq_ref, *rest):
    x_refs, (out_ref, strip_ref) = rest[:-2], rest[-2:]
    rows = out_ref.shape[0]
    groups, _, part = gain_ref.shape
    pieces_t = rows // PIECE_T
    tiles = pieces_t * (part // PIECE_F)
    whole = list(x_refs[:-2])

    def tile_rows(k, f):
        first = f * pieces_t
        if k < groups - 1:
            return x_refs[k][first : first + pieces_t].reshape(rows, PIECE_F)
        ref, start = (x_refs[-2], 0) if first < halved else (x_refs[-1], halved)
        return ref[first - start : first - start + pieces_t].reshape(rows, PIECE_F)

    squares = jnp.zeros((rows, PIECE_F), jnp.float32)
    for k in range(groups):
        for f in range(part // PIECE_F):
            wide = tile_rows(k, f).astype(jnp.float32)
            squares = squares + wide * wide
    mean = jnp.sum(squares, axis=1, keepdims=True) * (1.0 / (groups * part))
    inverse = lax.rsqrt(mean + 1e-06)
    total = jnp.zeros(out_ref.shape, jnp.float32)
    me = where_ref[0]
    for k in range(groups):
        group = where_ref[RING_ORDER[k]]
        x = jnp.concatenate([tile_rows(k, f) for f in range(part // PIECE_F)], axis=1)
        gain = gain_ref[group].astype(jnp.float32)
        normed = (x.astype(jnp.float32) * inverse * gain).astype(jnp.bfloat16)
        total = total + jnp.dot(normed, wq_ref[group], preferred_element_type=jnp.float32)
        for f in range(PIECES_WO):
            at = tiles + me * PIECES_WO + f
            ref = whole[k] if k < groups - 1 else x_refs[-1]
            at = at if k < groups - 1 else at - halved
            tile = ref[at]
            for dest in range(strip_ref.shape[0]):
                strip_ref[dest, group * PIECES_WO + f] = tile
    total = pltpu.roll(total * HS ** (-0.5), rows - shift, 0)
    out_ref[...] = total.astype(jnp.bfloat16)


def query(where, letters, gain, wq, rows, shift, copies):
    groups = where.shape[0]
    part = wq.shape[0] // groups
    cols = wq.shape[1]
    vmem = pl.BlockSpec(memory_space=pltpu.VMEM)
    return pl.pallas_call(
        functools.partial(query_kernel, shift, letters[-2].shape[0]),
        in_specs=[pl.BlockSpec(memory_space=pltpu.SMEM)] + [vmem] * (2 + len(letters)),
        out_specs=[vmem] * 2,
        out_shape=[
            jax.ShapeDtypeStruct((rows, cols), jnp.bfloat16),
            jax.ShapeDtypeStruct((copies, groups * PIECES_WO, PIECE_T, PIECE_F), jnp.bfloat16),
        ],
        compiler_params=pltpu.CompilerParams(vmem_limit_bytes=VMEM_LIMIT),
        cost_estimate=pl.CostEstimate(
            flops=8 * rows * groups * part * cols,
            bytes_accessed=4 * groups * part * (rows + cols),
            transcendentals=0,
        ),
        name="query",
    )(where, gain.reshape(groups, 1, part), wq.reshape(groups, part, cols), *letters)


def gather_kernel(places, first, last, where_ref, w_ref, *rest):
    count = len(places)
    x_refs, rest = rest[:count], rest[count:]
    if not first:
        acc, squares = rest[0][...], rest[1][...]
        rest = rest[2:]
    for at, (x_ref, (place, start)) in enumerate(zip(x_refs, places)):
        x, more = unpack(x_ref)
        lane = start * PIECE_F
        w = w_ref[where_ref[place], lane : lane + x.shape[1], :]
        term = jnp.dot(x, w, preferred_element_type=jnp.float32)
        if first and at == 0:
            acc, squares = term, more
        else:
            acc, squares = acc + term, squares + more
    if last:
        store_spans(acc, squares, w_ref.shape[0] * w_ref.shape[1], rest)
    else:
        rest[0][...] = acc
        rest[1][...] = squares


def gather_step(blocks, places, where, weights, state, last):
    _, part, cols = weights.shape
    _, pieces_t, items = blocks[0].shape[:3]
    rows = pieces_t * items * PIECE_T
    vmem = pl.BlockSpec(memory_space=pltpu.VMEM)
    if last:
        span = jax.ShapeDtypeStruct((pieces_t, NB, PIECE_T, cols), jnp.bfloat16)
        out_shape = [span] * (items // NB)
    else:
        out_shape = [
            jax.ShapeDtypeStruct((rows, cols), jnp.float32),
            jax.ShapeDtypeStruct((rows, PIECE_F), jnp.float32),
        ]
    return pl.pallas_call(
        functools.partial(gather_kernel, tuple(places), not state, last),
        in_specs=[pl.BlockSpec(memory_space=pltpu.SMEM)]
        + [vmem] * (1 + len(blocks) + len(state)),
        out_specs=[vmem] * len(out_shape),
        out_shape=out_shape,
        compiler_params=pltpu.CompilerParams(vmem_limit_bytes=VMEM_LIMIT),
        cost_estimate=pl.CostEstimate(
            flops=8 * rows * cols * sum(block.shape[0] for block in blocks) * PIECE_F,
            bytes_accessed=2 * sum(block.size for block in blocks) + 8 * rows * cols,
            transcendentals=0,
        ),
        name="gather_last" if last else "gather_step",
    )(where, weights, *blocks, *state)


def ring_ways(n_ten):
    right = [(i, (i + 1) % n_ten) for i in range(n_ten)]
    left = [(i, (i - 1) % n_ten) for i in range(n_ten)]
    return right, left


def ring_gather(block, n_ten, cut_at):
    right, left = ring_ways(n_ten)
    go_right = go_left = block
    blocks = [block]
    for _ in range(1, n_ten // 2):
        go_right = lax.ppermute(go_right, "tensor", right)
        go_left = lax.ppermute(go_left, "tensor", left)
        blocks += [go_right, go_left]
    return blocks + [
        lax.ppermute(go_right[:cut_at], "tensor", right),
        lax.ppermute(go_left[cut_at:], "tensor", left),
    ]


def ring_project(streams, where, weights, n_ten):
    right, left = ring_ways(n_ten)
    half = streams[0].shape[0] // 2
    last = n_ten // 2
    go_right, go_left = list(streams), list(streams)
    blocks = [[x] for x in streams]
    places = [[(0, 0)] for _ in streams]
    states = [()] * len(streams)
    for step in range(1, last):
        for s in range(len(streams)):
            go_right[s] = lax.ppermute(go_right[s], "tensor", right)
            go_left[s] = lax.ppermute(go_left[s], "tensor", left)
            blocks[s] += [go_right[s], go_left[s]]
            places[s] += [(n_ten - step, 0), (step, 0)]
            if step == last - 2:
                states[s] = gather_step(blocks[s], places[s], where, weights, (), False)
                blocks[s], places[s] = [], []
    arrivals = None
    for s in range(len(streams)):
        blocks[s] += [
            lax.ppermute(go_right[s][:half], "tensor", right),
            lax.ppermute(go_left[s][half:], "tensor", left),
        ]
        places[s] += [(last, 0), (last, half)]
        arrivals = blocks[s][-2:] if arrivals is None else arrivals
        states[s] = gather_step(blocks[s], places[s], where, weights, states[s], True)
    return states, arrivals


def weigh(scores, count, keys_axis_owner):
    scores = jnp.where(keys_axis_owner < count, scores, jnp.float32(-1e30))
    top = jnp.max(scores, axis=-1, keepdims=True)
    expo = jnp.exp(scores - top)
    return expo / jnp.sum(expo, axis=-1, keepdims=True)


def scores_of(queries, keys):
    return lax.dot_general(
        queries, keys, (((1,), (1,)), ((), ())), preferred_element_type=jnp.float32
    )


def attend_kernel(first, with_prev, span_len, count_ref, q_ref, *rest):
    out_ref = rest[-1]
    pair_refs, other_ref = rest[:-2], rest[-2]
    if not with_prev:
        done = other_ref.shape[0]
        out_ref[out_ref.shape[0] - done :, :] = other_ref[...]
    cols = out_ref.shape[1]
    heads = cols // HS
    spans = len(pair_refs)
    keys = pair_refs[0].shape[0] * pair_refs[0].shape[1] * pair_refs[0].shape[2]
    owner = (lax.broadcasted_iota(jnp.int32, (span_len, keys), 1) // PIECE_T) % NB
    row = lax.broadcasted_iota(jnp.int32, (span_len, keys), 0)
    for span in range(spans):
        pair = pair_refs[span][...].reshape(keys, 2 * cols)
        queries = q_ref[(first + span) * span_len : (first + span + 1) * span_len, :]
        mixed_heads = []
        for head in range(heads):
            at = slice(head * HS, (head + 1) * HS)
            value_at = slice(cols + head * HS, cols + (head + 1) * HS)
            query = queries[:, at]
            scores = scores_of(query, pair[:, at])
            if with_prev and span == spans - 1:
                prev = other_ref[...].reshape(keys, 2 * cols)
                own = row == 0
                scores = jnp.where(own, scores, scores_of(query, prev[:, at]))
                count = jnp.where(own, count_ref[first + span], count_ref[first + span + 1])
                weights = weigh(scores, count, owner)
                ours = jnp.where(own, weights, 0.0).astype(jnp.bfloat16)
                theirs = jnp.where(own, 0.0, weights).astype(jnp.bfloat16)
                result = jnp.dot(
                    ours, pair[:, value_at], preferred_element_type=jnp.float32
                ) + jnp.dot(theirs, prev[:, value_at], preferred_element_type=jnp.float32)
            else:
                weights = weigh(scores, count_ref[first + span], owner).astype(jnp.bfloat16)
                result = jnp.dot(
                    weights, pair[:, value_at], preferred_element_type=jnp.float32
                )
            mixed_heads.append(result.astype(jnp.bfloat16))
        out_ref[span * span_len : (span + 1) * span_len, :] = jnp.concatenate(mixed_heads, axis=1)


def attend(counts, queries, pairs, first, span_len, prev=None, after=None):
    cols = queries.shape[1]
    with_prev = prev is not None
    rows = len(pairs) * span_len + (0 if with_prev else after.shape[0])
    operands = [counts, queries, *pairs, prev if with_prev else after]
    vmem = pl.BlockSpec(memory_space=pltpu.VMEM)
    return pl.pallas_call(
        functools.partial(attend_kernel, first, with_prev, span_len),
        in_specs=[pl.BlockSpec(memory_space=pltpu.SMEM)] + [vmem] * (len(operands) - 1),
        out_specs=vmem,
        out_shape=jax.ShapeDtypeStruct((rows, cols), jnp.bfloat16),
        compiler_params=pltpu.CompilerParams(vmem_limit_bytes=VMEM_LIMIT),
        cost_estimate=pl.CostEstimate(
            flops=32 * len(pairs) * span_len * 256 * cols,
            bytes_accessed=4 * rows * cols,
            transcendentals=0,
        ),
        name="attend_prev" if with_prev else "attend",
    )(*operands)


def finish_kernel(shift, where_ref, mail_ref, tokens_ref, *rest):
    attended_refs, out_ref = rest[:-1], rest[-1]
    groups = where_ref.shape[0]
    depth = attended_refs[0].shape[1]
    total = None
    for k in range(groups):
        group = where_ref[RING_ORDER[k]]
        if k < groups - 1:
            attended = attended_refs[k][...]
        else:
            attended = jnp.concatenate([ref[...] for ref in attended_refs[k:]], axis=0)
        tiles = [
            mail_ref[:, h, group * PIECES_WO + f].reshape(depth, PIECE_F)
            for h in range(mail_ref.shape[1])
            for f in range(PIECES_WO)
        ]
        wo = jnp.concatenate(tiles, axis=1)
        part = jnp.dot(attended, wo, preferred_element_type=jnp.float32)
        part = part.astype(jnp.bfloat16).astype(jnp.float32)
        total = part if total is None else total + part
    total = pltpu.roll(total, shift, 0)
    out_ref[...] = (tokens_ref[...].astype(jnp.float32) + total).astype(jnp.bfloat16)


def finish(where, mail, tokens, attended, shift):
    vmem = pl.BlockSpec(memory_space=pltpu.VMEM)
    return pl.pallas_call(
        functools.partial(finish_kernel, shift),
        in_specs=[pl.BlockSpec(memory_space=pltpu.SMEM)] + [vmem] * (2 + len(attended)),
        out_specs=vmem,
        out_shape=jax.ShapeDtypeStruct(tokens.shape, jnp.bfloat16),
        compiler_params=pltpu.CompilerParams(vmem_limit_bytes=VMEM_LIMIT),
        name="finish",
    )(where, mail, tokens, *attended)


def body(tokens, x_gain, nbr_gain, database, nbr_shard, nbr_row, nbr_count, wq, wk, wv, wo):
    n_seq = lax.axis_size("seq")
    n_ten = lax.axis_size("tensor")
    tok_dev = tokens.shape[0]
    span_dev = nbr_shard.shape[0]
    span_len = tok_dev // span_dev
    shift = span_len - 1
    per_shard, nbr_len, d_part = database.shape
    items = span_dev * NB
    pieces_t = nbr_len // PIECE_T
    pieces_f = d_part // PIECE_F
    seq_at = lax.axis_index("seq")
    me = lax.axis_index("tensor")
    where = ((me + jnp.arange(n_ten, dtype=jnp.int32)) % n_ten).astype(jnp.int32)

    pieces = cut(nbr_shard, nbr_row, nbr_count, database)
    spread = lax.all_to_all(pieces, "seq", split_axis=0, concat_axis=0, tiled=True)
    n_notes = 2 * items + span_dev
    notes = spread[:, per_shard, 0, :n_notes].astype(jnp.int32)
    index = notes[:, :items] * (per_shard + 1) + notes[:, items : 2 * items]
    prev_count = jnp.where(seq_at > 0, notes[jnp.maximum(seq_at - 1, 0), n_notes - 1], 0)
    counts = jnp.concatenate([nbr_count, prev_count[None]])

    halves = d_part // (PIECES_WO * PIECE_F)
    strips = n_seq // halves
    own = jnp.stack([seq_at // halves, seq_at % halves]).astype(jnp.int32)
    own, _ = lax.optimization_barrier((own, pieces))
    mine = letter(own, tokens, wo, wo.shape[0] // strips)
    letters = ring_gather(mine, n_ten, tok_dev // PIECE_T * (pieces_f // 2))

    both = jnp.concatenate([wk, wv], axis=1).astype(jnp.float32)
    both = (both * nbr_gain.astype(jnp.float32)[:, None]).astype(jnp.bfloat16)
    both = both.reshape(n_ten, d_part, both.shape[1])
    spread, index, both, _ = lax.optimization_barrier((spread, index, both, letters[3:5]))
    spread = spread.reshape(n_seq * (per_shard + 1), PIECE_T, PIECE_F)
    (picked,) = pick(index, spread, 1)
    rows = lax.all_to_all(picked, "seq", split_axis=0, concat_axis=0, tiled=True)
    queries, strip = query(where, letters, x_gain, wq, tok_dev, shift, n_seq)
    rows, queries, counts = lax.optimization_barrier((rows, queries, counts))

    rows = rows.reshape(pieces_f, pieces_t, items, PIECE_T, PIECE_F)
    streams = [rows[:, :, items // 2 :], rows[:, :, : items // 2]]
    (late, early), arrivals = ring_project(streams, where, both, n_ten)
    strip, _ = lax.optimization_barrier((strip, arrivals))
    mail = lax.all_to_all(strip, "seq", split_axis=0, concat_axis=0, tiled=True)
    mail = mail.reshape(strips, halves, *strip.shape[1:])
    prev = lax.ppermute(late[-1], "seq", [(i, i + 1) for i in range(n_seq - 1)])
    attended = attend(counts, queries, late, span_dev // 2, span_len, prev=prev)
    attended = attend(counts, queries, early, 0, span_len, after=attended)
    gathered = ring_gather(attended, n_ten, tok_dev // 2)
    return finish(where, mail, tokens, gathered, shift)


def solution(mesh):
    placed = (
        P("seq", "tensor"),
        P(),
        P(),
        P("seq", None, "tensor"),
        P("seq", None),
        P("seq", None),
        P("seq"),
        P(None, "tensor"),
        P(None, "tensor"),
        P(None, "tensor"),
        P("tensor", None),
    )
    return jax.shard_map(
        body, mesh=mesh, in_specs=placed, out_specs=P("seq", "tensor"), check_vma=False
    )
```

```python
import functools

import jax
import jax.numpy as jnp
from jax import lax
from jax.experimental import pallas as pl
from jax.experimental.pallas import tpu as pltpu
from jax.sharding import PartitionSpec as P

HS = 128
NB = 2
PIECE_T = 16
PIECE_F = 128
PIECES_WO = 2
RING_ORDER = (0, 7, 1, 6, 2, 5, 3, 4)
VMEM_LIMIT = 48 * 1024 * 1024


def cut_kernel(shard_ref, row_ref, count_ref, db_ref, out_ref):
    shard = db_ref.shape[0]
    pieces_t = db_ref.shape[1] // PIECE_T
    pieces_f = db_ref.shape[2] // PIECE_F
    each, spans = shard_ref.shape
    lane = lax.broadcasted_iota(jnp.int32, (PIECE_T, PIECE_F), 1)
    note = jnp.zeros((PIECE_T, PIECE_F), jnp.int32)
    for span in range(spans):
        for j in range(each):
            at = span * each + j
            note = jnp.where(lane == at, shard_ref[j : j + 1, span : span + 1], note)
            row = row_ref[j : j + 1, span : span + 1]
            note = jnp.where(lane == spans * each + at, row, note)
        count = count_ref[:, span : span + 1]
        note = jnp.where(lane == 2 * spans * each + span, count, note)
    note = note.astype(jnp.float32).astype(jnp.bfloat16)
    for f in range(pieces_f):
        for i in range(pieces_t):
            piece = f * pieces_t + i
            out_ref[piece, :shard] = db_ref[
                :, i * PIECE_T : (i + 1) * PIECE_T, f * PIECE_F : (f + 1) * PIECE_F
            ]
            out_ref[piece, shard] = note


def cut(nbr_shard, nbr_row, nbr_count, database):
    shard, length, part = database.shape
    pieces = (length // PIECE_T) * (part // PIECE_F)
    vmem = pl.BlockSpec(memory_space=pltpu.VMEM)
    return pl.pallas_call(
        cut_kernel,
        in_specs=[vmem] * 4,
        out_specs=vmem,
        out_shape=jax.ShapeDtypeStruct((pieces, shard + 1, PIECE_T, PIECE_F), database.dtype),
        compiler_params=pltpu.CompilerParams(vmem_limit_bytes=VMEM_LIMIT),
        name="cut",
    )(nbr_shard.T, nbr_row.T, nbr_count.reshape(1, -1), database)


def pick_kernel(index_ref, spread_ref, *out_refs):
    n_seq, items = out_refs[0].shape[:2]

    def one(dest, carry):
        for at, out_ref in enumerate(out_refs):
            for j in range(items):
                out_ref[dest, j] = spread_ref[index_ref[dest, at * items + j]]
        return carry

    lax.fori_loop(0, n_seq, one, 0, unroll=2)


def pick(index, spread, parts):
    vmem = pl.BlockSpec(memory_space=pltpu.VMEM)
    shape = (index.shape[0], index.shape[1] // parts, PIECE_T, PIECE_F)
    return pl.pallas_call(
        pick_kernel,
        in_specs=[pl.BlockSpec(memory_space=pltpu.SMEM), vmem],
        out_specs=[vmem] * parts,
        out_shape=[jax.ShapeDtypeStruct(shape, spread.dtype)] * parts,
        compiler_params=pltpu.CompilerParams(vmem_limit_bytes=VMEM_LIMIT),
        name="pick",
    )(index, spread)


def letter_kernel(at_ref, tokens_ref, wo_ref, out_ref):
    rows, part = tokens_ref.shape
    pieces_t = rows // PIECE_T
    pieces_f = part // PIECE_F
    for f in range(pieces_f):
        for i in range(pieces_t):
            out_ref[f * pieces_t + i] = tokens_ref[
                i * PIECE_T : (i + 1) * PIECE_T, f * PIECE_F : (f + 1) * PIECE_F
            ]
    strip = PIECES_WO * PIECE_F
    for group in range(wo_ref.shape[1] // part):
        for f in range(PIECES_WO):
            start = pl.multiple_of(group * part + at_ref[1] * strip + f * PIECE_F, PIECE_F)
            out_ref[pieces_f * pieces_t + group * PIECES_WO + f] = wo_ref[:, pl.ds(start, PIECE_F)]


def letter(at, tokens, wo, depth):
    rows, part = tokens.shape
    tiles = rows * part // (PIECE_T * PIECE_F) + wo.shape[1] // part * PIECES_WO
    return pl.pallas_call(
        letter_kernel,
        grid_spec=pltpu.PrefetchScalarGridSpec(
            num_scalar_prefetch=1,
            grid=(1,),
            in_specs=[
                pl.BlockSpec((rows, part), lambda g, at: (0, 0)),
                pl.BlockSpec((depth, wo.shape[1]), lambda g, at: (at[0], 0)),
            ],
            out_specs=pl.BlockSpec((tiles, PIECE_T, PIECE_F), lambda g, at: (0, 0, 0)),
        ),
        out_shape=jax.ShapeDtypeStruct((tiles, PIECE_T, PIECE_F), tokens.dtype),
        name="letter",
    )(at, tokens, wo)


def unpack(x_ref):
    features, pieces_t, items = x_ref.shape[:3]
    rows = pieces_t * items * PIECE_T
    pieces = [x_ref[f].reshape(rows, PIECE_F) for f in range(features)]
    squares = jnp.zeros((rows, PIECE_F), jnp.float32)
    for piece in pieces:
        wide = piece.astype(jnp.float32)
        squares = squares + wide * wide
    return jnp.concatenate(pieces, axis=1), squares


def store_spans(acc, squares, features, out_refs):
    mean = jnp.sum(squares, axis=1, keepdims=True) * (1.0 / features)
    done = (acc * lax.rsqrt(mean + 1e-06)).astype(jnp.bfloat16)
    pieces_t = out_refs[0].shape[0]
    done = done.reshape(pieces_t, NB * len(out_refs), PIECE_T, done.shape[-1])
    for span, ref in enumerate(out_refs):
        ref[...] = done[:, span * NB : (span + 1) * NB]


def query_kernel(shift, halved, where_ref, gain_ref, wq_ref, *rest):
    x_refs, (out_ref, strip_ref) = rest[:-2], rest[-2:]
    rows = out_ref.shape[0]
    groups, _, part = gain_ref.shape
    pieces_t = rows // PIECE_T
    tiles = pieces_t * (part // PIECE_F)
    whole = list(x_refs[:-2])

    def tile_rows(k, f):
        first = f * pieces_t
        if k < groups - 1:
            return x_refs[k][first : first + pieces_t].reshape(rows, PIECE_F)
        ref, start = (x_refs[-2], 0) if first < halved else (x_refs[-1], halved)
        return ref[first - start : first - start + pieces_t].reshape(rows, PIECE_F)

    squares = jnp.zeros((rows, PIECE_F), jnp.float32)
    for k in range(groups):
        for f in range(part // PIECE_F):
            wide = tile_rows(k, f).astype(jnp.float32)
            squares = squares + wide * wide
    mean = jnp.sum(squares, axis=1, keepdims=True) * (1.0 / (groups * part))
    inverse = lax.rsqrt(mean + 1e-06)
    total = jnp.zeros(out_ref.shape, jnp.float32)
    me = where_ref[0]
    for k in range(groups):
        group = where_ref[RING_ORDER[k]]
        x = jnp.concatenate([tile_rows(k, f) for f in range(part // PIECE_F)], axis=1)
        gain = gain_ref[group].astype(jnp.float32)
        normed = (x.astype(jnp.float32) * inverse * gain).astype(jnp.bfloat16)
        total = total + jnp.dot(normed, wq_ref[group], preferred_element_type=jnp.float32)
        for f in range(PIECES_WO):
            at = tiles + me * PIECES_WO + f
            ref = whole[k] if k < groups - 1 else x_refs[-1]
            at = at if k < groups - 1 else at - halved
            tile = ref[at]
            for dest in range(strip_ref.shape[0]):
                strip_ref[dest, group * PIECES_WO + f] = tile
    total = pltpu.roll(total * HS ** (-0.5), rows - shift, 0)
    out_ref[...] = total.astype(jnp.bfloat16)


def query(where, letters, gain, wq, rows, shift, copies):
    groups = where.shape[0]
    part = wq.shape[0] // groups
    cols = wq.shape[1]
    vmem = pl.BlockSpec(memory_space=pltpu.VMEM)
    return pl.pallas_call(
        functools.partial(query_kernel, shift, letters[-2].shape[0]),
        in_specs=[pl.BlockSpec(memory_space=pltpu.SMEM)] + [vmem] * (2 + len(letters)),
        out_specs=[vmem] * 2,
        out_shape=[
            jax.ShapeDtypeStruct((rows, cols), jnp.bfloat16),
            jax.ShapeDtypeStruct((copies, groups * PIECES_WO, PIECE_T, PIECE_F), jnp.bfloat16),
        ],
        compiler_params=pltpu.CompilerParams(vmem_limit_bytes=VMEM_LIMIT),
        cost_estimate=pl.CostEstimate(
            flops=8 * rows * groups * part * cols,
            bytes_accessed=4 * groups * part * (rows + cols),
            transcendentals=0,
        ),
        name="query",
    )(where, gain.reshape(groups, 1, part), wq.reshape(groups, part, cols), *letters)


def gather_kernel(places, first, last, where_ref, w_ref, *rest):
    count = len(places)
    x_refs, rest = rest[:count], rest[count:]
    if not first:
        acc, squares = rest[0][...], rest[1][...]
        rest = rest[2:]
    for at, (x_ref, (place, start)) in enumerate(zip(x_refs, places)):
        x, more = unpack(x_ref)
        lane = start * PIECE_F
        w = w_ref[where_ref[place], lane : lane + x.shape[1], :]
        term = jnp.dot(x, w, preferred_element_type=jnp.float32)
        if first and at == 0:
            acc, squares = term, more
        else:
            acc, squares = acc + term, squares + more
    if last:
        store_spans(acc, squares, w_ref.shape[0] * w_ref.shape[1], rest)
    else:
        rest[0][...] = acc
        rest[1][...] = squares


def gather_step(blocks, places, where, weights, state, last):
    _, part, cols = weights.shape
    _, pieces_t, items = blocks[0].shape[:3]
    rows = pieces_t * items * PIECE_T
    vmem = pl.BlockSpec(memory_space=pltpu.VMEM)
    if last:
        span = jax.ShapeDtypeStruct((pieces_t, NB, PIECE_T, cols), jnp.bfloat16)
        out_shape = [span] * (items // NB)
    else:
        out_shape = [
            jax.ShapeDtypeStruct((rows, cols), jnp.float32),
            jax.ShapeDtypeStruct((rows, PIECE_F), jnp.float32),
        ]
    return pl.pallas_call(
        functools.partial(gather_kernel, tuple(places), not state, last),
        in_specs=[pl.BlockSpec(memory_space=pltpu.SMEM)]
        + [vmem] * (1 + len(blocks) + len(state)),
        out_specs=[vmem] * len(out_shape),
        out_shape=out_shape,
        compiler_params=pltpu.CompilerParams(vmem_limit_bytes=VMEM_LIMIT),
        cost_estimate=pl.CostEstimate(
            flops=8 * rows * cols * sum(block.shape[0] for block in blocks) * PIECE_F,
            bytes_accessed=2 * sum(block.size for block in blocks) + 8 * rows * cols,
            transcendentals=0,
        ),
        name="gather_last" if last else "gather_step",
    )(where, weights, *blocks, *state)


def ring_ways(n_ten):
    right = [(i, (i + 1) % n_ten) for i in range(n_ten)]
    left = [(i, (i - 1) % n_ten) for i in range(n_ten)]
    return right, left


def ring_gather(block, n_ten, cut_at):
    right, left = ring_ways(n_ten)
    go_right = go_left = block
    blocks = [block]
    for _ in range(1, n_ten // 2):
        go_right = lax.ppermute(go_right, "tensor", right)
        go_left = lax.ppermute(go_left, "tensor", left)
        blocks += [go_right, go_left]
    return blocks + [
        lax.ppermute(go_right[:cut_at], "tensor", right),
        lax.ppermute(go_left[cut_at:], "tensor", left),
    ]


def ring_project(streams, where, weights, n_ten, beside):
    right, left = ring_ways(n_ten)
    half = streams[0].shape[0] // 2
    last = n_ten // 2
    go_right, go_left = list(streams), list(streams)
    blocks = [[x] for x in streams]
    places = [[(0, 0)] for _ in streams]
    states = [()] * len(streams)
    for step in range(1, last + 1):
        for s in range(len(streams)):
            from_left, from_right = go_right[s], go_left[s]
            if step == last:
                held = lax.optimization_barrier((from_left, from_right, beside))
                from_left, from_right, beside = held
                from_left, from_right = from_left[:half], from_right[half:]
            if (step, s) in ((last - 1, 1), (last, 0)):
                other = states[1 - s]
                held = lax.optimization_barrier((from_left, from_right, other))
                from_left, from_right, states[1 - s] = held
            go_right[s] = lax.ppermute(from_left, "tensor", right)
            go_left[s] = lax.ppermute(from_right, "tensor", left)
            blocks[s] += [go_right[s], go_left[s]]
            places[s] += [(n_ten - step, 0), (step, half if step == last else 0)]
            if step in (last - 2, last):
                state = gather_step(blocks[s], places[s], where, weights, states[s], step == last)
                blocks[s], places[s], states[s] = [], [], state
    return states, beside


def weigh(scores, count, keys_axis_owner):
    scores = jnp.where(keys_axis_owner < count, scores, jnp.float32(-1e30))
    top = jnp.max(scores, axis=-1, keepdims=True)
    expo = jnp.exp(scores - top)
    return expo / jnp.sum(expo, axis=-1, keepdims=True)


def scores_of(queries, keys):
    return lax.dot_general(
        queries, keys, (((1,), (1,)), ((), ())), preferred_element_type=jnp.float32
    )


def attend_kernel(first, with_prev, span_len, count_ref, q_ref, *rest):
    out_ref = rest[-1]
    pair_refs, other_ref = rest[:-2], rest[-2]
    if not with_prev:
        done = other_ref.shape[0]
        out_ref[out_ref.shape[0] - done :, :] = other_ref[...]
    cols = out_ref.shape[1]
    heads = cols // HS
    spans = len(pair_refs)
    keys = pair_refs[0].shape[0] * pair_refs[0].shape[1] * pair_refs[0].shape[2]
    owner = (lax.broadcasted_iota(jnp.int32, (span_len, keys), 1) // PIECE_T) % NB
    row = lax.broadcasted_iota(jnp.int32, (span_len, keys), 0)
    for span in range(spans):
        pair = pair_refs[span][...].reshape(keys, 2 * cols)
        queries = q_ref[(first + span) * span_len : (first + span + 1) * span_len, :]
        mixed_heads = []
        for head in range(heads):
            at = slice(head * HS, (head + 1) * HS)
            value_at = slice(cols + head * HS, cols + (head + 1) * HS)
            query = queries[:, at]
            scores = scores_of(query, pair[:, at])
            if with_prev and span == spans - 1:
                prev = other_ref[...].reshape(keys, 2 * cols)
                own = row == 0
                scores = jnp.where(own, scores, scores_of(query, prev[:, at]))
                count = jnp.where(own, count_ref[first + span], count_ref[first + span + 1])
                weights = weigh(scores, count, owner)
                ours = jnp.where(own, weights, 0.0).astype(jnp.bfloat16)
                theirs = jnp.where(own, 0.0, weights).astype(jnp.bfloat16)
                result = jnp.dot(
                    ours, pair[:, value_at], preferred_element_type=jnp.float32
                ) + jnp.dot(theirs, prev[:, value_at], preferred_element_type=jnp.float32)
            else:
                weights = weigh(scores, count_ref[first + span], owner).astype(jnp.bfloat16)
                result = jnp.dot(
                    weights, pair[:, value_at], preferred_element_type=jnp.float32
                )
            mixed_heads.append(result.astype(jnp.bfloat16))
        out_ref[span * span_len : (span + 1) * span_len, :] = jnp.concatenate(mixed_heads, axis=1)


def attend(counts, queries, pairs, first, span_len, prev=None, after=None):
    cols = queries.shape[1]
    with_prev = prev is not None
    rows = len(pairs) * span_len + (0 if with_prev else after.shape[0])
    operands = [counts, queries, *pairs, prev if with_prev else after]
    vmem = pl.BlockSpec(memory_space=pltpu.VMEM)
    return pl.pallas_call(
        functools.partial(attend_kernel, first, with_prev, span_len),
        in_specs=[pl.BlockSpec(memory_space=pltpu.SMEM)] + [vmem] * (len(operands) - 1),
        out_specs=vmem,
        out_shape=jax.ShapeDtypeStruct((rows, cols), jnp.bfloat16),
        compiler_params=pltpu.CompilerParams(vmem_limit_bytes=VMEM_LIMIT),
        cost_estimate=pl.CostEstimate(
            flops=32 * len(pairs) * span_len * 256 * cols,
            bytes_accessed=4 * rows * cols,
            transcendentals=0,
        ),
        name="attend_prev" if with_prev else "attend",
    )(*operands)


def finish_kernel(shift, where_ref, mail_ref, tokens_ref, *rest):
    attended_refs, out_ref = rest[:-1], rest[-1]
    groups = where_ref.shape[0]
    depth = attended_refs[0].shape[1]
    total = None
    for k in range(groups):
        group = where_ref[RING_ORDER[k]]
        if k < groups - 1:
            attended = attended_refs[k][...]
        else:
            attended = jnp.concatenate([ref[...] for ref in attended_refs[k:]], axis=0)
        tiles = [
            mail_ref[:, h, group * PIECES_WO + f].reshape(depth, PIECE_F)
            for h in range(mail_ref.shape[1])
            for f in range(PIECES_WO)
        ]
        wo = jnp.concatenate(tiles, axis=1)
        part = jnp.dot(attended, wo, preferred_element_type=jnp.float32)
        part = part.astype(jnp.bfloat16).astype(jnp.float32)
        total = part if total is None else total + part
    total = pltpu.roll(total, shift, 0)
    out_ref[...] = (tokens_ref[...].astype(jnp.float32) + total).astype(jnp.bfloat16)


def finish(where, mail, tokens, attended, shift):
    vmem = pl.BlockSpec(memory_space=pltpu.VMEM)
    return pl.pallas_call(
        functools.partial(finish_kernel, shift),
        in_specs=[pl.BlockSpec(memory_space=pltpu.SMEM)] + [vmem] * (2 + len(attended)),
        out_specs=vmem,
        out_shape=jax.ShapeDtypeStruct(tokens.shape, jnp.bfloat16),
        compiler_params=pltpu.CompilerParams(vmem_limit_bytes=VMEM_LIMIT),
        name="finish",
    )(where, mail, tokens, *attended)


def body(tokens, x_gain, nbr_gain, database, nbr_shard, nbr_row, nbr_count, wq, wk, wv, wo):
    n_seq = lax.axis_size("seq")
    n_ten = lax.axis_size("tensor")
    tok_dev = tokens.shape[0]
    span_dev = nbr_shard.shape[0]
    span_len = tok_dev // span_dev
    shift = span_len - 1
    per_shard, nbr_len, d_part = database.shape
    items = span_dev * NB
    pieces_t = nbr_len // PIECE_T
    pieces_f = d_part // PIECE_F
    seq_at = lax.axis_index("seq")
    me = lax.axis_index("tensor")
    where = ((me + jnp.arange(n_ten, dtype=jnp.int32)) % n_ten).astype(jnp.int32)

    pieces = cut(nbr_shard, nbr_row, nbr_count, database)
    spread = lax.all_to_all(pieces, "seq", split_axis=0, concat_axis=0, tiled=True)

    halves = d_part // (PIECES_WO * PIECE_F)
    strips = n_seq // halves
    own = jnp.stack([seq_at // halves, seq_at % halves]).astype(jnp.int32)
    own, _ = lax.optimization_barrier((own, pieces))
    mine = letter(own, tokens, wo, wo.shape[0] // strips)
    letters = ring_gather(mine, n_ten, tok_dev // PIECE_T * (pieces_f // 2))

    both = jnp.concatenate([wk, wv], axis=1).astype(jnp.float32)
    both = (both * nbr_gain.astype(jnp.float32)[:, None]).astype(jnp.bfloat16)
    both = both.reshape(n_ten, d_part, both.shape[1])
    spread, both, _ = lax.optimization_barrier((spread, both, letters[3:5]))
    n_notes = 2 * items + span_dev
    spread = spread.reshape(n_seq * (per_shard + 1), PIECE_T, PIECE_F)
    notes = spread[per_shard :: per_shard + 1, 0, :n_notes].astype(jnp.int32)
    index = notes[:, :items] * (per_shard + 1) + notes[:, items : 2 * items]
    prev_count = jnp.where(seq_at > 0, notes[jnp.maximum(seq_at - 1, 0), n_notes - 1], 0)
    counts = jnp.concatenate([nbr_count, prev_count[None]])
    (picked,) = pick(index, spread, 1)
    rows = lax.all_to_all(picked, "seq", split_axis=0, concat_axis=0, tiled=True)
    queries, strip = query(where, letters, x_gain, wq, tok_dev, shift, n_seq)
    rows, queries, strip, counts = lax.optimization_barrier((rows, queries, strip, counts))
    mail = lax.all_to_all(strip, "seq", split_axis=0, concat_axis=0, tiled=True)
    mail = mail.reshape(strips, halves, *strip.shape[1:])

    rows = rows.reshape(pieces_f, pieces_t, items, PIECE_T, PIECE_F)
    streams = [rows[:, :, items // 2 :], rows[:, :, : items // 2]]
    (late, early), mail = ring_project(streams, where, both, n_ten, mail)
    prev = lax.ppermute(late[-1], "seq", [(i, i + 1) for i in range(n_seq - 1)])
    attended = attend(counts, queries, late, span_dev // 2, span_len, prev=prev)
    attended = attend(counts, queries, early, 0, span_len, after=attended)
    gathered = ring_gather(attended, n_ten, tok_dev // 2)
    return finish(where, mail, tokens, gathered, shift)


def solution(mesh):
    placed = (
        P("seq", "tensor"),
        P(),
        P(),
        P("seq", None, "tensor"),
        P("seq", None),
        P("seq", None),
        P("seq"),
        P(None, "tensor"),
        P(None, "tensor"),
        P(None, "tensor"),
        P("tensor", None),
    )
    return jax.shard_map(
        body, mesh=mesh, in_specs=placed, out_specs=P("seq", "tensor"), check_vma=False
    )
```

```python
import functools

import jax
import jax.numpy as jnp
from jax import lax
from jax.experimental import pallas as pl
from jax.experimental.pallas import tpu as pltpu
from jax.sharding import PartitionSpec as P

HS = 128
NB = 2
PIECE_T = 16
PIECE_F = 128
PIECES_WO = 2
RING_ORDER = (0, 7, 1, 6, 2, 5, 3, 4)
VMEM_LIMIT = 48 * 1024 * 1024


def cut_kernel(shard_ref, row_ref, count_ref, db_ref, out_ref):
    shard = db_ref.shape[0]
    pieces_t = db_ref.shape[1] // PIECE_T
    pieces_f = db_ref.shape[2] // PIECE_F
    each, spans = shard_ref.shape
    lane = lax.broadcasted_iota(jnp.int32, (PIECE_T, PIECE_F), 1)
    note = jnp.zeros((PIECE_T, PIECE_F), jnp.int32)
    for span in range(spans):
        for j in range(each):
            at = span * each + j
            note = jnp.where(lane == at, shard_ref[j : j + 1, span : span + 1], note)
            row = row_ref[j : j + 1, span : span + 1]
            note = jnp.where(lane == spans * each + at, row, note)
        count = count_ref[:, span : span + 1]
        note = jnp.where(lane == 2 * spans * each + span, count, note)
    note = note.astype(jnp.float32).astype(jnp.bfloat16)
    for f in range(pieces_f):
        for i in range(pieces_t):
            piece = f * pieces_t + i
            out_ref[piece, :shard] = db_ref[
                :, i * PIECE_T : (i + 1) * PIECE_T, f * PIECE_F : (f + 1) * PIECE_F
            ]
            out_ref[piece, shard] = note


def cut(nbr_shard, nbr_row, nbr_count, database):
    shard, length, part = database.shape
    pieces = (length // PIECE_T) * (part // PIECE_F)
    vmem = pl.BlockSpec(memory_space=pltpu.VMEM)
    return pl.pallas_call(
        cut_kernel,
        in_specs=[vmem] * 4,
        out_specs=vmem,
        out_shape=jax.ShapeDtypeStruct((pieces, shard + 1, PIECE_T, PIECE_F), database.dtype),
        compiler_params=pltpu.CompilerParams(vmem_limit_bytes=VMEM_LIMIT),
        name="cut",
    )(nbr_shard.T, nbr_row.T, nbr_count.reshape(1, -1), database)


def pick_kernel(index_ref, spread_ref, *out_refs):
    n_seq, items = out_refs[0].shape[:2]

    def one(dest, carry):
        for at, out_ref in enumerate(out_refs):
            for j in range(items):
                out_ref[dest, j] = spread_ref[index_ref[dest, at * items + j]]
        return carry

    lax.fori_loop(0, n_seq, one, 0, unroll=2)


def pick(index, spread, parts):
    vmem = pl.BlockSpec(memory_space=pltpu.VMEM)
    shape = (index.shape[0], index.shape[1] // parts, PIECE_T, PIECE_F)
    return pl.pallas_call(
        pick_kernel,
        in_specs=[pl.BlockSpec(memory_space=pltpu.SMEM), vmem],
        out_specs=[vmem] * parts,
        out_shape=[jax.ShapeDtypeStruct(shape, spread.dtype)] * parts,
        compiler_params=pltpu.CompilerParams(vmem_limit_bytes=VMEM_LIMIT),
        name="pick",
    )(index, spread)


def letter_kernel(at_ref, tokens_ref, wo_ref, out_ref):
    rows, part = tokens_ref.shape
    pieces_t = rows // PIECE_T
    pieces_f = part // PIECE_F
    for f in range(pieces_f):
        for i in range(pieces_t):
            out_ref[f * pieces_t + i] = tokens_ref[
                i * PIECE_T : (i + 1) * PIECE_T, f * PIECE_F : (f + 1) * PIECE_F
            ]
    strip = PIECES_WO * PIECE_F
    for group in range(wo_ref.shape[1] // part):
        for f in range(PIECES_WO):
            start = pl.multiple_of(group * part + at_ref[1] * strip + f * PIECE_F, PIECE_F)
            out_ref[pieces_f * pieces_t + group * PIECES_WO + f] = wo_ref[:, pl.ds(start, PIECE_F)]


def letter(at, tokens, wo, depth):
    rows, part = tokens.shape
    tiles = rows * part // (PIECE_T * PIECE_F) + wo.shape[1] // part * PIECES_WO
    return pl.pallas_call(
        letter_kernel,
        grid_spec=pltpu.PrefetchScalarGridSpec(
            num_scalar_prefetch=1,
            grid=(1,),
            in_specs=[
                pl.BlockSpec((rows, part), lambda g, at: (0, 0)),
                pl.BlockSpec((depth, wo.shape[1]), lambda g, at: (at[0], 0)),
            ],
            out_specs=pl.BlockSpec((tiles, PIECE_T, PIECE_F), lambda g, at: (0, 0, 0)),
        ),
        out_shape=jax.ShapeDtypeStruct((tiles, PIECE_T, PIECE_F), tokens.dtype),
        name="letter",
    )(at, tokens, wo)


def unpack(x_ref):
    features, pieces_t, items = x_ref.shape[:3]
    rows = pieces_t * items * PIECE_T
    pieces = [x_ref[f].reshape(rows, PIECE_F) for f in range(features)]
    squares = jnp.zeros((rows, PIECE_F), jnp.float32)
    for piece in pieces:
        wide = piece.astype(jnp.float32)
        squares = squares + wide * wide
    return jnp.concatenate(pieces, axis=1), squares


def store_spans(acc, squares, features, out_refs):
    mean = jnp.sum(squares, axis=1, keepdims=True) * (1.0 / features)
    done = (acc * lax.rsqrt(mean + 1e-06)).astype(jnp.bfloat16)
    pieces_t = out_refs[0].shape[0]
    done = done.reshape(pieces_t, NB * len(out_refs), PIECE_T, done.shape[-1])
    for span, ref in enumerate(out_refs):
        ref[...] = done[:, span * NB : (span + 1) * NB]


def query_kernel(shift, halved, where_ref, gain_ref, wq_ref, *rest):
    x_refs, (out_ref, strip_ref) = rest[:-2], rest[-2:]
    rows = out_ref.shape[0]
    groups, _, part = gain_ref.shape
    pieces_t = rows // PIECE_T
    tiles = pieces_t * (part // PIECE_F)
    whole = list(x_refs[:-2])

    def tile_rows(k, f):
        first = f * pieces_t
        if k < groups - 1:
            return x_refs[k][first : first + pieces_t].reshape(rows, PIECE_F)
        ref, start = (x_refs[-2], 0) if first < halved else (x_refs[-1], halved)
        return ref[first - start : first - start + pieces_t].reshape(rows, PIECE_F)

    squares = jnp.zeros((rows, PIECE_F), jnp.float32)
    for k in range(groups):
        for f in range(part // PIECE_F):
            wide = tile_rows(k, f).astype(jnp.float32)
            squares = squares + wide * wide
    mean = jnp.sum(squares, axis=1, keepdims=True) * (1.0 / (groups * part))
    inverse = lax.rsqrt(mean + 1e-06)
    total = jnp.zeros(out_ref.shape, jnp.float32)
    me = where_ref[0]
    for k in range(groups):
        group = where_ref[RING_ORDER[k]]
        x = jnp.concatenate([tile_rows(k, f) for f in range(part // PIECE_F)], axis=1)
        gain = gain_ref[group].astype(jnp.float32)
        normed = (x.astype(jnp.float32) * inverse * gain).astype(jnp.bfloat16)
        total = total + jnp.dot(normed, wq_ref[group], preferred_element_type=jnp.float32)
        for f in range(PIECES_WO):
            at = tiles + me * PIECES_WO + f
            ref = whole[k] if k < groups - 1 else x_refs[-1]
            at = at if k < groups - 1 else at - halved
            tile = ref[at]
            for dest in range(strip_ref.shape[0]):
                strip_ref[dest, group * PIECES_WO + f] = tile
    total = pltpu.roll(total * HS ** (-0.5), rows - shift, 0)
    out_ref[...] = total.astype(jnp.bfloat16)


def query(where, letters, gain, wq, rows, shift, copies):
    groups = where.shape[0]
    part = wq.shape[0] // groups
    cols = wq.shape[1]
    vmem = pl.BlockSpec(memory_space=pltpu.VMEM)
    return pl.pallas_call(
        functools.partial(query_kernel, shift, letters[-2].shape[0]),
        in_specs=[pl.BlockSpec(memory_space=pltpu.SMEM)] + [vmem] * (2 + len(letters)),
        out_specs=[vmem] * 2,
        out_shape=[
            jax.ShapeDtypeStruct((rows, cols), jnp.bfloat16),
            jax.ShapeDtypeStruct((copies, groups * PIECES_WO, PIECE_T, PIECE_F), jnp.bfloat16),
        ],
        compiler_params=pltpu.CompilerParams(vmem_limit_bytes=VMEM_LIMIT),
        cost_estimate=pl.CostEstimate(
            flops=8 * rows * groups * part * cols,
            bytes_accessed=4 * groups * part * (rows + cols),
            transcendentals=0,
        ),
        name="query",
    )(where, gain.reshape(groups, 1, part), wq.reshape(groups, part, cols), *letters)


def gather_kernel(places, first, last, where_ref, w_ref, *rest):
    count = len(places)
    x_refs, rest = rest[:count], rest[count:]
    if not first:
        acc, squares = rest[0][...], rest[1][...]
        rest = rest[2:]
    for at, (x_ref, (place, start)) in enumerate(zip(x_refs, places)):
        x, more = unpack(x_ref)
        lane = start * PIECE_F
        w = w_ref[where_ref[place], lane : lane + x.shape[1], :]
        term = jnp.dot(x, w, preferred_element_type=jnp.float32)
        if first and at == 0:
            acc, squares = term, more
        else:
            acc, squares = acc + term, squares + more
    if last:
        store_spans(acc, squares, w_ref.shape[0] * w_ref.shape[1], rest)
    else:
        rest[0][...] = acc
        rest[1][...] = squares


def gather_step(blocks, places, where, weights, state, last):
    _, part, cols = weights.shape
    _, pieces_t, items = blocks[0].shape[:3]
    rows = pieces_t * items * PIECE_T
    vmem = pl.BlockSpec(memory_space=pltpu.VMEM)
    if last:
        span = jax.ShapeDtypeStruct((pieces_t, NB, PIECE_T, cols), jnp.bfloat16)
        out_shape = [span] * (items // NB)
    else:
        out_shape = [
            jax.ShapeDtypeStruct((rows, cols), jnp.float32),
            jax.ShapeDtypeStruct((rows, PIECE_F), jnp.float32),
        ]
    return pl.pallas_call(
        functools.partial(gather_kernel, tuple(places), not state, last),
        in_specs=[pl.BlockSpec(memory_space=pltpu.SMEM)]
        + [vmem] * (1 + len(blocks) + len(state)),
        out_specs=[vmem] * len(out_shape),
        out_shape=out_shape,
        compiler_params=pltpu.CompilerParams(vmem_limit_bytes=VMEM_LIMIT),
        cost_estimate=pl.CostEstimate(
            flops=8 * rows * cols * sum(block.shape[0] for block in blocks) * PIECE_F,
            bytes_accessed=2 * sum(block.size for block in blocks) + 8 * rows * cols,
            transcendentals=0,
        ),
        name="gather_last" if last else "gather_step",
    )(where, weights, *blocks, *state)


def ring_ways(n_ten):
    right = [(i, (i + 1) % n_ten) for i in range(n_ten)]
    left = [(i, (i - 1) % n_ten) for i in range(n_ten)]
    return right, left


def ring_gather(block, n_ten, cut_at):
    right, left = ring_ways(n_ten)
    go_right = go_left = block
    blocks = [block]
    for _ in range(1, n_ten // 2):
        go_right = lax.ppermute(go_right, "tensor", right)
        go_left = lax.ppermute(go_left, "tensor", left)
        blocks += [go_right, go_left]
    return blocks + [
        lax.ppermute(go_right[:cut_at], "tensor", right),
        lax.ppermute(go_left[cut_at:], "tensor", left),
    ]


def ring_project(streams, where, weights, n_ten, beside):
    right, left = ring_ways(n_ten)
    half = streams[0].shape[0] // 2
    last = n_ten // 2
    go_right, go_left = list(streams), list(streams)
    blocks = [[x] for x in streams]
    places = [[(0, 0)] for _ in streams]
    states = [()] * len(streams)
    first_parts = []
    for step in range(1, last + 1):
        for s in range(len(streams)):
            from_left, from_right = go_right[s], go_left[s]
            if step == last:
                held = lax.optimization_barrier((from_left, from_right, beside))
                from_left, from_right, beside = held
                from_left, from_right = from_left[:half], from_right[half:]
            if (step, s) == (last - 1, 1):
                held = lax.optimization_barrier((from_left, from_right, first_parts[0]))
                from_left, from_right, _ = held
            if (step, s) == (last, 0):
                held = lax.optimization_barrier((from_left, from_right, first_parts[1]))
                from_left, from_right, _ = held
            go_right[s] = lax.ppermute(from_left, "tensor", right)
            go_left[s] = lax.ppermute(from_right, "tensor", left)
            blocks[s] += [go_right[s], go_left[s]]
            places[s] += [(n_ten - step, 0), (step, half if step == last else 0)]
            if step >= last - 2:
                state = gather_step(blocks[s], places[s], where, weights, states[s], step == last)
                blocks[s], places[s], states[s] = [], [], state
                if step == last - 2:
                    first_parts.append(state)
    return states, beside


def weigh(scores, count, keys_axis_owner):
    scores = jnp.where(keys_axis_owner < count, scores, jnp.float32(-1e30))
    top = jnp.max(scores, axis=-1, keepdims=True)
    expo = jnp.exp(scores - top)
    return expo / jnp.sum(expo, axis=-1, keepdims=True)


def scores_of(queries, keys):
    return lax.dot_general(
        queries, keys, (((1,), (1,)), ((), ())), preferred_element_type=jnp.float32
    )


def attend_kernel(first, with_prev, span_len, count_ref, q_ref, *rest):
    out_ref = rest[-1]
    pair_refs, prev_ref, done = rest[:-1], None, 0
    if with_prev:
        pair_refs, (prev_ref, before_ref) = rest[:-3], rest[-3:-1]
        done = before_ref.shape[0]
        out_ref[:done, :] = before_ref[...]
    cols = out_ref.shape[1]
    heads = cols // HS
    spans = len(pair_refs)
    keys = pair_refs[0].shape[0] * pair_refs[0].shape[1] * pair_refs[0].shape[2]
    owner = (lax.broadcasted_iota(jnp.int32, (span_len, keys), 1) // PIECE_T) % NB
    row = lax.broadcasted_iota(jnp.int32, (span_len, keys), 0)
    for span in range(spans):
        pair = pair_refs[span][...].reshape(keys, 2 * cols)
        queries = q_ref[(first + span) * span_len : (first + span + 1) * span_len, :]
        mixed_heads = []
        for head in range(heads):
            at = slice(head * HS, (head + 1) * HS)
            value_at = slice(cols + head * HS, cols + (head + 1) * HS)
            query = queries[:, at]
            scores = scores_of(query, pair[:, at])
            if with_prev and span == spans - 1:
                prev = prev_ref[...].reshape(keys, 2 * cols)
                own = row == 0
                scores = jnp.where(own, scores, scores_of(query, prev[:, at]))
                count = jnp.where(own, count_ref[first + span], count_ref[first + span + 1])
                weights = weigh(scores, count, owner)
                ours = jnp.where(own, weights, 0.0).astype(jnp.bfloat16)
                theirs = jnp.where(own, 0.0, weights).astype(jnp.bfloat16)
                result = jnp.dot(
                    ours, pair[:, value_at], preferred_element_type=jnp.float32
                ) + jnp.dot(theirs, prev[:, value_at], preferred_element_type=jnp.float32)
            else:
                weights = weigh(scores, count_ref[first + span], owner).astype(jnp.bfloat16)
                result = jnp.dot(
                    weights, pair[:, value_at], preferred_element_type=jnp.float32
                )
            mixed_heads.append(result.astype(jnp.bfloat16))
        rows = slice(done + span * span_len, done + (span + 1) * span_len)
        out_ref[rows, :] = jnp.concatenate(mixed_heads, axis=1)


def attend(counts, queries, pairs, first, span_len, prev=None, before=None):
    cols = queries.shape[1]
    with_prev = prev is not None
    rows = len(pairs) * span_len + (before.shape[0] if with_prev else 0)
    operands = [counts, queries, *pairs] + ([prev, before] if with_prev else [])
    vmem = pl.BlockSpec(memory_space=pltpu.VMEM)
    return pl.pallas_call(
        functools.partial(attend_kernel, first, with_prev, span_len),
        in_specs=[pl.BlockSpec(memory_space=pltpu.SMEM)] + [vmem] * (len(operands) - 1),
        out_specs=vmem,
        out_shape=jax.ShapeDtypeStruct((rows, cols), jnp.bfloat16),
        compiler_params=pltpu.CompilerParams(vmem_limit_bytes=VMEM_LIMIT),
        cost_estimate=pl.CostEstimate(
            flops=32 * len(pairs) * span_len * 256 * cols,
            bytes_accessed=4 * rows * cols,
            transcendentals=0,
        ),
        name="attend_prev" if with_prev else "attend",
    )(*operands)


def finish_kernel(shift, where_ref, mail_ref, tokens_ref, *rest):
    attended_refs, out_ref = rest[:-1], rest[-1]
    groups = where_ref.shape[0]
    depth = attended_refs[0].shape[1]
    total = None
    for k in range(groups):
        group = where_ref[RING_ORDER[k]]
        if k < groups - 1:
            attended = attended_refs[k][...]
        else:
            attended = jnp.concatenate([ref[...] for ref in attended_refs[k:]], axis=0)
        tiles = [
            mail_ref[:, h, group * PIECES_WO + f].reshape(depth, PIECE_F)
            for h in range(mail_ref.shape[1])
            for f in range(PIECES_WO)
        ]
        wo = jnp.concatenate(tiles, axis=1)
        part = jnp.dot(attended, wo, preferred_element_type=jnp.float32)
        part = part.astype(jnp.bfloat16).astype(jnp.float32)
        total = part if total is None else total + part
    total = pltpu.roll(total, shift, 0)
    out_ref[...] = (tokens_ref[...].astype(jnp.float32) + total).astype(jnp.bfloat16)


def finish(where, mail, tokens, attended, shift):
    vmem = pl.BlockSpec(memory_space=pltpu.VMEM)
    return pl.pallas_call(
        functools.partial(finish_kernel, shift),
        in_specs=[pl.BlockSpec(memory_space=pltpu.SMEM)] + [vmem] * (2 + len(attended)),
        out_specs=vmem,
        out_shape=jax.ShapeDtypeStruct(tokens.shape, jnp.bfloat16),
        compiler_params=pltpu.CompilerParams(vmem_limit_bytes=VMEM_LIMIT),
        name="finish",
    )(where, mail, tokens, *attended)


def body(tokens, x_gain, nbr_gain, database, nbr_shard, nbr_row, nbr_count, wq, wk, wv, wo):
    n_seq = lax.axis_size("seq")
    n_ten = lax.axis_size("tensor")
    tok_dev = tokens.shape[0]
    span_dev = nbr_shard.shape[0]
    span_len = tok_dev // span_dev
    shift = span_len - 1
    per_shard, nbr_len, d_part = database.shape
    items = span_dev * NB
    pieces_t = nbr_len // PIECE_T
    pieces_f = d_part // PIECE_F
    seq_at = lax.axis_index("seq")
    me = lax.axis_index("tensor")
    where = ((me + jnp.arange(n_ten, dtype=jnp.int32)) % n_ten).astype(jnp.int32)

    pieces = cut(nbr_shard, nbr_row, nbr_count, database)
    spread = lax.all_to_all(pieces, "seq", split_axis=0, concat_axis=0, tiled=True)

    halves = d_part // (PIECES_WO * PIECE_F)
    strips = n_seq // halves
    own = jnp.stack([seq_at // halves, seq_at % halves]).astype(jnp.int32)
    own, _ = lax.optimization_barrier((own, pieces))
    mine = letter(own, tokens, wo, wo.shape[0] // strips)
    letters = ring_gather(mine, n_ten, tok_dev // PIECE_T * (pieces_f // 2))

    spread, _ = lax.optimization_barrier((spread, letters[3:5]))
    n_notes = 2 * items + span_dev
    spread = spread.reshape(n_seq * (per_shard + 1), PIECE_T, PIECE_F)
    notes = spread[per_shard :: per_shard + 1, 0, :n_notes].astype(jnp.int32)
    index = notes[:, :items] * (per_shard + 1) + notes[:, items : 2 * items]
    prev_count = jnp.where(seq_at > 0, notes[jnp.maximum(seq_at - 1, 0), n_notes - 1], 0)
    counts = jnp.concatenate([nbr_count, prev_count[None]])
    (picked,) = pick(index, spread, 1)
    rows = lax.all_to_all(picked, "seq", split_axis=0, concat_axis=0, tiled=True)
    nbr_gain, _ = lax.optimization_barrier((nbr_gain, picked))
    both = jnp.concatenate([wk, wv], axis=1).astype(jnp.float32)
    both = (both * nbr_gain.astype(jnp.float32)[:, None]).astype(jnp.bfloat16)
    both = both.reshape(n_ten, d_part, both.shape[1])
    *tail, both = lax.optimization_barrier((*letters[7:], both))
    letters = letters[:7] + tail
    queries, strip = query(where, letters, x_gain, wq, tok_dev, shift, n_seq)
    rows, queries, strip, counts = lax.optimization_barrier((rows, queries, strip, counts))
    mail = lax.all_to_all(strip, "seq", split_axis=0, concat_axis=0, tiled=True)
    mail = mail.reshape(strips, halves, *strip.shape[1:])

    rows = rows.reshape(pieces_f, pieces_t, items, PIECE_T, PIECE_F)
    streams = [rows[:, :, items // 2 :], rows[:, :, : items // 2]]
    (late, early), mail = ring_project(streams, where, both, n_ten, mail)
    prev = lax.ppermute(late[-1], "seq", [(i, i + 1) for i in range(n_seq - 1)])
    attended = attend(counts, queries, early, 0, span_len)
    attended = attend(counts, queries, late, span_dev // 2, span_len, prev, attended)
    gathered = ring_gather(attended, n_ten, tok_dev // 2)
    return finish(where, mail, tokens, gathered, shift)


def solution(mesh):
    placed = (
        P("seq", "tensor"),
        P(),
        P(),
        P("seq", None, "tensor"),
        P("seq", None),
        P("seq", None),
        P("seq"),
        P(None, "tensor"),
        P(None, "tensor"),
        P(None, "tensor"),
        P("tensor", None),
    )
    return jax.shard_map(
        body, mesh=mesh, in_specs=placed, out_specs=P("seq", "tensor"), check_vma=False
    )
```

```python
import functools

import jax
import jax.numpy as jnp
from jax import lax
from jax.experimental import pallas as pl
from jax.experimental.pallas import tpu as pltpu
from jax.sharding import PartitionSpec as P

HS = 128
NB = 2
PIECE_T = 16
PIECE_F = 128
PIECES_WO = 2
RING_ORDER = (0, 7, 1, 6, 2, 5, 3, 4)
VMEM_LIMIT = 48 * 1024 * 1024


def cut_kernel(shard_ref, row_ref, count_ref, db_ref, out_ref):
    shard = db_ref.shape[0]
    pieces_t = db_ref.shape[1] // PIECE_T
    pieces_f = db_ref.shape[2] // PIECE_F
    each, spans = shard_ref.shape
    lane = lax.broadcasted_iota(jnp.int32, (PIECE_T, PIECE_F), 1)
    note = jnp.zeros((PIECE_T, PIECE_F), jnp.int32)
    for span in range(spans):
        for j in range(each):
            at = span * each + j
            note = jnp.where(lane == at, shard_ref[j : j + 1, span : span + 1], note)
            row = row_ref[j : j + 1, span : span + 1]
            note = jnp.where(lane == spans * each + at, row, note)
        count = count_ref[:, span : span + 1]
        note = jnp.where(lane == 2 * spans * each + span, count, note)
    note = note.astype(jnp.float32).astype(jnp.bfloat16)
    for f in range(pieces_f):
        for i in range(pieces_t):
            piece = f * pieces_t + i
            out_ref[piece, :shard] = db_ref[
                :, i * PIECE_T : (i + 1) * PIECE_T, f * PIECE_F : (f + 1) * PIECE_F
            ]
            out_ref[piece, shard] = note


def cut(nbr_shard, nbr_row, nbr_count, database):
    shard, length, part = database.shape
    pieces = (length // PIECE_T) * (part // PIECE_F)
    vmem = pl.BlockSpec(memory_space=pltpu.VMEM)
    return pl.pallas_call(
        cut_kernel,
        in_specs=[vmem] * 4,
        out_specs=vmem,
        out_shape=jax.ShapeDtypeStruct((pieces, shard + 1, PIECE_T, PIECE_F), database.dtype),
        compiler_params=pltpu.CompilerParams(vmem_limit_bytes=VMEM_LIMIT),
        name="cut",
    )(nbr_shard.T, nbr_row.T, nbr_count.reshape(1, -1), database)


def pick_kernel(index_ref, spread_ref, *out_refs):
    n_seq, items = out_refs[0].shape[:2]

    def one(dest, carry):
        for at, out_ref in enumerate(out_refs):
            for j in range(items):
                out_ref[dest, j] = spread_ref[index_ref[dest, at * items + j]]
        return carry

    lax.fori_loop(0, n_seq, one, 0, unroll=2)


def pick(index, spread, parts):
    vmem = pl.BlockSpec(memory_space=pltpu.VMEM)
    shape = (index.shape[0], index.shape[1] // parts, PIECE_T, PIECE_F)
    return pl.pallas_call(
        pick_kernel,
        in_specs=[pl.BlockSpec(memory_space=pltpu.SMEM), vmem],
        out_specs=[vmem] * parts,
        out_shape=[jax.ShapeDtypeStruct(shape, spread.dtype)] * parts,
        compiler_params=pltpu.CompilerParams(vmem_limit_bytes=VMEM_LIMIT),
        name="pick",
    )(index, spread)


def letter_kernel(at_ref, tokens_ref, wo_ref, out_ref):
    rows, part = tokens_ref.shape
    pieces_t = rows // PIECE_T
    pieces_f = part // PIECE_F
    for f in range(pieces_f):
        for i in range(pieces_t):
            out_ref[f * pieces_t + i] = tokens_ref[
                i * PIECE_T : (i + 1) * PIECE_T, f * PIECE_F : (f + 1) * PIECE_F
            ]
    strip = PIECES_WO * PIECE_F
    for group in range(wo_ref.shape[1] // part):
        for f in range(PIECES_WO):
            start = pl.multiple_of(group * part + at_ref[1] * strip + f * PIECE_F, PIECE_F)
            out_ref[pieces_f * pieces_t + group * PIECES_WO + f] = wo_ref[:, pl.ds(start, PIECE_F)]


def letter(at, tokens, wo, depth):
    rows, part = tokens.shape
    tiles = rows * part // (PIECE_T * PIECE_F) + wo.shape[1] // part * PIECES_WO
    return pl.pallas_call(
        letter_kernel,
        grid_spec=pltpu.PrefetchScalarGridSpec(
            num_scalar_prefetch=1,
            grid=(1,),
            in_specs=[
                pl.BlockSpec((rows, part), lambda g, at: (0, 0)),
                pl.BlockSpec((depth, wo.shape[1]), lambda g, at: (at[0], 0)),
            ],
            out_specs=pl.BlockSpec((tiles, PIECE_T, PIECE_F), lambda g, at: (0, 0, 0)),
        ),
        out_shape=jax.ShapeDtypeStruct((tiles, PIECE_T, PIECE_F), tokens.dtype),
        name="letter",
    )(at, tokens, wo)


def unpack(x_ref):
    features, pieces_t, items = x_ref.shape[:3]
    rows = pieces_t * items * PIECE_T
    pieces = [x_ref[f].reshape(rows, PIECE_F) for f in range(features)]
    squares = jnp.zeros((rows, PIECE_F), jnp.float32)
    for piece in pieces:
        wide = piece.astype(jnp.float32)
        squares = squares + wide * wide
    return jnp.concatenate(pieces, axis=1), squares


def store_spans(acc, squares, features, out_refs):
    mean = jnp.sum(squares, axis=1, keepdims=True) * (1.0 / features)
    done = (acc * lax.rsqrt(mean + 1e-06)).astype(jnp.bfloat16)
    pieces_t = out_refs[0].shape[0]
    done = done.reshape(pieces_t, NB * len(out_refs), PIECE_T, done.shape[-1])
    for span, ref in enumerate(out_refs):
        ref[...] = done[:, span * NB : (span + 1) * NB]


def query_kernel(shift, halved, where_ref, gain_ref, wq_ref, *rest):
    x_refs, (out_ref, strip_ref) = rest[:-2], rest[-2:]
    rows = out_ref.shape[0]
    groups, _, part = gain_ref.shape
    pieces_t = rows // PIECE_T
    tiles = pieces_t * (part // PIECE_F)
    whole = list(x_refs[:-2])

    def tile_rows(k, f):
        first = f * pieces_t
        if k < groups - 1:
            return x_refs[k][first : first + pieces_t].reshape(rows, PIECE_F)
        ref, start = (x_refs[-2], 0) if first < halved else (x_refs[-1], halved)
        return ref[first - start : first - start + pieces_t].reshape(rows, PIECE_F)

    squares = jnp.zeros((rows, PIECE_F), jnp.float32)
    for k in range(groups):
        for f in range(part // PIECE_F):
            wide = tile_rows(k, f).astype(jnp.float32)
            squares = squares + wide * wide
    mean = jnp.sum(squares, axis=1, keepdims=True) * (1.0 / (groups * part))
    inverse = lax.rsqrt(mean + 1e-06)
    total = jnp.zeros(out_ref.shape, jnp.float32)
    me = where_ref[0]
    for k in range(groups):
        group = where_ref[RING_ORDER[k]]
        x = jnp.concatenate([tile_rows(k, f) for f in range(part // PIECE_F)], axis=1)
        gain = gain_ref[group].astype(jnp.float32)
        normed = (x.astype(jnp.float32) * inverse * gain).astype(jnp.bfloat16)
        total = total + jnp.dot(normed, wq_ref[group], preferred_element_type=jnp.float32)
        for f in range(PIECES_WO):
            at = tiles + me * PIECES_WO + f
            ref = whole[k] if k < groups - 1 else x_refs[-1]
            at = at if k < groups - 1 else at - halved
            tile = ref[at]
            for dest in range(strip_ref.shape[0]):
                strip_ref[dest, group * PIECES_WO + f] = tile
    total = pltpu.roll(total * HS ** (-0.5), rows - shift, 0)
    out_ref[...] = total.astype(jnp.bfloat16)


def query(where, letters, gain, wq, rows, shift, copies):
    groups = where.shape[0]
    part = wq.shape[0] // groups
    cols = wq.shape[1]
    vmem = pl.BlockSpec(memory_space=pltpu.VMEM)
    return pl.pallas_call(
        functools.partial(query_kernel, shift, letters[-2].shape[0]),
        in_specs=[pl.BlockSpec(memory_space=pltpu.SMEM)] + [vmem] * (2 + len(letters)),
        out_specs=[vmem] * 2,
        out_shape=[
            jax.ShapeDtypeStruct((rows, cols), jnp.bfloat16),
            jax.ShapeDtypeStruct((copies, groups * PIECES_WO, PIECE_T, PIECE_F), jnp.bfloat16),
        ],
        compiler_params=pltpu.CompilerParams(vmem_limit_bytes=VMEM_LIMIT),
        cost_estimate=pl.CostEstimate(
            flops=8 * rows * groups * part * cols,
            bytes_accessed=4 * groups * part * (rows + cols),
            transcendentals=0,
        ),
        name="query",
    )(where, gain.reshape(groups, 1, part), wq.reshape(groups, part, cols), *letters)


def gather_kernel(places, first, last, where_ref, w_ref, *rest):
    count = len(places)
    x_refs, rest = rest[:count], rest[count:]
    if not first:
        acc, squares = rest[0][...], rest[1][...]
        rest = rest[2:]
    for at, (x_ref, (place, start)) in enumerate(zip(x_refs, places)):
        x, more = unpack(x_ref)
        lane = start * PIECE_F
        w = w_ref[where_ref[place], lane : lane + x.shape[1], :]
        term = jnp.dot(x, w, preferred_element_type=jnp.float32)
        if first and at == 0:
            acc, squares = term, more
        else:
            acc, squares = acc + term, squares + more
    if last:
        store_spans(acc, squares, w_ref.shape[0] * w_ref.shape[1], rest)
    else:
        rest[0][...] = acc
        rest[1][...] = squares


def gather_step(blocks, places, where, weights, state, last):
    _, part, cols = weights.shape
    _, pieces_t, items = blocks[0].shape[:3]
    rows = pieces_t * items * PIECE_T
    vmem = pl.BlockSpec(memory_space=pltpu.VMEM)
    if last:
        span = jax.ShapeDtypeStruct((pieces_t, NB, PIECE_T, cols), jnp.bfloat16)
        out_shape = [span] * (items // NB)
    else:
        out_shape = [
            jax.ShapeDtypeStruct((rows, cols), jnp.float32),
            jax.ShapeDtypeStruct((rows, PIECE_F), jnp.float32),
        ]
    return pl.pallas_call(
        functools.partial(gather_kernel, tuple(places), not state, last),
        in_specs=[pl.BlockSpec(memory_space=pltpu.SMEM)]
        + [vmem] * (1 + len(blocks) + len(state)),
        out_specs=[vmem] * len(out_shape),
        out_shape=out_shape,
        compiler_params=pltpu.CompilerParams(vmem_limit_bytes=VMEM_LIMIT),
        cost_estimate=pl.CostEstimate(
            flops=8 * rows * cols * sum(block.shape[0] for block in blocks) * PIECE_F,
            bytes_accessed=2 * sum(block.size for block in blocks) + 8 * rows * cols,
            transcendentals=0,
        ),
        name="gather_last" if last else "gather_step",
    )(where, weights, *blocks, *state)


def ring_ways(n_ten):
    right = [(i, (i + 1) % n_ten) for i in range(n_ten)]
    left = [(i, (i - 1) % n_ten) for i in range(n_ten)]
    return right, left


def ring_gather(block, n_ten, cut_at):
    right, left = ring_ways(n_ten)
    go_right = go_left = block
    blocks = [block]
    for _ in range(1, n_ten // 2):
        go_right = lax.ppermute(go_right, "tensor", right)
        go_left = lax.ppermute(go_left, "tensor", left)
        blocks += [go_right, go_left]
    return blocks + [
        lax.ppermute(go_right[:cut_at], "tensor", right),
        lax.ppermute(go_left[cut_at:], "tensor", left),
    ]


def ring_project(streams, where, weights, n_ten, beside):
    right, left = ring_ways(n_ten)
    half = streams[0].shape[0] // 2
    last = n_ten // 2
    go_right, go_left = list(streams), list(streams)
    blocks = [[x] for x in streams]
    places = [[(0, 0)] for _ in streams]
    states = [()] * len(streams)
    first_parts = []
    for step in range(1, last + 1):
        for s in range(len(streams)):
            from_left, from_right = go_right[s], go_left[s]
            if step == last:
                held = lax.optimization_barrier((from_left, from_right, beside))
                from_left, from_right, beside = held
                from_left, from_right = from_left[:half], from_right[half:]
            if (step, s) == (last - 1, 1):
                held = lax.optimization_barrier((from_left, from_right, first_parts[0]))
                from_left, from_right, _ = held
            if (step, s) == (last, 0):
                held = lax.optimization_barrier((from_left, from_right, first_parts[1]))
                from_left, from_right, _ = held
            go_right[s] = lax.ppermute(from_left, "tensor", right)
            go_left[s] = lax.ppermute(from_right, "tensor", left)
            blocks[s] += [go_right[s], go_left[s]]
            places[s] += [(n_ten - step, 0), (step, half if step == last else 0)]
            if step in (last - 2, last) or (step, s) == (last - 1, 0):
                state = gather_step(blocks[s], places[s], where, weights, states[s], step == last)
                blocks[s], places[s], states[s] = [], [], state
                if step == last - 2:
                    first_parts.append(state)
    return states, beside


def weigh(scores, count, keys_axis_owner):
    scores = jnp.where(keys_axis_owner < count, scores, jnp.float32(-1e30))
    top = jnp.max(scores, axis=-1, keepdims=True)
    expo = jnp.exp(scores - top)
    return expo / jnp.sum(expo, axis=-1, keepdims=True)


def scores_of(queries, keys):
    return lax.dot_general(
        queries, keys, (((1,), (1,)), ((), ())), preferred_element_type=jnp.float32
    )


def attend_kernel(first, with_prev, span_len, count_ref, q_ref, *rest):
    out_ref = rest[-1]
    pair_refs, prev_ref, done = rest[:-1], None, 0
    if with_prev:
        pair_refs, (prev_ref, before_ref) = rest[:-3], rest[-3:-1]
        done = before_ref.shape[0]
        out_ref[:done, :] = before_ref[...]
    cols = out_ref.shape[1]
    heads = cols // HS
    spans = len(pair_refs)
    keys = pair_refs[0].shape[0] * pair_refs[0].shape[1] * pair_refs[0].shape[2]
    owner = (lax.broadcasted_iota(jnp.int32, (span_len, keys), 1) // PIECE_T) % NB
    row = lax.broadcasted_iota(jnp.int32, (span_len, keys), 0)
    for span in range(spans):
        pair = pair_refs[span][...].reshape(keys, 2 * cols)
        queries = q_ref[(first + span) * span_len : (first + span + 1) * span_len, :]
        mixed_heads = []
        for head in range(heads):
            at = slice(head * HS, (head + 1) * HS)
            value_at = slice(cols + head * HS, cols + (head + 1) * HS)
            query = queries[:, at]
            scores = scores_of(query, pair[:, at])
            if with_prev and span == spans - 1:
                prev = prev_ref[...].reshape(keys, 2 * cols)
                own = row == 0
                scores = jnp.where(own, scores, scores_of(query, prev[:, at]))
                count = jnp.where(own, count_ref[first + span], count_ref[first + span + 1])
                weights = weigh(scores, count, owner)
                ours = jnp.where(own, weights, 0.0).astype(jnp.bfloat16)
                theirs = jnp.where(own, 0.0, weights).astype(jnp.bfloat16)
                result = jnp.dot(
                    ours, pair[:, value_at], preferred_element_type=jnp.float32
                ) + jnp.dot(theirs, prev[:, value_at], preferred_element_type=jnp.float32)
            else:
                weights = weigh(scores, count_ref[first + span], owner).astype(jnp.bfloat16)
                result = jnp.dot(
                    weights, pair[:, value_at], preferred_element_type=jnp.float32
                )
            mixed_heads.append(result.astype(jnp.bfloat16))
        rows = slice(done + span * span_len, done + (span + 1) * span_len)
        out_ref[rows, :] = jnp.concatenate(mixed_heads, axis=1)


def attend(counts, queries, pairs, first, span_len, prev=None, before=None):
    cols = queries.shape[1]
    with_prev = prev is not None
    rows = len(pairs) * span_len + (before.shape[0] if with_prev else 0)
    operands = [counts, queries, *pairs] + ([prev, before] if with_prev else [])
    vmem = pl.BlockSpec(memory_space=pltpu.VMEM)
    return pl.pallas_call(
        functools.partial(attend_kernel, first, with_prev, span_len),
        in_specs=[pl.BlockSpec(memory_space=pltpu.SMEM)] + [vmem] * (len(operands) - 1),
        out_specs=vmem,
        out_shape=jax.ShapeDtypeStruct((rows, cols), jnp.bfloat16),
        compiler_params=pltpu.CompilerParams(vmem_limit_bytes=VMEM_LIMIT),
        cost_estimate=pl.CostEstimate(
            flops=32 * len(pairs) * span_len * 256 * cols,
            bytes_accessed=4 * rows * cols,
            transcendentals=0,
        ),
        name="attend_prev" if with_prev else "attend",
    )(*operands)


def finish_kernel(shift, where_ref, mail_ref, tokens_ref, *rest):
    attended_refs, out_ref = rest[:-1], rest[-1]
    groups = where_ref.shape[0]
    depth = attended_refs[0].shape[1]
    total = None
    for k in range(groups):
        group = where_ref[RING_ORDER[k]]
        if k < groups - 1:
            attended = attended_refs[k][...]
        else:
            attended = jnp.concatenate([ref[...] for ref in attended_refs[k:]], axis=0)
        tiles = [
            mail_ref[:, h, group * PIECES_WO + f].reshape(depth, PIECE_F)
            for h in range(mail_ref.shape[1])
            for f in range(PIECES_WO)
        ]
        wo = jnp.concatenate(tiles, axis=1)
        part = jnp.dot(attended, wo, preferred_element_type=jnp.float32)
        part = part.astype(jnp.bfloat16).astype(jnp.float32)
        total = part if total is None else total + part
    total = pltpu.roll(total, shift, 0)
    out_ref[...] = (tokens_ref[...].astype(jnp.float32) + total).astype(jnp.bfloat16)


def finish(where, mail, tokens, attended, shift):
    vmem = pl.BlockSpec(memory_space=pltpu.VMEM)
    return pl.pallas_call(
        functools.partial(finish_kernel, shift),
        in_specs=[pl.BlockSpec(memory_space=pltpu.SMEM)] + [vmem] * (2 + len(attended)),
        out_specs=vmem,
        out_shape=jax.ShapeDtypeStruct(tokens.shape, jnp.bfloat16),
        compiler_params=pltpu.CompilerParams(vmem_limit_bytes=VMEM_LIMIT),
        name="finish",
    )(where, mail, tokens, *attended)


def body(tokens, x_gain, nbr_gain, database, nbr_shard, nbr_row, nbr_count, wq, wk, wv, wo):
    n_seq = lax.axis_size("seq")
    n_ten = lax.axis_size("tensor")
    tok_dev = tokens.shape[0]
    span_dev = nbr_shard.shape[0]
    span_len = tok_dev // span_dev
    shift = span_len - 1
    per_shard, nbr_len, d_part = database.shape
    items = span_dev * NB
    pieces_t = nbr_len // PIECE_T
    pieces_f = d_part // PIECE_F
    seq_at = lax.axis_index("seq")
    me = lax.axis_index("tensor")
    where = ((me + jnp.arange(n_ten, dtype=jnp.int32)) % n_ten).astype(jnp.int32)

    pieces = cut(nbr_shard, nbr_row, nbr_count, database)
    spread = lax.all_to_all(pieces, "seq", split_axis=0, concat_axis=0, tiled=True)

    halves = d_part // (PIECES_WO * PIECE_F)
    strips = n_seq // halves
    own = jnp.stack([seq_at // halves, seq_at % halves]).astype(jnp.int32)
    own, _ = lax.optimization_barrier((own, pieces))
    mine = letter(own, tokens, wo, wo.shape[0] // strips)
    letters = ring_gather(mine, n_ten, tok_dev // PIECE_T * (pieces_f // 2))

    spread, _ = lax.optimization_barrier((spread, letters[3:5]))
    n_notes = 2 * items + span_dev
    spread = spread.reshape(n_seq * (per_shard + 1), PIECE_T, PIECE_F)
    notes = spread[per_shard :: per_shard + 1, 0, :n_notes].astype(jnp.int32)
    index = notes[:, :items] * (per_shard + 1) + notes[:, items : 2 * items]
    prev_count = jnp.where(seq_at > 0, notes[jnp.maximum(seq_at - 1, 0), n_notes - 1], 0)
    counts = jnp.concatenate([nbr_count, prev_count[None]])
    (picked,) = pick(index, spread, 1)
    rows = lax.all_to_all(picked, "seq", split_axis=0, concat_axis=0, tiled=True)
    nbr_gain, _ = lax.optimization_barrier((nbr_gain, picked))
    both = jnp.concatenate([wk, wv], axis=1).astype(jnp.float32)
    both = (both * nbr_gain.astype(jnp.float32)[:, None]).astype(jnp.bfloat16)
    both = both.reshape(n_ten, d_part, both.shape[1])
    *tail, both = lax.optimization_barrier((*letters[7:], both))
    letters = letters[:7] + tail
    rows, letters, counts = lax.optimization_barrier((rows, letters, counts))
    queries, strip = query(where, letters, x_gain, wq, tok_dev, shift, n_seq)
    mail = lax.all_to_all(strip, "seq", split_axis=0, concat_axis=0, tiled=True)
    mail = mail.reshape(strips, halves, *strip.shape[1:])

    rows = rows.reshape(pieces_f, pieces_t, items, PIECE_T, PIECE_F)
    streams = [rows[:, :, items // 2 :], rows[:, :, : items // 2]]
    (late, early), mail = ring_project(streams, where, both, n_ten, mail)
    prev = lax.ppermute(late[-1], "seq", [(i, i + 1) for i in range(n_seq - 1)])
    attended = attend(counts, queries, early, 0, span_len)
    attended = attend(counts, queries, late, span_dev // 2, span_len, prev, attended)
    gathered = ring_gather(attended, n_ten, tok_dev // 2)
    return finish(where, mail, tokens, gathered, shift)


def solution(mesh):
    placed = (
        P("seq", "tensor"),
        P(),
        P(),
        P("seq", None, "tensor"),
        P("seq", None),
        P("seq", None),
        P("seq"),
        P(None, "tensor"),
        P(None, "tensor"),
        P(None, "tensor"),
        P("tensor", None),
    )
    return jax.shard_map(
        body, mesh=mesh, in_specs=placed, out_specs=P("seq", "tensor"), check_vma=False
    )
```

```python
import functools

import jax
import jax.numpy as jnp
from jax import lax
from jax.experimental import pallas as pl
from jax.experimental.pallas import tpu as pltpu
from jax.sharding import PartitionSpec as P

HS = 128
NB = 2
PIECE_T = 16
PIECE_F = 128
PIECES_WO = 2
RING_ORDER = (0, 7, 1, 6, 2, 5, 3, 4)
VMEM_LIMIT = 48 * 1024 * 1024


def cut_kernel(shard_ref, row_ref, count_ref, db_ref, out_ref):
    shard = db_ref.shape[0]
    pieces_t = db_ref.shape[1] // PIECE_T
    pieces_f = db_ref.shape[2] // PIECE_F
    each, spans = shard_ref.shape
    lane = lax.broadcasted_iota(jnp.int32, (PIECE_T, PIECE_F), 1)
    note = jnp.zeros((PIECE_T, PIECE_F), jnp.int32)
    for span in range(spans):
        for j in range(each):
            at = span * each + j
            note = jnp.where(lane == at, shard_ref[j : j + 1, span : span + 1], note)
            row = row_ref[j : j + 1, span : span + 1]
            note = jnp.where(lane == spans * each + at, row, note)
        count = count_ref[:, span : span + 1]
        note = jnp.where(lane == 2 * spans * each + span, count, note)
    note = note.astype(jnp.float32).astype(jnp.bfloat16)
    for f in range(pieces_f):
        for i in range(pieces_t):
            piece = f * pieces_t + i
            out_ref[piece, :shard] = db_ref[
                :, i * PIECE_T : (i + 1) * PIECE_T, f * PIECE_F : (f + 1) * PIECE_F
            ]
            out_ref[piece, shard] = note


def cut(nbr_shard, nbr_row, nbr_count, database):
    shard, length, part = database.shape
    pieces = (length // PIECE_T) * (part // PIECE_F)
    vmem = pl.BlockSpec(memory_space=pltpu.VMEM)
    return pl.pallas_call(
        cut_kernel,
        in_specs=[vmem] * 4,
        out_specs=vmem,
        out_shape=jax.ShapeDtypeStruct((pieces, shard + 1, PIECE_T, PIECE_F), database.dtype),
        compiler_params=pltpu.CompilerParams(vmem_limit_bytes=VMEM_LIMIT),
        name="cut",
    )(nbr_shard.T, nbr_row.T, nbr_count.reshape(1, -1), database)


def pick_kernel(index_ref, spread_ref, *out_refs):
    n_seq, items = out_refs[0].shape[:2]

    def one(dest, carry):
        for at, out_ref in enumerate(out_refs):
            for j in range(items):
                out_ref[dest, j] = spread_ref[index_ref[dest, at * items + j]]
        return carry

    lax.fori_loop(0, n_seq, one, 0, unroll=2)


def pick(index, spread, parts):
    vmem = pl.BlockSpec(memory_space=pltpu.VMEM)
    shape = (index.shape[0], index.shape[1] // parts, PIECE_T, PIECE_F)
    return pl.pallas_call(
        pick_kernel,
        in_specs=[pl.BlockSpec(memory_space=pltpu.SMEM), vmem],
        out_specs=[vmem] * parts,
        out_shape=[jax.ShapeDtypeStruct(shape, spread.dtype)] * parts,
        compiler_params=pltpu.CompilerParams(vmem_limit_bytes=VMEM_LIMIT),
        name="pick",
    )(index, spread)


def letter_kernel(at_ref, tokens_ref, wo_ref, out_ref):
    rows, part = tokens_ref.shape
    pieces_t = rows // PIECE_T
    pieces_f = part // PIECE_F
    for f in range(pieces_f):
        for i in range(pieces_t):
            out_ref[f * pieces_t + i] = tokens_ref[
                i * PIECE_T : (i + 1) * PIECE_T, f * PIECE_F : (f + 1) * PIECE_F
            ]
    strip = PIECES_WO * PIECE_F
    for group in range(wo_ref.shape[1] // part):
        for f in range(PIECES_WO):
            start = pl.multiple_of(group * part + at_ref[1] * strip + f * PIECE_F, PIECE_F)
            out_ref[pieces_f * pieces_t + group * PIECES_WO + f] = wo_ref[:, pl.ds(start, PIECE_F)]


def letter(at, tokens, wo, depth):
    rows, part = tokens.shape
    tiles = rows * part // (PIECE_T * PIECE_F) + wo.shape[1] // part * PIECES_WO
    return pl.pallas_call(
        letter_kernel,
        grid_spec=pltpu.PrefetchScalarGridSpec(
            num_scalar_prefetch=1,
            grid=(1,),
            in_specs=[
                pl.BlockSpec((rows, part), lambda g, at: (0, 0)),
                pl.BlockSpec((depth, wo.shape[1]), lambda g, at: (at[0], 0)),
            ],
            out_specs=pl.BlockSpec((tiles, PIECE_T, PIECE_F), lambda g, at: (0, 0, 0)),
        ),
        out_shape=jax.ShapeDtypeStruct((tiles, PIECE_T, PIECE_F), tokens.dtype),
        name="letter",
    )(at, tokens, wo)


def unpack(x_ref):
    features, pieces_t, items = x_ref.shape[:3]
    rows = pieces_t * items * PIECE_T
    pieces = [x_ref[f].reshape(rows, PIECE_F) for f in range(features)]
    squares = jnp.zeros((rows, PIECE_F), jnp.float32)
    for piece in pieces:
        wide = piece.astype(jnp.float32)
        squares = squares + wide * wide
    return jnp.concatenate(pieces, axis=1), squares


def store_spans(acc, squares, features, out_refs):
    mean = jnp.sum(squares, axis=1, keepdims=True) * (1.0 / features)
    done = (acc * lax.rsqrt(mean + 1e-06)).astype(jnp.bfloat16)
    pieces_t = out_refs[0].shape[0]
    done = done.reshape(pieces_t, NB * len(out_refs), PIECE_T, done.shape[-1])
    for span, ref in enumerate(out_refs):
        ref[...] = done[:, span * NB : (span + 1) * NB]


def query_kernel(shift, halved, where_ref, gain_ref, wq_ref, *rest):
    x_refs, (out_ref, strip_ref) = rest[:-2], rest[-2:]
    rows = out_ref.shape[0]
    groups, _, part = gain_ref.shape
    pieces_t = rows // PIECE_T
    tiles = pieces_t * (part // PIECE_F)
    whole = list(x_refs[:-2])

    def tile_rows(k, f):
        first = f * pieces_t
        if k < groups - 1:
            return x_refs[k][first : first + pieces_t].reshape(rows, PIECE_F)
        ref, start = (x_refs[-2], 0) if first < halved else (x_refs[-1], halved)
        return ref[first - start : first - start + pieces_t].reshape(rows, PIECE_F)

    squares = jnp.zeros((rows, PIECE_F), jnp.float32)
    for k in range(groups):
        for f in range(part // PIECE_F):
            wide = tile_rows(k, f).astype(jnp.float32)
            squares = squares + wide * wide
    mean = jnp.sum(squares, axis=1, keepdims=True) * (1.0 / (groups * part))
    inverse = lax.rsqrt(mean + 1e-06)
    total = jnp.zeros(out_ref.shape, jnp.float32)
    me = where_ref[0]
    for k in range(groups):
        group = where_ref[RING_ORDER[k]]
        x = jnp.concatenate([tile_rows(k, f) for f in range(part // PIECE_F)], axis=1)
        gain = gain_ref[group].astype(jnp.float32)
        normed = (x.astype(jnp.float32) * inverse * gain).astype(jnp.bfloat16)
        total = total + jnp.dot(normed, wq_ref[group], preferred_element_type=jnp.float32)
        for f in range(PIECES_WO):
            at = tiles + me * PIECES_WO + f
            ref = whole[k] if k < groups - 1 else x_refs[-1]
            at = at if k < groups - 1 else at - halved
            tile = ref[at]
            for dest in range(strip_ref.shape[0]):
                strip_ref[dest, group * PIECES_WO + f] = tile
    total = pltpu.roll(total * HS ** (-0.5), rows - shift, 0)
    out_ref[...] = total.astype(jnp.bfloat16)


def query(where, letters, gain, wq, rows, shift, copies):
    groups = where.shape[0]
    part = wq.shape[0] // groups
    cols = wq.shape[1]
    vmem = pl.BlockSpec(memory_space=pltpu.VMEM)
    return pl.pallas_call(
        functools.partial(query_kernel, shift, letters[-2].shape[0]),
        in_specs=[pl.BlockSpec(memory_space=pltpu.SMEM)] + [vmem] * (2 + len(letters)),
        out_specs=[vmem] * 2,
        out_shape=[
            jax.ShapeDtypeStruct((rows, cols), jnp.bfloat16),
            jax.ShapeDtypeStruct((copies, groups * PIECES_WO, PIECE_T, PIECE_F), jnp.bfloat16),
        ],
        compiler_params=pltpu.CompilerParams(vmem_limit_bytes=VMEM_LIMIT),
        cost_estimate=pl.CostEstimate(
            flops=8 * rows * groups * part * cols,
            bytes_accessed=4 * groups * part * (rows + cols),
            transcendentals=0,
        ),
        name="query",
    )(where, gain.reshape(groups, 1, part), wq.reshape(groups, part, cols), *letters)


def gather_kernel(places, first, last, where_ref, w_ref, *rest):
    count = len(places)
    x_refs, rest = rest[:count], rest[count:]
    if not first:
        acc, squares = rest[0][...], rest[1][...]
        rest = rest[2:]
    for at, (x_ref, (place, start)) in enumerate(zip(x_refs, places)):
        x, more = unpack(x_ref)
        lane = start * PIECE_F
        w = w_ref[where_ref[place], lane : lane + x.shape[1], :]
        term = jnp.dot(x, w, preferred_element_type=jnp.float32)
        if first and at == 0:
            acc, squares = term, more
        else:
            acc, squares = acc + term, squares + more
    if last:
        store_spans(acc, squares, w_ref.shape[0] * w_ref.shape[1], rest)
    else:
        rest[0][...] = acc
        rest[1][...] = squares


def gather_step(blocks, places, where, weights, state, last):
    _, part, cols = weights.shape
    _, pieces_t, items = blocks[0].shape[:3]
    rows = pieces_t * items * PIECE_T
    vmem = pl.BlockSpec(memory_space=pltpu.VMEM)
    if last:
        span = jax.ShapeDtypeStruct((pieces_t, NB, PIECE_T, cols), jnp.bfloat16)
        out_shape = [span] * (items // NB)
    else:
        out_shape = [
            jax.ShapeDtypeStruct((rows, cols), jnp.float32),
            jax.ShapeDtypeStruct((rows, PIECE_F), jnp.float32),
        ]
    return pl.pallas_call(
        functools.partial(gather_kernel, tuple(places), not state, last),
        in_specs=[pl.BlockSpec(memory_space=pltpu.SMEM)]
        + [vmem] * (1 + len(blocks) + len(state)),
        out_specs=[vmem] * len(out_shape),
        out_shape=out_shape,
        compiler_params=pltpu.CompilerParams(vmem_limit_bytes=VMEM_LIMIT),
        cost_estimate=pl.CostEstimate(
            flops=8 * rows * cols * sum(block.shape[0] for block in blocks) * PIECE_F,
            bytes_accessed=2 * sum(block.size for block in blocks) + 8 * rows * cols,
            transcendentals=0,
        ),
        name="gather_last" if last else "gather_step",
    )(where, weights, *blocks, *state)


def ring_ways(n_ten):
    right = [(i, (i + 1) % n_ten) for i in range(n_ten)]
    left = [(i, (i - 1) % n_ten) for i in range(n_ten)]
    return right, left


def ring_gather(block, n_ten, cut_at):
    right, left = ring_ways(n_ten)
    go_right = go_left = block
    blocks = [block]
    for _ in range(1, n_ten // 2):
        go_right = lax.ppermute(go_right, "tensor", right)
        go_left = lax.ppermute(go_left, "tensor", left)
        blocks += [go_right, go_left]
    return blocks + [
        lax.ppermute(go_right[:cut_at], "tensor", right),
        lax.ppermute(go_left[cut_at:], "tensor", left),
    ]


def ring_project(streams, where, weights, n_ten, beside):
    right, left = ring_ways(n_ten)
    half = streams[0].shape[0] // 2
    last = n_ten // 2
    go_right, go_left = list(streams), list(streams)
    blocks = [[x] for x in streams]
    places = [[(0, 0)] for _ in streams]
    states = [()] * len(streams)
    first_parts = []
    for step in range(1, last + 1):
        for s in range(len(streams)):
            from_left, from_right = go_right[s], go_left[s]
            if step == last:
                held = lax.optimization_barrier((from_left, from_right, beside))
                from_left, from_right, beside = held
                from_left, from_right = from_left[:half], from_right[half:]
            if (step, s) == (last - 1, 1):
                held = lax.optimization_barrier((from_left, from_right, first_parts[0]))
                from_left, from_right, _ = held
            if (step, s) == (last, 0):
                held = lax.optimization_barrier((from_left, from_right, first_parts[1]))
                from_left, from_right, _ = held
            go_right[s] = lax.ppermute(from_left, "tensor", right)
            go_left[s] = lax.ppermute(from_right, "tensor", left)
            blocks[s] += [go_right[s], go_left[s]]
            places[s] += [(n_ten - step, 0), (step, half if step == last else 0)]
            if step in (last - 2, last) or (step, s) == (last - 1, 0):
                state = gather_step(blocks[s], places[s], where, weights, states[s], step == last)
                blocks[s], places[s], states[s] = [], [], state
                if step == last - 2:
                    first_parts.append(state)
    return states, beside


def weigh(scores, count, keys_axis_owner):
    scores = jnp.where(keys_axis_owner < count, scores, jnp.float32(-1e30))
    top = jnp.max(scores, axis=-1, keepdims=True)
    expo = jnp.exp(scores - top)
    return expo / jnp.sum(expo, axis=-1, keepdims=True)


def scores_of(queries, keys):
    return lax.dot_general(
        queries, keys, (((1,), (1,)), ((), ())), preferred_element_type=jnp.float32
    )


def attend_kernel(first, with_prev, span_len, count_ref, q_ref, *rest):
    out_ref = rest[-1]
    pair_refs, prev_ref, done = rest[:-1], None, 0
    if with_prev:
        pair_refs, (prev_ref, before_ref) = rest[:-3], rest[-3:-1]
        done = before_ref.shape[0]
        out_ref[:done, :] = before_ref[...]
    cols = out_ref.shape[1]
    heads = cols // HS
    spans = len(pair_refs)
    keys = pair_refs[0].shape[0] * pair_refs[0].shape[1] * pair_refs[0].shape[2]
    owner = (lax.broadcasted_iota(jnp.int32, (span_len, keys), 1) // PIECE_T) % NB
    row = lax.broadcasted_iota(jnp.int32, (span_len, keys), 0)
    for span in range(spans):
        pair = pair_refs[span][...].reshape(keys, 2 * cols)
        queries = q_ref[(first + span) * span_len : (first + span + 1) * span_len, :]
        mixed_heads = []
        for head in range(heads):
            at = slice(head * HS, (head + 1) * HS)
            value_at = slice(cols + head * HS, cols + (head + 1) * HS)
            query = queries[:, at]
            scores = scores_of(query, pair[:, at])
            if with_prev and span == spans - 1:
                prev = prev_ref[...].reshape(keys, 2 * cols)
                own = row == 0
                scores = jnp.where(own, scores, scores_of(query, prev[:, at]))
                count = jnp.where(own, count_ref[first + span], count_ref[first + span + 1])
                weights = weigh(scores, count, owner)
                ours = jnp.where(own, weights, 0.0).astype(jnp.bfloat16)
                theirs = jnp.where(own, 0.0, weights).astype(jnp.bfloat16)
                result = jnp.dot(
                    ours, pair[:, value_at], preferred_element_type=jnp.float32
                ) + jnp.dot(theirs, prev[:, value_at], preferred_element_type=jnp.float32)
            else:
                weights = weigh(scores, count_ref[first + span], owner).astype(jnp.bfloat16)
                result = jnp.dot(
                    weights, pair[:, value_at], preferred_element_type=jnp.float32
                )
            mixed_heads.append(result.astype(jnp.bfloat16))
        rows = slice(done + span * span_len, done + (span + 1) * span_len)
        out_ref[rows, :] = jnp.concatenate(mixed_heads, axis=1)


def attend(counts, queries, pairs, first, span_len, prev=None, before=None):
    cols = queries.shape[1]
    with_prev = prev is not None
    rows = len(pairs) * span_len + (before.shape[0] if with_prev else 0)
    operands = [counts, queries, *pairs] + ([prev, before] if with_prev else [])
    vmem = pl.BlockSpec(memory_space=pltpu.VMEM)
    return pl.pallas_call(
        functools.partial(attend_kernel, first, with_prev, span_len),
        in_specs=[pl.BlockSpec(memory_space=pltpu.SMEM)] + [vmem] * (len(operands) - 1),
        out_specs=vmem,
        out_shape=jax.ShapeDtypeStruct((rows, cols), jnp.bfloat16),
        compiler_params=pltpu.CompilerParams(vmem_limit_bytes=VMEM_LIMIT),
        cost_estimate=pl.CostEstimate(
            flops=32 * len(pairs) * span_len * 256 * cols,
            bytes_accessed=4 * rows * cols,
            transcendentals=0,
        ),
        name="attend_prev" if with_prev else "attend",
    )(*operands)


def finish_kernel(shift, where_ref, mail_ref, tokens_ref, *rest):
    attended_refs, out_ref = rest[:-1], rest[-1]
    groups = where_ref.shape[0]
    depth = attended_refs[0].shape[1]
    total = None
    for k in range(groups):
        group = where_ref[RING_ORDER[k]]
        if k < groups - 1:
            attended = attended_refs[k][...]
        else:
            attended = jnp.concatenate([ref[...] for ref in attended_refs[k:]], axis=0)
        tiles = [
            mail_ref[:, h, group * PIECES_WO + f].reshape(depth, PIECE_F)
            for h in range(mail_ref.shape[1])
            for f in range(PIECES_WO)
        ]
        wo = jnp.concatenate(tiles, axis=1)
        part = jnp.dot(attended, wo, preferred_element_type=jnp.float32)
        part = part.astype(jnp.bfloat16).astype(jnp.float32)
        total = part if total is None else total + part
    total = pltpu.roll(total, shift, 0)
    out_ref[...] = (tokens_ref[...].astype(jnp.float32) + total).astype(jnp.bfloat16)


def finish(where, mail, tokens, attended, shift):
    vmem = pl.BlockSpec(memory_space=pltpu.VMEM)
    return pl.pallas_call(
        functools.partial(finish_kernel, shift),
        in_specs=[pl.BlockSpec(memory_space=pltpu.SMEM)] + [vmem] * (2 + len(attended)),
        out_specs=vmem,
        out_shape=jax.ShapeDtypeStruct(tokens.shape, jnp.bfloat16),
        compiler_params=pltpu.CompilerParams(vmem_limit_bytes=VMEM_LIMIT),
        name="finish",
    )(where, mail, tokens, *attended)


def body(tokens, x_gain, nbr_gain, database, nbr_shard, nbr_row, nbr_count, wq, wk, wv, wo):
    n_seq = lax.axis_size("seq")
    n_ten = lax.axis_size("tensor")
    tok_dev = tokens.shape[0]
    span_dev = nbr_shard.shape[0]
    span_len = tok_dev // span_dev
    shift = span_len - 1
    per_shard, nbr_len, d_part = database.shape
    items = span_dev * NB
    pieces_t = nbr_len // PIECE_T
    pieces_f = d_part // PIECE_F
    seq_at = lax.axis_index("seq")
    me = lax.axis_index("tensor")
    where = ((me + jnp.arange(n_ten, dtype=jnp.int32)) % n_ten).astype(jnp.int32)

    pieces = cut(nbr_shard, nbr_row, nbr_count, database)
    spread = lax.all_to_all(pieces, "seq", split_axis=0, concat_axis=0, tiled=True)

    halves = d_part // (PIECES_WO * PIECE_F)
    strips = n_seq // halves
    own = jnp.stack([seq_at // halves, seq_at % halves]).astype(jnp.int32)
    own, _ = lax.optimization_barrier((own, pieces))
    mine = letter(own, tokens, wo, wo.shape[0] // strips)
    letters = ring_gather(mine, n_ten, tok_dev // PIECE_T * (pieces_f // 2))

    spread, _ = lax.optimization_barrier((spread, letters[3:5]))
    n_notes = 2 * items + span_dev
    spread = spread.reshape(n_seq * (per_shard + 1), PIECE_T, PIECE_F)
    notes = spread[per_shard :: per_shard + 1, 0, :n_notes].astype(jnp.int32)
    index = notes[:, :items] * (per_shard + 1) + notes[:, items : 2 * items]
    prev_count = jnp.where(seq_at > 0, notes[jnp.maximum(seq_at - 1, 0), n_notes - 1], 0)
    counts = jnp.concatenate([nbr_count, prev_count[None]])
    (picked,) = pick(index, spread, 1)
    rows = lax.all_to_all(picked, "seq", split_axis=0, concat_axis=0, tiled=True)
    nbr_gain, _ = lax.optimization_barrier((nbr_gain, picked))
    both = jnp.concatenate([wk, wv], axis=1).astype(jnp.float32)
    both = (both * nbr_gain.astype(jnp.float32)[:, None]).astype(jnp.bfloat16)
    both = both.reshape(n_ten, d_part, both.shape[1])
    *tail, both = lax.optimization_barrier((*letters[7:], both))
    letters = letters[:7] + tail
    queries, strip = query(where, letters, x_gain, wq, tok_dev, shift, n_seq)
    rows, queries, strip, counts = lax.optimization_barrier((rows, queries, strip, counts))
    mail = lax.all_to_all(strip, "seq", split_axis=0, concat_axis=0, tiled=True)
    mail = mail.reshape(strips, halves, *strip.shape[1:])

    rows = rows.reshape(pieces_f, pieces_t, items, PIECE_T, PIECE_F)
    streams = [rows[:, :, items // 2 :], rows[:, :, : items // 2]]
    (late, early), mail = ring_project(streams, where, both, n_ten, mail)
    prev = lax.ppermute(late[-1], "seq", [(i, i + 1) for i in range(n_seq - 1)])
    attended = attend(counts, queries, early, 0, span_len)
    attended = attend(counts, queries, late, span_dev // 2, span_len, prev, attended)
    gathered = ring_gather(attended, n_ten, tok_dev // 2)
    return finish(where, mail, tokens, gathered, shift)


def solution(mesh):
    placed = (
        P("seq", "tensor"),
        P(),
        P(),
        P("seq", None, "tensor"),
        P("seq", None),
        P("seq", None),
        P("seq"),
        P(None, "tensor"),
        P(None, "tensor"),
        P(None, "tensor"),
        P("tensor", None),
    )
    return jax.shard_map(
        body, mesh=mesh, in_specs=placed, out_specs=P("seq", "tensor"), check_vma=False
    )
```

```python
import functools

import jax
import jax.numpy as jnp
from jax import lax
from jax.experimental import pallas as pl
from jax.experimental.pallas import tpu as pltpu
from jax.sharding import PartitionSpec as P

HS = 128
NB = 2
PIECE_T = 16
PIECE_F = 128
PIECES_WO = 2
RING_ORDER = (0, 7, 1, 6, 2, 5, 3, 4)
VMEM_LIMIT = 48 * 1024 * 1024


def cut_kernel(shard_ref, row_ref, count_ref, db_ref, out_ref):
    shard = db_ref.shape[0]
    pieces_t = db_ref.shape[1] // PIECE_T
    pieces_f = db_ref.shape[2] // PIECE_F
    each, spans = shard_ref.shape
    lane = lax.broadcasted_iota(jnp.int32, (PIECE_T, PIECE_F), 1)
    note = jnp.zeros((PIECE_T, PIECE_F), jnp.int32)
    for span in range(spans):
        for j in range(each):
            at = span * each + j
            note = jnp.where(lane == at, shard_ref[j : j + 1, span : span + 1], note)
            row = row_ref[j : j + 1, span : span + 1]
            note = jnp.where(lane == spans * each + at, row, note)
        count = count_ref[:, span : span + 1]
        note = jnp.where(lane == 2 * spans * each + span, count, note)
    note = note.astype(jnp.float32).astype(jnp.bfloat16)
    for f in range(pieces_f):
        for i in range(pieces_t):
            piece = f * pieces_t + i
            out_ref[piece, :shard] = db_ref[
                :, i * PIECE_T : (i + 1) * PIECE_T, f * PIECE_F : (f + 1) * PIECE_F
            ]
            out_ref[piece, shard] = note


def cut(nbr_shard, nbr_row, nbr_count, database):
    shard, length, part = database.shape
    pieces = (length // PIECE_T) * (part // PIECE_F)
    vmem = pl.BlockSpec(memory_space=pltpu.VMEM)
    return pl.pallas_call(
        cut_kernel,
        in_specs=[vmem] * 4,
        out_specs=vmem,
        out_shape=jax.ShapeDtypeStruct((pieces, shard + 1, PIECE_T, PIECE_F), database.dtype),
        compiler_params=pltpu.CompilerParams(vmem_limit_bytes=VMEM_LIMIT),
        name="cut",
    )(nbr_shard.T, nbr_row.T, nbr_count.reshape(1, -1), database)


def pick_kernel(index_ref, spread_ref, *out_refs):
    n_seq, items = out_refs[0].shape[:2]

    def one(dest, carry):
        for at, out_ref in enumerate(out_refs):
            for j in range(items):
                out_ref[dest, j] = spread_ref[index_ref[dest, at * items + j]]
        return carry

    lax.fori_loop(0, n_seq, one, 0, unroll=2)


def pick(index, spread, parts):
    vmem = pl.BlockSpec(memory_space=pltpu.VMEM)
    shape = (index.shape[0], index.shape[1] // parts, PIECE_T, PIECE_F)
    return pl.pallas_call(
        pick_kernel,
        in_specs=[pl.BlockSpec(memory_space=pltpu.SMEM), vmem],
        out_specs=[vmem] * parts,
        out_shape=[jax.ShapeDtypeStruct(shape, spread.dtype)] * parts,
        compiler_params=pltpu.CompilerParams(vmem_limit_bytes=VMEM_LIMIT),
        name="pick",
    )(index, spread)


def letter_kernel(at_ref, tokens_ref, wo_ref, out_ref):
    rows, part = tokens_ref.shape
    pieces_t = rows // PIECE_T
    pieces_f = part // PIECE_F
    for f in range(pieces_f):
        for i in range(pieces_t):
            out_ref[f * pieces_t + i] = tokens_ref[
                i * PIECE_T : (i + 1) * PIECE_T, f * PIECE_F : (f + 1) * PIECE_F
            ]
    strip = PIECES_WO * PIECE_F
    for group in range(wo_ref.shape[1] // part):
        for f in range(PIECES_WO):
            start = pl.multiple_of(group * part + at_ref[1] * strip + f * PIECE_F, PIECE_F)
            out_ref[pieces_f * pieces_t + group * PIECES_WO + f] = wo_ref[:, pl.ds(start, PIECE_F)]


def letter(at, tokens, wo, depth):
    rows, part = tokens.shape
    tiles = rows * part // (PIECE_T * PIECE_F) + wo.shape[1] // part * PIECES_WO
    return pl.pallas_call(
        letter_kernel,
        grid_spec=pltpu.PrefetchScalarGridSpec(
            num_scalar_prefetch=1,
            grid=(1,),
            in_specs=[
                pl.BlockSpec((rows, part), lambda g, at: (0, 0)),
                pl.BlockSpec((depth, wo.shape[1]), lambda g, at: (at[0], 0)),
            ],
            out_specs=pl.BlockSpec((tiles, PIECE_T, PIECE_F), lambda g, at: (0, 0, 0)),
        ),
        out_shape=jax.ShapeDtypeStruct((tiles, PIECE_T, PIECE_F), tokens.dtype),
        name="letter",
    )(at, tokens, wo)


def unpack(x_ref):
    features, pieces_t, items = x_ref.shape[:3]
    rows = pieces_t * items * PIECE_T
    pieces = [x_ref[f].reshape(rows, PIECE_F) for f in range(features)]
    squares = jnp.zeros((rows, PIECE_F), jnp.float32)
    for piece in pieces:
        wide = piece.astype(jnp.float32)
        squares = squares + wide * wide
    return jnp.concatenate(pieces, axis=1), squares


def store_spans(acc, squares, features, out_refs):
    mean = jnp.sum(squares, axis=1, keepdims=True) * (1.0 / features)
    done = (acc * lax.rsqrt(mean + 1e-06)).astype(jnp.bfloat16)
    pieces_t = out_refs[0].shape[0]
    done = done.reshape(pieces_t, NB * len(out_refs), PIECE_T, done.shape[-1])
    for span, ref in enumerate(out_refs):
        ref[...] = done[:, span * NB : (span + 1) * NB]


def query_kernel(shift, halved, where_ref, gain_ref, wq_ref, *rest):
    x_refs, (out_ref, strip_ref) = rest[:-2], rest[-2:]
    rows = out_ref.shape[0]
    groups, _, part = gain_ref.shape
    pieces_t = rows // PIECE_T
    tiles = pieces_t * (part // PIECE_F)
    whole = list(x_refs[:-2])

    def tile_rows(k, f):
        first = f * pieces_t
        if k < groups - 1:
            return x_refs[k][first : first + pieces_t].reshape(rows, PIECE_F)
        ref, start = (x_refs[-2], 0) if first < halved else (x_refs[-1], halved)
        return ref[first - start : first - start + pieces_t].reshape(rows, PIECE_F)

    squares = jnp.zeros((rows, PIECE_F), jnp.float32)
    for k in range(groups):
        for f in range(part // PIECE_F):
            wide = tile_rows(k, f).astype(jnp.float32)
            squares = squares + wide * wide
    mean = jnp.sum(squares, axis=1, keepdims=True) * (1.0 / (groups * part))
    inverse = lax.rsqrt(mean + 1e-06)
    total = jnp.zeros(out_ref.shape, jnp.float32)
    me = where_ref[0]
    for k in range(groups):
        group = where_ref[RING_ORDER[k]]
        x = jnp.concatenate([tile_rows(k, f) for f in range(part // PIECE_F)], axis=1)
        gain = gain_ref[group].astype(jnp.float32)
        normed = (x.astype(jnp.float32) * inverse * gain).astype(jnp.bfloat16)
        total = total + jnp.dot(normed, wq_ref[group], preferred_element_type=jnp.float32)
        for f in range(PIECES_WO):
            at = tiles + me * PIECES_WO + f
            ref = whole[k] if k < groups - 1 else x_refs[-1]
            at = at if k < groups - 1 else at - halved
            tile = ref[at]
            for dest in range(strip_ref.shape[0]):
                strip_ref[dest, group * PIECES_WO + f] = tile
    total = pltpu.roll(total * HS ** (-0.5), rows - shift, 0)
    out_ref[...] = total.astype(jnp.bfloat16)


def query(where, letters, gain, wq, rows, shift, copies):
    groups = where.shape[0]
    part = wq.shape[0] // groups
    cols = wq.shape[1]
    vmem = pl.BlockSpec(memory_space=pltpu.VMEM)
    return pl.pallas_call(
        functools.partial(query_kernel, shift, letters[-2].shape[0]),
        in_specs=[pl.BlockSpec(memory_space=pltpu.SMEM)] + [vmem] * (2 + len(letters)),
        out_specs=[vmem] * 2,
        out_shape=[
            jax.ShapeDtypeStruct((rows, cols), jnp.bfloat16),
            jax.ShapeDtypeStruct((copies, groups * PIECES_WO, PIECE_T, PIECE_F), jnp.bfloat16),
        ],
        compiler_params=pltpu.CompilerParams(vmem_limit_bytes=VMEM_LIMIT),
        cost_estimate=pl.CostEstimate(
            flops=8 * rows * groups * part * cols,
            bytes_accessed=4 * groups * part * (rows + cols),
            transcendentals=0,
        ),
        name="query",
    )(where, gain.reshape(groups, 1, part), wq.reshape(groups, part, cols), *letters)


def gather_kernel(places, first, last, where_ref, w_ref, *rest):
    count = len(places)
    x_refs, rest = rest[:count], rest[count:]
    if not first:
        acc, squares = rest[0][...], rest[1][...]
        rest = rest[2:]
    for at, (x_ref, (place, start)) in enumerate(zip(x_refs, places)):
        x, more = unpack(x_ref)
        lane = start * PIECE_F
        w = w_ref[where_ref[place], lane : lane + x.shape[1], :]
        term = jnp.dot(x, w, preferred_element_type=jnp.float32)
        if first and at == 0:
            acc, squares = term, more
        else:
            acc, squares = acc + term, squares + more
    if last:
        store_spans(acc, squares, w_ref.shape[0] * w_ref.shape[1], rest)
    else:
        rest[0][...] = acc
        rest[1][...] = squares


def gather_step(blocks, places, where, weights, state, last):
    _, part, cols = weights.shape
    _, pieces_t, items = blocks[0].shape[:3]
    rows = pieces_t * items * PIECE_T
    vmem = pl.BlockSpec(memory_space=pltpu.VMEM)
    if last:
        span = jax.ShapeDtypeStruct((pieces_t, NB, PIECE_T, cols), jnp.bfloat16)
        out_shape = [span] * (items // NB)
    else:
        out_shape = [
            jax.ShapeDtypeStruct((rows, cols), jnp.float32),
            jax.ShapeDtypeStruct((rows, PIECE_F), jnp.float32),
        ]
    return pl.pallas_call(
        functools.partial(gather_kernel, tuple(places), not state, last),
        in_specs=[pl.BlockSpec(memory_space=pltpu.SMEM)]
        + [vmem] * (1 + len(blocks) + len(state)),
        out_specs=[vmem] * len(out_shape),
        out_shape=out_shape,
        compiler_params=pltpu.CompilerParams(vmem_limit_bytes=VMEM_LIMIT),
        cost_estimate=pl.CostEstimate(
            flops=8 * rows * cols * sum(block.shape[0] for block in blocks) * PIECE_F,
            bytes_accessed=2 * sum(block.size for block in blocks) + 8 * rows * cols,
            transcendentals=0,
        ),
        name="gather_last" if last else "gather_step",
    )(where, weights, *blocks, *state)


def ring_ways(n_ten):
    right = [(i, (i + 1) % n_ten) for i in range(n_ten)]
    left = [(i, (i - 1) % n_ten) for i in range(n_ten)]
    return right, left


def ring_gather(block, n_ten, cut_at):
    right, left = ring_ways(n_ten)
    go_right = go_left = block
    blocks = [block]
    for _ in range(1, n_ten // 2):
        go_right = lax.ppermute(go_right, "tensor", right)
        go_left = lax.ppermute(go_left, "tensor", left)
        blocks += [go_right, go_left]
    return blocks + [
        lax.ppermute(go_right[:cut_at], "tensor", right),
        lax.ppermute(go_left[cut_at:], "tensor", left),
    ]


def ring_project(streams, where, weights, n_ten, beside):
    right, left = ring_ways(n_ten)
    half = streams[0].shape[0] // 2
    last = n_ten // 2
    go_right, go_left = list(streams), list(streams)
    blocks = [[x] for x in streams]
    places = [[(0, 0)] for _ in streams]
    states = [()] * len(streams)
    first_parts = []
    for step in range(1, last + 1):
        for s in range(len(streams)):
            from_left, from_right = go_right[s], go_left[s]
            if step == last:
                held = lax.optimization_barrier((from_left, from_right, beside))
                from_left, from_right, beside = held
                from_left, from_right = from_left[:half], from_right[half:]
            if (step, s) == (last - 1, 1):
                held = lax.optimization_barrier((from_left, from_right, first_parts[0]))
                from_left, from_right, _ = held
            if step == last:
                held = lax.optimization_barrier((from_left, from_right, first_parts[1 + s]))
                from_left, from_right, _ = held
            go_right[s] = lax.ppermute(from_left, "tensor", right)
            go_left[s] = lax.ppermute(from_right, "tensor", left)
            blocks[s] += [go_right[s], go_left[s]]
            places[s] += [(n_ten - step, 0), (step, half if step == last else 0)]
            if step in (last - 2, last) or (step, s) == (last - 1, 0):
                state = gather_step(blocks[s], places[s], where, weights, states[s], step == last)
                blocks[s], places[s], states[s] = [], [], state
                if step < last:
                    first_parts.append(state)
    return states, beside


def weigh(scores, count, keys_axis_owner):
    scores = jnp.where(keys_axis_owner < count, scores, jnp.float32(-1e30))
    top = jnp.max(scores, axis=-1, keepdims=True)
    expo = jnp.exp(scores - top)
    return expo / jnp.sum(expo, axis=-1, keepdims=True)


def scores_of(queries, keys):
    return lax.dot_general(
        queries, keys, (((1,), (1,)), ((), ())), preferred_element_type=jnp.float32
    )


def attend_kernel(span_len, count_ref, q_ref, prev_ref, *rest):
    pair_refs, out_ref = rest[:-1], rest[-1]
    cols = out_ref.shape[1]
    heads = cols // HS
    spans = len(pair_refs)
    keys = prev_ref.shape[0] * prev_ref.shape[1] * prev_ref.shape[2]
    owner = (lax.broadcasted_iota(jnp.int32, (span_len, keys), 1) // PIECE_T) % NB
    row = lax.broadcasted_iota(jnp.int32, (span_len, keys), 0)
    for span in range(spans):
        pair = pair_refs[span][...].reshape(keys, 2 * cols)
        rows = slice(span * span_len, (span + 1) * span_len)
        queries = q_ref[rows, :]
        mixed_heads = []
        for head in range(heads):
            at = slice(head * HS, (head + 1) * HS)
            value_at = slice(cols + head * HS, cols + (head + 1) * HS)
            query = queries[:, at]
            scores = scores_of(query, pair[:, at])
            if span == spans - 1:
                prev = prev_ref[...].reshape(keys, 2 * cols)
                own = row == 0
                scores = jnp.where(own, scores, scores_of(query, prev[:, at]))
                count = jnp.where(own, count_ref[span], count_ref[span + 1])
                weights = weigh(scores, count, owner)
                ours = jnp.where(own, weights, 0.0).astype(jnp.bfloat16)
                theirs = jnp.where(own, 0.0, weights).astype(jnp.bfloat16)
                result = jnp.dot(
                    ours, pair[:, value_at], preferred_element_type=jnp.float32
                ) + jnp.dot(theirs, prev[:, value_at], preferred_element_type=jnp.float32)
            else:
                weights = weigh(scores, count_ref[span], owner).astype(jnp.bfloat16)
                result = jnp.dot(
                    weights, pair[:, value_at], preferred_element_type=jnp.float32
                )
            mixed_heads.append(result.astype(jnp.bfloat16))
        out_ref[rows, :] = jnp.concatenate(mixed_heads, axis=1)


def attend(counts, queries, pairs, prev, span_len):
    cols = queries.shape[1]
    rows = len(pairs) * span_len
    vmem = pl.BlockSpec(memory_space=pltpu.VMEM)
    return pl.pallas_call(
        functools.partial(attend_kernel, span_len),
        in_specs=[pl.BlockSpec(memory_space=pltpu.SMEM)] + [vmem] * (2 + len(pairs)),
        out_specs=vmem,
        out_shape=jax.ShapeDtypeStruct((rows, cols), jnp.bfloat16),
        compiler_params=pltpu.CompilerParams(vmem_limit_bytes=VMEM_LIMIT),
        cost_estimate=pl.CostEstimate(
            flops=32 * rows * 256 * cols, bytes_accessed=4 * rows * cols, transcendentals=0
        ),
        name="attend",
    )(counts, queries, prev, *pairs)


def finish_kernel(shift, where_ref, mail_ref, tokens_ref, *rest):
    attended_refs, out_ref = rest[:-1], rest[-1]
    groups = where_ref.shape[0]
    depth = attended_refs[0].shape[1]
    total = None
    for k in range(groups):
        group = where_ref[RING_ORDER[k]]
        if k < groups - 1:
            attended = attended_refs[k][...]
        else:
            attended = jnp.concatenate([ref[...] for ref in attended_refs[k:]], axis=0)
        tiles = [
            mail_ref[:, h, group * PIECES_WO + f].reshape(depth, PIECE_F)
            for h in range(mail_ref.shape[1])
            for f in range(PIECES_WO)
        ]
        wo = jnp.concatenate(tiles, axis=1)
        part = jnp.dot(attended, wo, preferred_element_type=jnp.float32)
        part = part.astype(jnp.bfloat16).astype(jnp.float32)
        total = part if total is None else total + part
    total = pltpu.roll(total, shift, 0)
    out_ref[...] = (tokens_ref[...].astype(jnp.float32) + total).astype(jnp.bfloat16)


def finish(where, mail, tokens, attended, shift):
    vmem = pl.BlockSpec(memory_space=pltpu.VMEM)
    return pl.pallas_call(
        functools.partial(finish_kernel, shift),
        in_specs=[pl.BlockSpec(memory_space=pltpu.SMEM)] + [vmem] * (2 + len(attended)),
        out_specs=vmem,
        out_shape=jax.ShapeDtypeStruct(tokens.shape, jnp.bfloat16),
        compiler_params=pltpu.CompilerParams(vmem_limit_bytes=VMEM_LIMIT),
        name="finish",
    )(where, mail, tokens, *attended)


def body(tokens, x_gain, nbr_gain, database, nbr_shard, nbr_row, nbr_count, wq, wk, wv, wo):
    n_seq = lax.axis_size("seq")
    n_ten = lax.axis_size("tensor")
    tok_dev = tokens.shape[0]
    span_dev = nbr_shard.shape[0]
    span_len = tok_dev // span_dev
    shift = span_len - 1
    per_shard, nbr_len, d_part = database.shape
    items = span_dev * NB
    pieces_t = nbr_len // PIECE_T
    pieces_f = d_part // PIECE_F
    seq_at = lax.axis_index("seq")
    me = lax.axis_index("tensor")
    where = ((me + jnp.arange(n_ten, dtype=jnp.int32)) % n_ten).astype(jnp.int32)

    pieces = cut(nbr_shard, nbr_row, nbr_count, database)
    spread = lax.all_to_all(pieces, "seq", split_axis=0, concat_axis=0, tiled=True)

    halves = d_part // (PIECES_WO * PIECE_F)
    strips = n_seq // halves
    own = jnp.stack([seq_at // halves, seq_at % halves]).astype(jnp.int32)
    own, _ = lax.optimization_barrier((own, pieces))
    mine = letter(own, tokens, wo, wo.shape[0] // strips)
    letters = ring_gather(mine, n_ten, tok_dev // PIECE_T * (pieces_f // 2))

    spread, _ = lax.optimization_barrier((spread, letters[3:5]))
    n_notes = 2 * items + span_dev
    spread = spread.reshape(n_seq * (per_shard + 1), PIECE_T, PIECE_F)
    notes = spread[per_shard :: per_shard + 1, 0, :n_notes].astype(jnp.int32)
    index = notes[:, :items] * (per_shard + 1) + notes[:, items : 2 * items]
    prev_count = jnp.where(seq_at > 0, notes[jnp.maximum(seq_at - 1, 0), n_notes - 1], 0)
    counts = jnp.concatenate([nbr_count, prev_count[None]])
    (picked,) = pick(index, spread, 1)
    rows = lax.all_to_all(picked, "seq", split_axis=0, concat_axis=0, tiled=True)
    nbr_gain, _ = lax.optimization_barrier((nbr_gain, picked))
    both = jnp.concatenate([wk, wv], axis=1).astype(jnp.float32)
    both = (both * nbr_gain.astype(jnp.float32)[:, None]).astype(jnp.bfloat16)
    both = both.reshape(n_ten, d_part, both.shape[1])
    *tail, both = lax.optimization_barrier((*letters[7:], both))
    letters = letters[:7] + tail
    queries, strip = query(where, letters, x_gain, wq, tok_dev, shift, n_seq)
    rows, queries, strip, counts = lax.optimization_barrier((rows, queries, strip, counts))
    mail = lax.all_to_all(strip, "seq", split_axis=0, concat_axis=0, tiled=True)
    mail = mail.reshape(strips, halves, *strip.shape[1:])

    rows = rows.reshape(pieces_f, pieces_t, items, PIECE_T, PIECE_F)
    streams = [rows[:, :, items // 2 :], rows[:, :, : items // 2]]
    (late, early), mail = ring_project(streams, where, both, n_ten, mail)
    prev = lax.ppermute(late[-1], "seq", [(i, i + 1) for i in range(n_seq - 1)])
    attended = attend(counts, queries, [*early, *late], prev, span_len)
    gathered = ring_gather(attended, n_ten, tok_dev // 2)
    return finish(where, mail, tokens, gathered, shift)


def solution(mesh):
    placed = (
        P("seq", "tensor"),
        P(),
        P(),
        P("seq", None, "tensor"),
        P("seq", None),
        P("seq", None),
        P("seq"),
        P(None, "tensor"),
        P(None, "tensor"),
        P(None, "tensor"),
        P("tensor", None),
    )
    return jax.shard_map(
        body, mesh=mesh, in_specs=placed, out_specs=P("seq", "tensor"), check_vma=False
    )
```

```python
import functools

import jax
import jax.numpy as jnp
from jax import lax
from jax.experimental import pallas as pl
from jax.experimental.pallas import tpu as pltpu
from jax.sharding import PartitionSpec as P

HS = 128
NB = 2
PIECE_T = 16
PIECE_F = 128
PIECES_WO = 2
RING_ORDER = (0, 7, 1, 6, 2, 5, 3, 4)
VMEM_LIMIT = 48 * 1024 * 1024


def cut_kernel(shard_ref, row_ref, count_ref, db_ref, out_ref):
    shard = db_ref.shape[0]
    pieces_t = db_ref.shape[1] // PIECE_T
    pieces_f = db_ref.shape[2] // PIECE_F
    each, spans = shard_ref.shape
    lane = lax.broadcasted_iota(jnp.int32, (PIECE_T, PIECE_F), 1)
    note = jnp.zeros((PIECE_T, PIECE_F), jnp.int32)
    for span in range(spans):
        for j in range(each):
            at = span * each + j
            note = jnp.where(lane == at, shard_ref[j : j + 1, span : span + 1], note)
            row = row_ref[j : j + 1, span : span + 1]
            note = jnp.where(lane == spans * each + at, row, note)
        count = count_ref[:, span : span + 1]
        note = jnp.where(lane == 2 * spans * each + span, count, note)
    note = note.astype(jnp.float32).astype(jnp.bfloat16)
    for f in range(pieces_f):
        for i in range(pieces_t):
            piece = f * pieces_t + i
            out_ref[piece, :shard] = db_ref[
                :, i * PIECE_T : (i + 1) * PIECE_T, f * PIECE_F : (f + 1) * PIECE_F
            ]
            out_ref[piece, shard] = note


def cut(nbr_shard, nbr_row, nbr_count, database):
    shard, length, part = database.shape
    pieces = (length // PIECE_T) * (part // PIECE_F)
    vmem = pl.BlockSpec(memory_space=pltpu.VMEM)
    return pl.pallas_call(
        cut_kernel,
        in_specs=[vmem] * 4,
        out_specs=vmem,
        out_shape=jax.ShapeDtypeStruct((pieces, shard + 1, PIECE_T, PIECE_F), database.dtype),
        compiler_params=pltpu.CompilerParams(vmem_limit_bytes=VMEM_LIMIT),
        name="cut",
    )(nbr_shard.T, nbr_row.T, nbr_count.reshape(1, -1), database)


def pick_kernel(index_ref, spread_ref, *out_refs):
    n_seq, items = out_refs[0].shape[:2]

    def one(dest, carry):
        for at, out_ref in enumerate(out_refs):
            for j in range(items):
                out_ref[dest, j] = spread_ref[index_ref[dest, at * items + j]]
        return carry

    lax.fori_loop(0, n_seq, one, 0, unroll=2)


def pick(index, spread, parts):
    vmem = pl.BlockSpec(memory_space=pltpu.VMEM)
    shape = (index.shape[0], index.shape[1] // parts, PIECE_T, PIECE_F)
    return pl.pallas_call(
        pick_kernel,
        in_specs=[pl.BlockSpec(memory_space=pltpu.SMEM), vmem],
        out_specs=[vmem] * parts,
        out_shape=[jax.ShapeDtypeStruct(shape, spread.dtype)] * parts,
        compiler_params=pltpu.CompilerParams(vmem_limit_bytes=VMEM_LIMIT),
        name="pick",
    )(index, spread)


def letter_kernel(at_ref, tokens_ref, wo_ref, out_ref):
    rows, part = tokens_ref.shape
    pieces_t = rows // PIECE_T
    pieces_f = part // PIECE_F
    for f in range(pieces_f):
        for i in range(pieces_t):
            out_ref[f * pieces_t + i] = tokens_ref[
                i * PIECE_T : (i + 1) * PIECE_T, f * PIECE_F : (f + 1) * PIECE_F
            ]
    strip = PIECES_WO * PIECE_F
    for group in range(wo_ref.shape[1] // part):
        for f in range(PIECES_WO):
            start = pl.multiple_of(group * part + at_ref[1] * strip + f * PIECE_F, PIECE_F)
            out_ref[pieces_f * pieces_t + group * PIECES_WO + f] = wo_ref[:, pl.ds(start, PIECE_F)]


def letter(at, tokens, wo, depth):
    rows, part = tokens.shape
    tiles = rows * part // (PIECE_T * PIECE_F) + wo.shape[1] // part * PIECES_WO
    return pl.pallas_call(
        letter_kernel,
        grid_spec=pltpu.PrefetchScalarGridSpec(
            num_scalar_prefetch=1,
            grid=(1,),
            in_specs=[
                pl.BlockSpec((rows, part), lambda g, at: (0, 0)),
                pl.BlockSpec((depth, wo.shape[1]), lambda g, at: (at[0], 0)),
            ],
            out_specs=pl.BlockSpec((tiles, PIECE_T, PIECE_F), lambda g, at: (0, 0, 0)),
        ),
        out_shape=jax.ShapeDtypeStruct((tiles, PIECE_T, PIECE_F), tokens.dtype),
        name="letter",
    )(at, tokens, wo)


def unpack(x_ref):
    features, pieces_t, items = x_ref.shape[:3]
    rows = pieces_t * items * PIECE_T
    pieces = [x_ref[f].reshape(rows, PIECE_F) for f in range(features)]
    squares = jnp.zeros((rows, PIECE_F), jnp.float32)
    for piece in pieces:
        wide = piece.astype(jnp.float32)
        squares = squares + wide * wide
    return jnp.concatenate(pieces, axis=1), squares


def store_spans(acc, squares, features, out_refs):
    mean = jnp.sum(squares, axis=1, keepdims=True) * (1.0 / features)
    done = (acc * lax.rsqrt(mean + 1e-06)).astype(jnp.bfloat16)
    pieces_t = out_refs[0].shape[0]
    done = done.reshape(pieces_t, NB * len(out_refs), PIECE_T, done.shape[-1])
    for span, ref in enumerate(out_refs):
        ref[...] = done[:, span * NB : (span + 1) * NB]


def query_kernel(shift, halved, where_ref, gain_ref, wq_ref, *rest):
    x_refs, (out_ref, strip_ref) = rest[:-2], rest[-2:]
    rows = out_ref.shape[0]
    groups, _, part = gain_ref.shape
    pieces_t = rows // PIECE_T
    tiles = pieces_t * (part // PIECE_F)
    whole = list(x_refs[:-2])

    def tile_rows(k, f):
        first = f * pieces_t
        if k < groups - 1:
            return x_refs[k][first : first + pieces_t].reshape(rows, PIECE_F)
        ref, start = (x_refs[-2], 0) if first < halved else (x_refs[-1], halved)
        return ref[first - start : first - start + pieces_t].reshape(rows, PIECE_F)

    squares = jnp.zeros((rows, PIECE_F), jnp.float32)
    for k in range(groups):
        for f in range(part // PIECE_F):
            wide = tile_rows(k, f).astype(jnp.float32)
            squares = squares + wide * wide
    mean = jnp.sum(squares, axis=1, keepdims=True) * (1.0 / (groups * part))
    inverse = lax.rsqrt(mean + 1e-06)
    total = jnp.zeros(out_ref.shape, jnp.float32)
    me = where_ref[0]
    for k in range(groups):
        group = where_ref[RING_ORDER[k]]
        x = jnp.concatenate([tile_rows(k, f) for f in range(part // PIECE_F)], axis=1)
        gain = gain_ref[group].astype(jnp.float32)
        normed = (x.astype(jnp.float32) * inverse * gain).astype(jnp.bfloat16)
        total = total + jnp.dot(normed, wq_ref[group], preferred_element_type=jnp.float32)
        for f in range(PIECES_WO):
            at = tiles + me * PIECES_WO + f
            ref = whole[k] if k < groups - 1 else x_refs[-1]
            at = at if k < groups - 1 else at - halved
            tile = ref[at]
            for dest in range(strip_ref.shape[0]):
                strip_ref[dest, group * PIECES_WO + f] = tile
    total = pltpu.roll(total * HS ** (-0.5), rows - shift, 0)
    out_ref[...] = total.astype(jnp.bfloat16)


def query(where, letters, gain, wq, rows, shift, copies):
    groups = where.shape[0]
    part = wq.shape[0] // groups
    cols = wq.shape[1]
    vmem = pl.BlockSpec(memory_space=pltpu.VMEM)
    return pl.pallas_call(
        functools.partial(query_kernel, shift, letters[-2].shape[0]),
        in_specs=[pl.BlockSpec(memory_space=pltpu.SMEM)] + [vmem] * (2 + len(letters)),
        out_specs=[vmem] * 2,
        out_shape=[
            jax.ShapeDtypeStruct((rows, cols), jnp.bfloat16),
            jax.ShapeDtypeStruct((copies, groups * PIECES_WO, PIECE_T, PIECE_F), jnp.bfloat16),
        ],
        compiler_params=pltpu.CompilerParams(vmem_limit_bytes=VMEM_LIMIT),
        cost_estimate=pl.CostEstimate(
            flops=8 * rows * groups * part * cols,
            bytes_accessed=4 * groups * part * (rows + cols),
            transcendentals=0,
        ),
        name="query",
    )(where, gain.reshape(groups, 1, part), wq.reshape(groups, part, cols), *letters)


def gather_kernel(places, first, last, where_ref, w_ref, *rest):
    count = len(places)
    x_refs, rest = rest[:count], rest[count:]
    if not first:
        acc, squares = rest[0][...], rest[1][...]
        rest = rest[2:]
    for at, (x_ref, (place, start)) in enumerate(zip(x_refs, places)):
        x, more = unpack(x_ref)
        lane = start * PIECE_F
        w = w_ref[where_ref[place], lane : lane + x.shape[1], :]
        term = jnp.dot(x, w, preferred_element_type=jnp.float32)
        if first and at == 0:
            acc, squares = term, more
        else:
            acc, squares = acc + term, squares + more
    if last:
        store_spans(acc, squares, w_ref.shape[0] * w_ref.shape[1], rest)
    else:
        rest[0][...] = acc
        rest[1][...] = squares


def gather_step(blocks, places, where, weights, state, last):
    _, part, cols = weights.shape
    _, pieces_t, items = blocks[0].shape[:3]
    rows = pieces_t * items * PIECE_T
    vmem = pl.BlockSpec(memory_space=pltpu.VMEM)
    if last:
        span = jax.ShapeDtypeStruct((pieces_t, NB, PIECE_T, cols), jnp.bfloat16)
        out_shape = [span] * (items // NB)
    else:
        out_shape = [
            jax.ShapeDtypeStruct((rows, cols), jnp.float32),
            jax.ShapeDtypeStruct((rows, PIECE_F), jnp.float32),
        ]
    return pl.pallas_call(
        functools.partial(gather_kernel, tuple(places), not state, last),
        in_specs=[pl.BlockSpec(memory_space=pltpu.SMEM)]
        + [vmem] * (1 + len(blocks) + len(state)),
        out_specs=[vmem] * len(out_shape),
        out_shape=out_shape,
        compiler_params=pltpu.CompilerParams(vmem_limit_bytes=VMEM_LIMIT),
        cost_estimate=pl.CostEstimate(
            flops=8 * rows * cols * sum(block.shape[0] for block in blocks) * PIECE_F,
            bytes_accessed=2 * sum(block.size for block in blocks) + 8 * rows * cols,
            transcendentals=0,
        ),
        name="gather_last" if last else "gather_step",
    )(where, weights, *blocks, *state)


def ring_ways(n_ten):
    right = [(i, (i + 1) % n_ten) for i in range(n_ten)]
    left = [(i, (i - 1) % n_ten) for i in range(n_ten)]
    return right, left


def ring_gather(block, n_ten, cut_at):
    right, left = ring_ways(n_ten)
    go_right = go_left = block
    blocks = [block]
    for _ in range(1, n_ten // 2):
        go_right = lax.ppermute(go_right, "tensor", right)
        go_left = lax.ppermute(go_left, "tensor", left)
        blocks += [go_right, go_left]
    return blocks + [
        lax.ppermute(go_right[:cut_at], "tensor", right),
        lax.ppermute(go_left[cut_at:], "tensor", left),
    ]


def ring_project(streams, where, weights, n_ten, beside):
    right, left = ring_ways(n_ten)
    half = streams[0].shape[0] // 2
    last = n_ten // 2
    go_right, go_left = list(streams), list(streams)
    blocks = [[x] for x in streams]
    places = [[(0, 0)] for _ in streams]
    states = [()] * len(streams)
    first_parts = []
    for step in range(1, last + 1):
        for s in range(len(streams)):
            from_left, from_right = go_right[s], go_left[s]
            if step == last:
                held = lax.optimization_barrier((from_left, from_right, beside))
                from_left, from_right, beside = held
                from_left, from_right = from_left[:half], from_right[half:]
            if (step, s) == (last - 1, 1):
                held = lax.optimization_barrier((from_left, from_right, first_parts[0]))
                from_left, from_right, _ = held
            if step == last:
                held = lax.optimization_barrier((from_left, from_right, first_parts[1 + s]))
                from_left, from_right, _ = held
            go_right[s] = lax.ppermute(from_left, "tensor", right)
            go_left[s] = lax.ppermute(from_right, "tensor", left)
            blocks[s] += [go_right[s], go_left[s]]
            places[s] += [(n_ten - step, 0), (step, half if step == last else 0)]
            if step in (last - 2, last) or (step, s) == (last - 1, 0):
                state = gather_step(blocks[s], places[s], where, weights, states[s], step == last)
                blocks[s], places[s], states[s] = [], [], state
                if step < last:
                    first_parts.append(state)
    return states, beside


def weigh(scores, count, keys_axis_owner):
    scores = jnp.where(keys_axis_owner < count, scores, jnp.float32(-1e30))
    top = jnp.max(scores, axis=-1, keepdims=True)
    expo = jnp.exp(scores - top)
    return expo / jnp.sum(expo, axis=-1, keepdims=True)


def scores_of(queries, keys):
    return lax.dot_general(
        queries, keys, (((1,), (1,)), ((), ())), preferred_element_type=jnp.float32
    )


def attend_kernel(first, with_prev, span_len, count_ref, q_ref, *rest):
    out_ref = rest[-1]
    pair_refs, prev_ref, done = rest[:-1], None, 0
    if with_prev:
        pair_refs, (prev_ref, before_ref) = rest[:-3], rest[-3:-1]
        done = before_ref.shape[0]
        out_ref[:done, :] = before_ref[...]
    cols = out_ref.shape[1]
    heads = cols // HS
    spans = len(pair_refs)
    keys = pair_refs[0].shape[0] * pair_refs[0].shape[1] * pair_refs[0].shape[2]
    owner = (lax.broadcasted_iota(jnp.int32, (span_len, keys), 1) // PIECE_T) % NB
    row = lax.broadcasted_iota(jnp.int32, (span_len, keys), 0)
    for span in range(spans):
        pair = pair_refs[span][...].reshape(keys, 2 * cols)
        queries = q_ref[(first + span) * span_len : (first + span + 1) * span_len, :]
        mixed_heads = []
        for head in range(heads):
            at = slice(head * HS, (head + 1) * HS)
            value_at = slice(cols + head * HS, cols + (head + 1) * HS)
            query = queries[:, at]
            scores = scores_of(query, pair[:, at])
            if with_prev and span == spans - 1:
                prev = prev_ref[...].reshape(keys, 2 * cols)
                own = row == 0
                scores = jnp.where(own, scores, scores_of(query, prev[:, at]))
                count = jnp.where(own, count_ref[first + span], count_ref[first + span + 1])
                weights = weigh(scores, count, owner)
                ours = jnp.where(own, weights, 0.0).astype(jnp.bfloat16)
                theirs = jnp.where(own, 0.0, weights).astype(jnp.bfloat16)
                result = jnp.dot(
                    ours, pair[:, value_at], preferred_element_type=jnp.float32
                ) + jnp.dot(theirs, prev[:, value_at], preferred_element_type=jnp.float32)
            else:
                weights = weigh(scores, count_ref[first + span], owner).astype(jnp.bfloat16)
                result = jnp.dot(
                    weights, pair[:, value_at], preferred_element_type=jnp.float32
                )
            mixed_heads.append(result.astype(jnp.bfloat16))
        rows = slice(done + span * span_len, done + (span + 1) * span_len)
        out_ref[rows, :] = jnp.concatenate(mixed_heads, axis=1)


def attend(counts, queries, pairs, first, span_len, prev=None, before=None):
    cols = queries.shape[1]
    with_prev = prev is not None
    rows = len(pairs) * span_len + (before.shape[0] if with_prev else 0)
    operands = [counts, queries, *pairs] + ([prev, before] if with_prev else [])
    vmem = pl.BlockSpec(memory_space=pltpu.VMEM)
    return pl.pallas_call(
        functools.partial(attend_kernel, first, with_prev, span_len),
        in_specs=[pl.BlockSpec(memory_space=pltpu.SMEM)] + [vmem] * (len(operands) - 1),
        out_specs=vmem,
        out_shape=jax.ShapeDtypeStruct((rows, cols), jnp.bfloat16),
        compiler_params=pltpu.CompilerParams(vmem_limit_bytes=VMEM_LIMIT),
        cost_estimate=pl.CostEstimate(
            flops=32 * len(pairs) * span_len * 256 * cols,
            bytes_accessed=4 * rows * cols,
            transcendentals=0,
        ),
        name="attend_prev" if with_prev else "attend",
    )(*operands)


def finish_kernel(shift, where_ref, mail_ref, tokens_ref, *rest):
    attended_refs, out_ref = rest[:-1], rest[-1]
    groups = where_ref.shape[0]
    depth = attended_refs[0].shape[1]
    total = None
    for k in range(groups):
        group = where_ref[RING_ORDER[k]]
        if k < groups - 1:
            attended = attended_refs[k][...]
        else:
            attended = jnp.concatenate([ref[...] for ref in attended_refs[k:]], axis=0)
        tiles = [
            mail_ref[:, h, group * PIECES_WO + f].reshape(depth, PIECE_F)
            for h in range(mail_ref.shape[1])
            for f in range(PIECES_WO)
        ]
        wo = jnp.concatenate(tiles, axis=1)
        part = jnp.dot(attended, wo, preferred_element_type=jnp.float32)
        part = part.astype(jnp.bfloat16).astype(jnp.float32)
        total = part if total is None else total + part
    total = pltpu.roll(total, shift, 0)
    out_ref[...] = (tokens_ref[...].astype(jnp.float32) + total).astype(jnp.bfloat16)


def finish(where, mail, tokens, attended, shift):
    vmem = pl.BlockSpec(memory_space=pltpu.VMEM)
    return pl.pallas_call(
        functools.partial(finish_kernel, shift),
        in_specs=[pl.BlockSpec(memory_space=pltpu.SMEM)] + [vmem] * (2 + len(attended)),
        out_specs=vmem,
        out_shape=jax.ShapeDtypeStruct(tokens.shape, jnp.bfloat16),
        compiler_params=pltpu.CompilerParams(vmem_limit_bytes=VMEM_LIMIT),
        name="finish",
    )(where, mail, tokens, *attended)


def body(tokens, x_gain, nbr_gain, database, nbr_shard, nbr_row, nbr_count, wq, wk, wv, wo):
    n_seq = lax.axis_size("seq")
    n_ten = lax.axis_size("tensor")
    tok_dev = tokens.shape[0]
    span_dev = nbr_shard.shape[0]
    span_len = tok_dev // span_dev
    shift = span_len - 1
    per_shard, nbr_len, d_part = database.shape
    items = span_dev * NB
    pieces_t = nbr_len // PIECE_T
    pieces_f = d_part // PIECE_F
    seq_at = lax.axis_index("seq")
    me = lax.axis_index("tensor")
    where = ((me + jnp.arange(n_ten, dtype=jnp.int32)) % n_ten).astype(jnp.int32)

    pieces = cut(nbr_shard, nbr_row, nbr_count, database)
    spread = lax.all_to_all(pieces, "seq", split_axis=0, concat_axis=0, tiled=True)

    halves = d_part // (PIECES_WO * PIECE_F)
    strips = n_seq // halves
    own = jnp.stack([seq_at // halves, seq_at % halves]).astype(jnp.int32)
    own, _ = lax.optimization_barrier((own, pieces))
    mine = letter(own, tokens, wo, wo.shape[0] // strips)
    letters = ring_gather(mine, n_ten, tok_dev // PIECE_T * (pieces_f // 2))

    spread, _ = lax.optimization_barrier((spread, letters[3:5]))
    n_notes = 2 * items + span_dev
    spread = spread.reshape(n_seq * (per_shard + 1), PIECE_T, PIECE_F)
    notes = spread[per_shard :: per_shard + 1, 0, :n_notes].astype(jnp.int32)
    index = notes[:, :items] * (per_shard + 1) + notes[:, items : 2 * items]
    prev_count = jnp.where(seq_at > 0, notes[jnp.maximum(seq_at - 1, 0), n_notes - 1], 0)
    counts = jnp.concatenate([nbr_count, prev_count[None]])
    (picked,) = pick(index, spread, 1)
    rows = lax.all_to_all(picked, "seq", split_axis=0, concat_axis=0, tiled=True)
    nbr_gain, _ = lax.optimization_barrier((nbr_gain, picked))
    both = jnp.concatenate([wk, wv], axis=1).astype(jnp.float32)
    both = (both * nbr_gain.astype(jnp.float32)[:, None]).astype(jnp.bfloat16)
    both = both.reshape(n_ten, d_part, both.shape[1])
    *tail, both = lax.optimization_barrier((*letters[7:], both))
    letters = letters[:7] + tail
    queries, strip = query(where, letters, x_gain, wq, tok_dev, shift, n_seq)
    rows, queries, strip, counts = lax.optimization_barrier((rows, queries, strip, counts))
    mail = lax.all_to_all(strip, "seq", split_axis=0, concat_axis=0, tiled=True)
    mail = mail.reshape(strips, halves, *strip.shape[1:])

    rows = rows.reshape(pieces_f, pieces_t, items, PIECE_T, PIECE_F)
    streams = [rows[:, :, items // 2 :], rows[:, :, : items // 2]]
    (late, early), mail = ring_project(streams, where, both, n_ten, mail)
    prev = lax.ppermute(late[-1], "seq", [(i, i + 1) for i in range(n_seq - 1)])
    attended = attend(counts, queries, early, 0, span_len)
    attended = attend(counts, queries, late, span_dev // 2, span_len, prev, attended)
    gathered = ring_gather(attended, n_ten, tok_dev // 2)
    return finish(where, mail, tokens, gathered, shift)


def solution(mesh):
    placed = (
        P("seq", "tensor"),
        P(),
        P(),
        P("seq", None, "tensor"),
        P("seq", None),
        P("seq", None),
        P("seq"),
        P(None, "tensor"),
        P(None, "tensor"),
        P(None, "tensor"),
        P("tensor", None),
    )
    return jax.shard_map(
        body, mesh=mesh, in_specs=placed, out_specs=P("seq", "tensor"), check_vma=False
    )
```

```python
import functools

import jax
import jax.numpy as jnp
from jax import lax
from jax.experimental import pallas as pl
from jax.experimental.pallas import tpu as pltpu
from jax.sharding import PartitionSpec as P

HS = 128
NB = 2
PIECE_T = 16
PIECE_F = 128
PIECES_WO = 2
RING_ORDER = (0, 7, 1, 6, 2, 5, 3, 4)
VMEM_LIMIT = 48 * 1024 * 1024


def cut_kernel(notes_ref, db_ref, out_ref):
    shard = db_ref.shape[0]
    pieces_t = db_ref.shape[1] // PIECE_T
    pieces_f = db_ref.shape[2] // PIECE_F
    kinds, spans = notes_ref.shape
    each = (kinds - 1) // 2
    lane = lax.broadcasted_iota(jnp.int32, (PIECE_T, PIECE_F), 1)
    note = jnp.zeros((PIECE_T, PIECE_F), jnp.int32)
    for span in range(spans):
        for kind in range(kinds):
            at = (kind // each * spans + span) * each + kind % each
            at = at if kind < 2 * each else 2 * each * spans + span
            note = jnp.where(lane == at, notes_ref[kind : kind + 1, span : span + 1], note)
    note = note.astype(jnp.float32).astype(jnp.bfloat16)
    for f in range(pieces_f):
        for i in range(pieces_t):
            piece = f * pieces_t + i
            out_ref[piece, :shard] = db_ref[
                :, i * PIECE_T : (i + 1) * PIECE_T, f * PIECE_F : (f + 1) * PIECE_F
            ]
            out_ref[piece, shard] = note


def cut(notes, database):
    shard, length, part = database.shape
    pieces = (length // PIECE_T) * (part // PIECE_F)
    vmem = pl.BlockSpec(memory_space=pltpu.VMEM)
    return pl.pallas_call(
        cut_kernel,
        in_specs=[vmem] * 2,
        out_specs=vmem,
        out_shape=jax.ShapeDtypeStruct((pieces, shard + 1, PIECE_T, PIECE_F), database.dtype),
        compiler_params=pltpu.CompilerParams(vmem_limit_bytes=VMEM_LIMIT),
        name="cut",
    )(notes, database)


def pick_kernel(index_ref, spread_ref, *out_refs):
    n_seq, items = out_refs[0].shape[:2]

    def one(dest, carry):
        for at, out_ref in enumerate(out_refs):
            for j in range(items):
                out_ref[dest, j] = spread_ref[index_ref[dest, at * items + j]]
        return carry

    lax.fori_loop(0, n_seq, one, 0, unroll=2)


def pick(index, spread, parts):
    vmem = pl.BlockSpec(memory_space=pltpu.VMEM)
    shape = (index.shape[0], index.shape[1] // parts, PIECE_T, PIECE_F)
    return pl.pallas_call(
        pick_kernel,
        in_specs=[pl.BlockSpec(memory_space=pltpu.SMEM), vmem],
        out_specs=[vmem] * parts,
        out_shape=[jax.ShapeDtypeStruct(shape, spread.dtype)] * parts,
        compiler_params=pltpu.CompilerParams(vmem_limit_bytes=VMEM_LIMIT),
        name="pick",
    )(index, spread)


def letter_kernel(at_ref, tokens_ref, wo_ref, out_ref):
    rows, part = tokens_ref.shape
    pieces_t = rows // PIECE_T
    pieces_f = part // PIECE_F
    for f in range(pieces_f):
        for i in range(pieces_t):
            out_ref[f * pieces_t + i] = tokens_ref[
                i * PIECE_T : (i + 1) * PIECE_T, f * PIECE_F : (f + 1) * PIECE_F
            ]
    strip = PIECES_WO * PIECE_F
    for group in range(wo_ref.shape[1] // part):
        for f in range(PIECES_WO):
            start = pl.multiple_of(group * part + at_ref[1] * strip + f * PIECE_F, PIECE_F)
            out_ref[pieces_f * pieces_t + group * PIECES_WO + f] = wo_ref[:, pl.ds(start, PIECE_F)]


def letter(at, tokens, wo, depth):
    rows, part = tokens.shape
    tiles = rows * part // (PIECE_T * PIECE_F) + wo.shape[1] // part * PIECES_WO
    return pl.pallas_call(
        letter_kernel,
        grid_spec=pltpu.PrefetchScalarGridSpec(
            num_scalar_prefetch=1,
            grid=(1,),
            in_specs=[
                pl.BlockSpec((rows, part), lambda g, at: (0, 0)),
                pl.BlockSpec((depth, wo.shape[1]), lambda g, at: (at[0], 0)),
            ],
            out_specs=pl.BlockSpec((tiles, PIECE_T, PIECE_F), lambda g, at: (0, 0, 0)),
        ),
        out_shape=jax.ShapeDtypeStruct((tiles, PIECE_T, PIECE_F), tokens.dtype),
        name="letter",
    )(at, tokens, wo)


def unpack(x_ref):
    features, pieces_t, items = x_ref.shape[:3]
    rows = pieces_t * items * PIECE_T
    pieces = [x_ref[f].reshape(rows, PIECE_F) for f in range(features)]
    squares = jnp.zeros((rows, PIECE_F), jnp.float32)
    for piece in pieces:
        wide = piece.astype(jnp.float32)
        squares = squares + wide * wide
    return jnp.concatenate(pieces, axis=1), squares


def store_spans(acc, squares, features, out_refs):
    mean = jnp.sum(squares, axis=1, keepdims=True) * (1.0 / features)
    done = (acc * lax.rsqrt(mean + 1e-06)).astype(jnp.bfloat16)
    pieces_t = out_refs[0].shape[0]
    done = done.reshape(pieces_t, NB * len(out_refs), PIECE_T, done.shape[-1])
    for span, ref in enumerate(out_refs):
        ref[...] = done[:, span * NB : (span + 1) * NB]


def query_kernel(shift, halved, where_ref, gain_ref, wq_ref, *rest):
    x_refs, (out_ref, strip_ref) = rest[:-2], rest[-2:]
    rows = out_ref.shape[0]
    groups, _, part = gain_ref.shape
    pieces_t = rows // PIECE_T
    tiles = pieces_t * (part // PIECE_F)
    whole = list(x_refs[:-2])

    def tile_rows(k, f):
        first = f * pieces_t
        if k < groups - 1:
            return x_refs[k][first : first + pieces_t].reshape(rows, PIECE_F)
        ref, start = (x_refs[-2], 0) if first < halved else (x_refs[-1], halved)
        return ref[first - start : first - start + pieces_t].reshape(rows, PIECE_F)

    squares = jnp.zeros((rows, PIECE_F), jnp.float32)
    for k in range(groups):
        for f in range(part // PIECE_F):
            wide = tile_rows(k, f).astype(jnp.float32)
            squares = squares + wide * wide
    mean = jnp.sum(squares, axis=1, keepdims=True) * (1.0 / (groups * part))
    inverse = lax.rsqrt(mean + 1e-06)
    total = jnp.zeros(out_ref.shape, jnp.float32)
    me = where_ref[0]
    for k in range(groups):
        group = where_ref[RING_ORDER[k]]
        x = jnp.concatenate([tile_rows(k, f) for f in range(part // PIECE_F)], axis=1)
        gain = gain_ref[group].astype(jnp.float32)
        normed = (x.astype(jnp.float32) * inverse * gain).astype(jnp.bfloat16)
        total = total + jnp.dot(normed, wq_ref[group], preferred_element_type=jnp.float32)
        for f in range(PIECES_WO):
            at = tiles + me * PIECES_WO + f
            ref = whole[k] if k < groups - 1 else x_refs[-1]
            at = at if k < groups - 1 else at - halved
            tile = ref[at]
            for dest in range(strip_ref.shape[0]):
                strip_ref[dest, group * PIECES_WO + f] = tile
    total = pltpu.roll(total * HS ** (-0.5), rows - shift, 0)
    out_ref[...] = total.astype(jnp.bfloat16)


def query(where, letters, gain, wq, rows, shift, copies):
    groups = where.shape[0]
    part = wq.shape[0] // groups
    cols = wq.shape[1]
    vmem = pl.BlockSpec(memory_space=pltpu.VMEM)
    return pl.pallas_call(
        functools.partial(query_kernel, shift, letters[-2].shape[0]),
        in_specs=[pl.BlockSpec(memory_space=pltpu.SMEM)] + [vmem] * (2 + len(letters)),
        out_specs=[vmem] * 2,
        out_shape=[
            jax.ShapeDtypeStruct((rows, cols), jnp.bfloat16),
            jax.ShapeDtypeStruct((copies, groups * PIECES_WO, PIECE_T, PIECE_F), jnp.bfloat16),
        ],
        compiler_params=pltpu.CompilerParams(vmem_limit_bytes=VMEM_LIMIT),
        cost_estimate=pl.CostEstimate(
            flops=8 * rows * groups * part * cols,
            bytes_accessed=4 * groups * part * (rows + cols),
            transcendentals=0,
        ),
        name="query",
    )(where, gain.reshape(groups, 1, part), wq.reshape(groups, part, cols), *letters)


def gather_kernel(places, first, last, where_ref, w_ref, *rest):
    count = len(places)
    x_refs, rest = rest[:count], rest[count:]
    if not first:
        acc, squares = rest[0][...], rest[1][...]
        rest = rest[2:]
    for at, (x_ref, (place, start)) in enumerate(zip(x_refs, places)):
        x, more = unpack(x_ref)
        lane = start * PIECE_F
        w = w_ref[where_ref[place], lane : lane + x.shape[1], :]
        term = jnp.dot(x, w, preferred_element_type=jnp.float32)
        if first and at == 0:
            acc, squares = term, more
        else:
            acc, squares = acc + term, squares + more
    if last:
        store_spans(acc, squares, w_ref.shape[0] * w_ref.shape[1], rest)
    else:
        rest[0][...] = acc
        rest[1][...] = squares


def gather_step(blocks, places, where, weights, state, last):
    _, part, cols = weights.shape
    _, pieces_t, items = blocks[0].shape[:3]
    rows = pieces_t * items * PIECE_T
    vmem = pl.BlockSpec(memory_space=pltpu.VMEM)
    if last:
        span = jax.ShapeDtypeStruct((pieces_t, NB, PIECE_T, cols), jnp.bfloat16)
        out_shape = [span] * (items // NB)
    else:
        out_shape = [
            jax.ShapeDtypeStruct((rows, cols), jnp.float32),
            jax.ShapeDtypeStruct((rows, PIECE_F), jnp.float32),
        ]
    return pl.pallas_call(
        functools.partial(gather_kernel, tuple(places), not state, last),
        in_specs=[pl.BlockSpec(memory_space=pltpu.SMEM)]
        + [vmem] * (1 + len(blocks) + len(state)),
        out_specs=[vmem] * len(out_shape),
        out_shape=out_shape,
        compiler_params=pltpu.CompilerParams(vmem_limit_bytes=VMEM_LIMIT),
        cost_estimate=pl.CostEstimate(
            flops=8 * rows * cols * sum(block.shape[0] for block in blocks) * PIECE_F,
            bytes_accessed=2 * sum(block.size for block in blocks) + 8 * rows * cols,
            transcendentals=0,
        ),
        name="gather_last" if last else "gather_step",
    )(where, weights, *blocks, *state)


def ring_ways(n_ten):
    right = [(i, (i + 1) % n_ten) for i in range(n_ten)]
    left = [(i, (i - 1) % n_ten) for i in range(n_ten)]
    return right, left


def ring_gather(block, n_ten, cut_at):
    right, left = ring_ways(n_ten)
    go_right = go_left = block
    blocks = [block]
    for _ in range(1, n_ten // 2):
        go_right = lax.ppermute(go_right, "tensor", right)
        go_left = lax.ppermute(go_left, "tensor", left)
        blocks += [go_right, go_left]
    return blocks + [
        lax.ppermute(go_right[:cut_at], "tensor", right),
        lax.ppermute(go_left[cut_at:], "tensor", left),
    ]


def ring_project(streams, where, weights, n_ten, beside):
    right, left = ring_ways(n_ten)
    half = streams[0].shape[0] // 2
    last = n_ten // 2
    go_right, go_left = list(streams), list(streams)
    blocks = [[x] for x in streams]
    places = [[(0, 0)] for _ in streams]
    states = [()] * len(streams)
    first_parts = []
    for step in range(1, last + 1):
        for s in range(len(streams)):
            from_left, from_right = go_right[s], go_left[s]
            if step == last:
                held = lax.optimization_barrier((from_left, from_right, beside))
                from_left, from_right, beside = held
                from_left, from_right = from_left[:half], from_right[half:]
            if (step, s) == (last - 1, 1):
                held = lax.optimization_barrier((from_left, from_right, first_parts[0]))
                from_left, from_right, _ = held
            if step == last:
                held = lax.optimization_barrier((from_left, from_right, first_parts[1 + s]))
                from_left, from_right, _ = held
            go_right[s] = lax.ppermute(from_left, "tensor", right)
            go_left[s] = lax.ppermute(from_right, "tensor", left)
            blocks[s] += [go_right[s], go_left[s]]
            places[s] += [(n_ten - step, 0), (step, half if step == last else 0)]
            if step in (last - 2, last) or (step, s) == (last - 1, 0):
                state = gather_step(blocks[s], places[s], where, weights, states[s], step == last)
                blocks[s], places[s], states[s] = [], [], state
                if step < last:
                    first_parts.append(state)
    return states, beside


def weigh(scores, count, keys_axis_owner):
    scores = jnp.where(keys_axis_owner < count, scores, jnp.float32(-1e30))
    top = jnp.max(scores, axis=-1, keepdims=True)
    expo = jnp.exp(scores - top)
    return expo / jnp.sum(expo, axis=-1, keepdims=True)


def scores_of(queries, keys):
    return lax.dot_general(
        queries, keys, (((1,), (1,)), ((), ())), preferred_element_type=jnp.float32
    )


def attend_kernel(first, with_prev, span_len, count_ref, q_ref, *rest):
    out_ref = rest[-1]
    pair_refs, prev_ref, done = rest[:-1], None, 0
    if with_prev:
        pair_refs, (prev_ref, before_ref) = rest[:-3], rest[-3:-1]
        done = before_ref.shape[0]
        out_ref[:done, :] = before_ref[...]
    cols = out_ref.shape[1]
    heads = cols // HS
    spans = len(pair_refs)
    keys = pair_refs[0].shape[0] * pair_refs[0].shape[1] * pair_refs[0].shape[2]
    owner = (lax.broadcasted_iota(jnp.int32, (span_len, keys), 1) // PIECE_T) % NB
    row = lax.broadcasted_iota(jnp.int32, (span_len, keys), 0)
    for span in range(spans):
        pair = pair_refs[span][...].reshape(keys, 2 * cols)
        queries = q_ref[(first + span) * span_len : (first + span + 1) * span_len, :]
        mixed_heads = []
        for head in range(heads):
            at = slice(head * HS, (head + 1) * HS)
            value_at = slice(cols + head * HS, cols + (head + 1) * HS)
            query = queries[:, at]
            scores = scores_of(query, pair[:, at])
            if with_prev and span == spans - 1:
                prev = prev_ref[...].reshape(keys, 2 * cols)
                own = row == 0
                scores = jnp.where(own, scores, scores_of(query, prev[:, at]))
                count = jnp.where(own, count_ref[first + span], count_ref[first + span + 1])
                weights = weigh(scores, count, owner)
                ours = jnp.where(own, weights, 0.0).astype(jnp.bfloat16)
                theirs = jnp.where(own, 0.0, weights).astype(jnp.bfloat16)
                result = jnp.dot(
                    ours, pair[:, value_at], preferred_element_type=jnp.float32
                ) + jnp.dot(theirs, prev[:, value_at], preferred_element_type=jnp.float32)
            else:
                weights = weigh(scores, count_ref[first + span], owner).astype(jnp.bfloat16)
                result = jnp.dot(
                    weights, pair[:, value_at], preferred_element_type=jnp.float32
                )
            mixed_heads.append(result.astype(jnp.bfloat16))
        rows = slice(done + span * span_len, done + (span + 1) * span_len)
        out_ref[rows, :] = jnp.concatenate(mixed_heads, axis=1)


def attend(counts, queries, pairs, first, span_len, prev=None, before=None):
    cols = queries.shape[1]
    with_prev = prev is not None
    rows = len(pairs) * span_len + (before.shape[0] if with_prev else 0)
    operands = [counts, queries, *pairs] + ([prev, before] if with_prev else [])
    vmem = pl.BlockSpec(memory_space=pltpu.VMEM)
    return pl.pallas_call(
        functools.partial(attend_kernel, first, with_prev, span_len),
        in_specs=[pl.BlockSpec(memory_space=pltpu.SMEM)] + [vmem] * (len(operands) - 1),
        out_specs=vmem,
        out_shape=jax.ShapeDtypeStruct((rows, cols), jnp.bfloat16),
        compiler_params=pltpu.CompilerParams(vmem_limit_bytes=VMEM_LIMIT),
        cost_estimate=pl.CostEstimate(
            flops=32 * len(pairs) * span_len * 256 * cols,
            bytes_accessed=4 * rows * cols,
            transcendentals=0,
        ),
        name="attend_prev" if with_prev else "attend",
    )(*operands)


def finish_kernel(shift, where_ref, mail_ref, tokens_ref, *rest):
    attended_refs, out_ref = rest[:-1], rest[-1]
    groups = where_ref.shape[0]
    depth = attended_refs[0].shape[1]
    total = None
    for k in range(groups):
        group = where_ref[RING_ORDER[k]]
        if k < groups - 1:
            attended = attended_refs[k][...]
        else:
            attended = jnp.concatenate([ref[...] for ref in attended_refs[k:]], axis=0)
        tiles = [
            mail_ref[:, h, group * PIECES_WO + f].reshape(depth, PIECE_F)
            for h in range(mail_ref.shape[1])
            for f in range(PIECES_WO)
        ]
        wo = jnp.concatenate(tiles, axis=1)
        part = jnp.dot(attended, wo, preferred_element_type=jnp.float32)
        part = part.astype(jnp.bfloat16).astype(jnp.float32)
        total = part if total is None else total + part
    total = pltpu.roll(total, shift, 0)
    out_ref[...] = (tokens_ref[...].astype(jnp.float32) + total).astype(jnp.bfloat16)


def finish(where, mail, tokens, attended, shift):
    vmem = pl.BlockSpec(memory_space=pltpu.VMEM)
    return pl.pallas_call(
        functools.partial(finish_kernel, shift),
        in_specs=[pl.BlockSpec(memory_space=pltpu.SMEM)] + [vmem] * (2 + len(attended)),
        out_specs=vmem,
        out_shape=jax.ShapeDtypeStruct(tokens.shape, jnp.bfloat16),
        compiler_params=pltpu.CompilerParams(vmem_limit_bytes=VMEM_LIMIT),
        name="finish",
    )(where, mail, tokens, *attended)


def body(tokens, x_gain, nbr_gain, database, nbr_shard, nbr_row, nbr_count, wq, wk, wv, wo):
    n_seq = lax.axis_size("seq")
    n_ten = lax.axis_size("tensor")
    tok_dev = tokens.shape[0]
    span_dev = nbr_shard.shape[0]
    span_len = tok_dev // span_dev
    shift = span_len - 1
    per_shard, nbr_len, d_part = database.shape
    items = span_dev * NB
    pieces_t = nbr_len // PIECE_T
    pieces_f = d_part // PIECE_F
    seq_at = lax.axis_index("seq")
    me = lax.axis_index("tensor")
    where = ((me + jnp.arange(n_ten, dtype=jnp.int32)) % n_ten).astype(jnp.int32)

    notes = jnp.concatenate([nbr_shard.T, nbr_row.T, nbr_count[None]], axis=0)
    pieces = cut(notes, database)
    spread = lax.all_to_all(pieces, "seq", split_axis=0, concat_axis=0, tiled=True)

    halves = d_part // (PIECES_WO * PIECE_F)
    strips = n_seq // halves
    own = jnp.stack([seq_at // halves, seq_at % halves]).astype(jnp.int32)
    own, _ = lax.optimization_barrier((own, pieces))
    mine = letter(own, tokens, wo, wo.shape[0] // strips)
    letters = ring_gather(mine, n_ten, tok_dev // PIECE_T * (pieces_f // 2))

    spread, _ = lax.optimization_barrier((spread, letters[3:5]))
    n_notes = 2 * items + span_dev
    spread = spread.reshape(n_seq * (per_shard + 1), PIECE_T, PIECE_F)
    notes = spread[per_shard :: per_shard + 1, 0, :n_notes].astype(jnp.int32)
    index = notes[:, :items] * (per_shard + 1) + notes[:, items : 2 * items]
    prev_count = jnp.where(seq_at > 0, notes[jnp.maximum(seq_at - 1, 0), n_notes - 1], 0)
    counts = jnp.concatenate([nbr_count, prev_count[None]])
    (picked,) = pick(index, spread, 1)
    rows = lax.all_to_all(picked, "seq", split_axis=0, concat_axis=0, tiled=True)
    nbr_gain, _ = lax.optimization_barrier((nbr_gain, picked))
    both = jnp.concatenate([wk, wv], axis=1).astype(jnp.float32)
    both = (both * nbr_gain.astype(jnp.float32)[:, None]).astype(jnp.bfloat16)
    both = both.reshape(n_ten, d_part, both.shape[1])
    *tail, both = lax.optimization_barrier((*letters[7:], both))
    letters = letters[:7] + tail
    queries, strip = query(where, letters, x_gain, wq, tok_dev, shift, n_seq)
    rows, queries, strip, counts = lax.optimization_barrier((rows, queries, strip, counts))
    mail = lax.all_to_all(strip, "seq", split_axis=0, concat_axis=0, tiled=True)
    mail = mail.reshape(strips, halves, *strip.shape[1:])

    rows = rows.reshape(pieces_f, pieces_t, items, PIECE_T, PIECE_F)
    streams = [rows[:, :, items // 2 :], rows[:, :, : items // 2]]
    (late, early), mail = ring_project(streams, where, both, n_ten, mail)
    prev = lax.ppermute(late[-1], "seq", [(i, i + 1) for i in range(n_seq - 1)])
    attended = attend(counts, queries, early, 0, span_len)
    attended = attend(counts, queries, late, span_dev // 2, span_len, prev, attended)
    gathered = ring_gather(attended, n_ten, tok_dev // 2)
    return finish(where, mail, tokens, gathered, shift)


def solution(mesh):
    placed = (
        P("seq", "tensor"),
        P(),
        P(),
        P("seq", None, "tensor"),
        P("seq", None),
        P("seq", None),
        P("seq"),
        P(None, "tensor"),
        P(None, "tensor"),
        P(None, "tensor"),
        P("tensor", None),
    )
    return jax.shard_map(
        body, mesh=mesh, in_specs=placed, out_specs=P("seq", "tensor"), check_vma=False
    )
```
